32 devices in a mesh: groups: 2 (over x), ctx: 16 (over z, y, core).
Axes of the slice: x: 2, y: 2, z: 4, core: 2. Of those that a mesh axis runs over, the one named last changes fastest.
Arguments:
- queries: bfloat16 [2048, 12288], P(('groups', 'ctx')), parts along dimension 0, may hold values from -460 to 460
- latent_kv: bfloat16 [2048, 576], P(('groups', 'ctx')), parts along dimension 0, may hold values from -4 to 4
- key_proj: bfloat16 [64, 128, 512], P('ctx'), may hold values from -0.25 to 0.25
- value_proj: bfloat16 [64, 512, 128], P('ctx'), may hold values from -0.25 to 0.25
- moe_input: bfloat16 [2048, 3584], P(('groups', 'ctx')), parts along dimension 0, may hold values from -6 to 6
- routes: int32 [2048, 2], P(('groups', 'ctx')), parts along dimension 0, may hold values from 0 to 7, all different within a row; in each aligned block of 64 rows (0 to 63, 64 to 127, ...) at most 22 rows name the same one
- gates: float32 [2048, 2], P(('groups', 'ctx')), parts along dimension 0, may hold values from 0.1 to 0.6
- expert_gate: bfloat16 [16, 3584, 512], P('ctx'), may hold values from -0.09375 to 0.09375
- expert_up: bfloat16 [16, 3584, 512], P('ctx'), may hold values from -0.09375 to 0.09375
- expert_down: bfloat16 [16, 512, 3584], P('ctx'), may hold values from -0.1875 to 0.1875
Outputs:
- attention_out: bfloat16 [2048, 8192], P(('groups', 'ctx')), parts along dimension 0
- moe_out: bfloat16 [2048, 3584], P(('groups', 'ctx')), parts along dimension 0
The draws below stay inside these ranges and needn't reach their ends.
There are 2 independent parts, one for each index of `groups`. The reference program is written for one: setup_inputs(seed, part) draws one part's arguments, and reference() takes and returns one part's arrays. A program takes and returns all parts, laid end to end along the dimension named above; an argument that names none is the same for every part. Nothing has to cross between parts.
Inputs may be any that keep to these rules, and one draw needn't show every extreme that they name: Within the 64 rows of one device at most 22 routes name the same expert; the routes of one row differ.
All inputs are finite; a program needn't handle non-finite values.
Results may differ from the reference program's by a relative error of at most 0.0059.
Values may be sent and summed in bfloat16 or wider, within the bound.
No kernel may reach another device: no remote copies, remote signals or barrier semaphores. Data moves between devices by JAX's collectives and lax.ppermute only.
A program may use at most 128 MiB of HBM per device.

```python
import math
import jax
import jax.numpy as jnp
import numpy as np
from jax import lax

D = 3584
HEADS = 64
NOPE = 128
ROPE = 64
LATENT = 512
VDIM = 128
MOE_HID = 1024
TOP = 2
TOK_DEV = 64
SEQ = 1024
EXPERTS = 8
HALF = 512
CAP = 22
N_CTX = 16


def rope_anchor(key):
    return jnp.clip(jax.random.normal(jax.random.fold_in(key, 97), (ROPE,), jnp.float32), -4.0, 4.0)


def draw_latent_kv(key, part):
    anchor = rope_anchor(key)
    key = jax.random.fold_in(key, 11)
    values = jnp.clip(jax.random.normal(key, (SEQ, LATENT + ROPE), jnp.float32), -4.0, 4.0)
    values = values.at[0, LATENT:].set(anchor)
    values = values.at[1, LATENT:].set(0.99 * anchor)
    return values.astype(jnp.bfloat16)


def draw_queries(key, part):
    key = jax.random.fold_in(key, 23)
    full_shape = (SEQ, HEADS, NOPE + ROPE)
    values = jnp.clip(jax.random.normal(key, full_shape, jnp.float32), -4.0, 4.0)
    return values.reshape(SEQ, HEADS * (NOPE + ROPE)).astype(jnp.bfloat16)


def steps_of(own_key, extent, shards, low, largest):
    level = 1.0
    for dim, blocks in shards:
        heights = jax.random.uniform(jax.random.fold_in(jax.random.fold_in(own_key, 6), dim), (blocks,), jnp.float32, low / len(shards), largest / len(shards))
        level = level * jnp.repeat(jnp.exp(heights), extent[dim] // blocks).reshape((-1,) + (1,) * (len(extent) - 1 - dim))
    return level


def shared_out(stream_key, own, number, rows, count, top, reach, lean):
    sequence = jax.random.permutation(stream_key, count)
    packed, usual = portions_of(count, rows * top, reach, lean, True), portions_of(count, rows * top, reach, lean, False)
    places = jnp.arange(count)

    def named(sizes, offset_by):
        used = int((sizes > 0).sum())
        fixed = max(1, used // 4)
        shifted = fixed + (places - fixed + offset_by * (used - fixed)) % max(1, count - fixed)
        return jnp.zeros((count,), jnp.int32).at[sequence[jnp.where(places < fixed, places, shifted)]].set(jnp.asarray(sizes, jnp.int32))

    sizes = jnp.where(number % 4 == 0, named(packed, number // 4), named(usual, number - number // 4 - 1))
    mixed = jax.random.permutation(jax.random.fold_in(own, 3), count)
    giver, taker = mixed[0:count // 2 * 2:2], mixed[1:count // 2 * 2:2]
    room = jnp.minimum(sizes[giver] - 1, reach - sizes[taker]) // 2
    room = jnp.where((giver == sequence[0]) | (taker == sequence[0]) | (sizes[taker] == 0), 0, jnp.maximum(room, 0))
    shifted = jax.random.randint(jax.random.fold_in(own, 4), (count // 2,), 0, 1 << 20) % (room + 1)
    sizes = sizes.at[giver].add(-shifted).at[taker].add(shifted)
    members = jnp.searchsorted(jnp.cumsum(sizes), jnp.arange(rows * top), side="right").astype(jnp.int32)
    listing = members.reshape(top, rows).T
    listing = listing[jax.random.permutation(jax.random.fold_in(own, 1), rows)]
    offset_by = jax.random.randint(jax.random.fold_in(own, 2), (rows, 1), 0, top)
    return jnp.take_along_axis(listing, (jnp.arange(top)[None, :] + offset_by) % top, axis=1)


def portions_of(count, total, reach, lean, full):
    weights = [(1 << 20) // math.isqrt(grade ** lean) + 1 for grade in range(1, count + 1)]
    largest = reach if full else min(reach, max(-(-total // count), total * weights[0] // sum(weights)))
    least = 1 if total - largest >= count - 1 else 0
    holding, spare = [largest] + [least] * (count - 1), total - largest - least * (count - 1)
    while spare > 0:
        free = [i for i in range(1, count) if holding[i] < largest] or [i for i in range(1, count) if holding[i] < reach]
        mass, remaining = sum([weights[i] for i in free]), spare
        for i in free:
            addition = min(reach - holding[i], max(1, remaining * weights[i] // mass), spare)
            holding[i] = holding[i] + addition
            spare = spare - addition
    return np.array(holding)


def bell_draw(own_key, dims, deviation, limit, cuts=(), held_as=jnp.bfloat16):
    drawn = jax.random.normal(own_key, dims, jnp.float32) * deviation
    if len(cuts) > 0:
        drawn = steps_of(own_key, dims, cuts, -0.22, 0.18) * drawn
    return jnp.clip(drawn, min=-limit, max=limit).astype(held_as)


def setup_inputs(seed: int = 0, part: int = 0) -> dict:
    streams_of = jax.random.split(jax.random.key(seed), 11)
    part_splits = jax.random.split(jax.random.fold_in(streams_of[10], part), 11)
    queries = draw_queries(jax.random.fold_in(jax.random.fold_in(streams_of[10], part), 71), part)
    latent_kv = draw_latent_kv(jax.random.fold_in(jax.random.fold_in(streams_of[10], part), 71), part)
    key_proj = bell_draw(streams_of[2], (HEADS, NOPE, LATENT), LATENT ** -0.5, 0.25, ((0, 16),))
    value_proj = bell_draw(streams_of[3], (HEADS, LATENT, VDIM), LATENT ** -0.5, 0.25, ((0, 16),))
    moe_input = bell_draw(part_splits[4], (SEQ, D), 1.0, 6.0, ((0, 16),))
    routes_keys = jax.random.split(jax.random.fold_in(part_splits[5], 1), SEQ // TOK_DEV)
    routes_turns = jax.random.permutation(jax.random.fold_in(part_splits[5], 3), SEQ // TOK_DEV)
    routes = jax.vmap(lambda own, number: shared_out(jax.random.fold_in(part_splits[5], 2), own, number, TOK_DEV, EXPERTS, TOP, CAP, 2))(routes_keys, routes_turns).reshape((SEQ, TOP))
    gates = jnp.clip(0.1 + 0.5 * jax.random.uniform(part_splits[6], (SEQ, TOP), jnp.float32) ** steps_of(part_splits[6], (SEQ, TOP), ((0, 16),), -0.2, 0.2), 0.1, 0.6)
    expert_gate = bell_draw(streams_of[7], (2 * EXPERTS, D, HALF), D ** -0.5, 0.09375, ((0, 16),))
    expert_up = bell_draw(streams_of[8], (2 * EXPERTS, D, HALF), D ** -0.5, 0.09375, ((0, 16),))
    expert_down = bell_draw(streams_of[9], (2 * EXPERTS, HALF, D), MOE_HID ** -0.5, 0.1875, ((0, 16),))
    return {"queries": queries, "latent_kv": latent_kv, "key_proj": key_proj, "value_proj": value_proj, "moe_input": moe_input, "routes": routes, "gates": gates, "expert_gate": expert_gate, "expert_up": expert_up, "expert_down": expert_down}


def attention_part(queries, latent_kv, key_proj, value_proj):
    score_scale = 1.0 / math.sqrt(NOPE + ROPE)
    shaped = queries.reshape(SEQ, HEADS, NOPE + ROPE)
    query_lat = jnp.einsum('thd,hdl->thl', shaped[:, :, :NOPE].astype(jnp.float32), key_proj.astype(jnp.float32)).astype(jnp.bfloat16)
    query_all = jnp.concatenate([query_lat, shaped[:, :, NOPE:]], axis=2)
    blocks_all = query_all.reshape(N_CTX, TOK_DEV * HEADS, LATENT + ROPE)
    key_pos = jnp.arange(SEQ, dtype=jnp.int32)

    def attend(block_index):
        query_rows = blocks_all[block_index]
        scores = jnp.dot(query_rows, latent_kv.T, preferred_element_type=jnp.float32) * score_scale
        query_pos = block_index * TOK_DEV + jnp.arange(TOK_DEV * HEADS, dtype=jnp.int32) // HEADS
        visible = key_pos[None, :] <= query_pos[:, None]
        scores = jnp.where(visible, scores, -jnp.inf)
        row_max = lax.optimization_barrier(jnp.max(scores, axis=1, keepdims=True))
        weights = jnp.exp(scores - row_max)
        running_sum = lax.optimization_barrier(jnp.sum(weights, axis=1, keepdims=True))
        weighted = jnp.dot(weights.astype(jnp.bfloat16), latent_kv[:, :LATENT], preferred_element_type=jnp.float32)
        return (weighted / running_sum).astype(jnp.bfloat16)
    output_lat = lax.map(attend, jnp.arange(N_CTX, dtype=jnp.int32)).reshape(SEQ, HEADS, LATENT)
    per_head = jnp.einsum('thl,hlv->thv', output_lat.astype(jnp.float32), value_proj.astype(jnp.float32)).astype(jnp.bfloat16)
    return per_head.reshape(SEQ, HEADS * VDIM)

def expert_part(moe_input, routes, gates, expert_gate, expert_up, expert_down):
    route_count = TOK_DEV * TOP
    flat_ids = routes.reshape(N_CTX, route_count)
    onehot = (flat_ids[:, :, None] == jnp.arange(EXPERTS, dtype=jnp.int32)[None, None, :]).astype(jnp.int32)
    rank_table = jnp.cumsum(onehot, axis=1) - 1
    slot_index = lax.optimization_barrier(jnp.sum(rank_table * onehot, axis=2))
    source_dev = jnp.arange(N_CTX, dtype=jnp.int32)[:, None]
    target = flat_ids * (N_CTX * CAP) + source_dev * CAP + slot_index
    token_row = source_dev * TOK_DEV + jnp.arange(route_count, dtype=jnp.int32)[None, :] // TOP
    bucket_rows = jnp.full((EXPERTS * N_CTX * CAP,), SEQ, jnp.int32).at[target.reshape(-1)].set(token_row.reshape(-1))
    padded = jnp.concatenate([moe_input, jnp.zeros((1, D), jnp.bfloat16)], axis=0)
    bucket = padded[bucket_rows].reshape(EXPERTS, N_CTX * CAP, D)

    def half_pass(half_index):
        row_data = bucket[half_index // 2]
        gate_pre = jnp.dot(row_data, expert_gate[half_index], preferred_element_type=jnp.float32)
        up_pre = jnp.dot(row_data, expert_up[half_index], preferred_element_type=jnp.float32)
        hidden = (jax.nn.silu(gate_pre) * up_pre).astype(jnp.bfloat16)
        return jnp.dot(hidden, expert_down[half_index], preferred_element_type=jnp.float32).astype(jnp.bfloat16)
    partials = lax.map(half_pass, jnp.arange(2 * EXPERTS, dtype=jnp.int32))
    summed = lax.optimization_barrier(jnp.sum(partials.reshape(EXPERTS, 2, N_CTX * CAP, D).astype(jnp.float32), axis=1)).reshape(EXPERTS * N_CTX * CAP, D)
    picked = summed[target.reshape(-1)].reshape(SEQ, TOP, D)
    return lax.optimization_barrier(jnp.sum(picked * gates[:, :, None], axis=1)).astype(jnp.bfloat16)

def reference(queries, latent_kv, key_proj, value_proj, moe_input, routes, gates, expert_gate, expert_up, expert_down):
    attention_out = attention_part(queries, latent_kv, key_proj, value_proj)
    moe_out = expert_part(moe_input, routes, gates, expert_gate, expert_up, expert_down)
    return (attention_out, moe_out)
```

```python
import functools
import math

import jax
import jax.numpy as jnp
from jax import lax
from jax.experimental import pallas as pl
from jax.experimental.pallas import tpu as pltpu
from jax.sharding import PartitionSpec as P

D = 3584
HEADS = 64
NOPE = 128
ROPE = 64
LATENT = 512
VDIM = 128
TOP = 2
HALF = 512
HALF_D = D // 2
VMEM_LIMIT = 50 * 1024 * 1024
F32 = jnp.float32
BF16 = jnp.bfloat16


def params(limit=VMEM_LIMIT):
    return pltpu.CompilerParams(vmem_limit_bytes=limit)


def slot_targets(routes, experts, rows):
    tok = routes.shape[0]
    lane = lax.broadcasted_iota(jnp.int32, (tok, 128), 1)
    first = routes[:, 0:1]
    second = routes[:, 1:2]
    hot0 = jnp.where(lane == first, 1.0, 0.0)
    hot1 = jnp.where(lane == second, 1.0, 0.0)
    earlier = jnp.where(
        lax.broadcasted_iota(jnp.int32, (tok, tok), 1) < lax.broadcasted_iota(jnp.int32, (tok, tok), 0),
        1.0,
        0.0,
    )
    counts = jnp.dot(earlier.astype(BF16), (hot0 + hot1).astype(BF16), preferred_element_type=F32)
    slot0 = jnp.sum(counts * hot0, axis=1, keepdims=True).astype(jnp.int32)
    slot1 = jnp.sum(counts * hot1, axis=1, keepdims=True).astype(jnp.int32)
    return first * rows + slot0, second * rows + slot1


def bucket_kernel(experts, rows, routes_ref, x_ref, out_ref):
    tok = x_ref.shape[0]
    target0, target1 = slot_targets(routes_ref[...], experts, rows)
    column = lax.broadcasted_iota(jnp.int32, (tok, experts * rows), 1)
    chosen = jnp.where((column == target0) | (column == target1), 1.0, 0.0).astype(BF16)
    for half in range(2):
        picked = lax.dot_general(
            chosen,
            x_ref[:, half * HALF_D : (half + 1) * HALF_D],
            (((0,), (0,)), ((), ())),
            preferred_element_type=F32,
        ).astype(BF16)
        for expert in range(experts):
            out_ref[2 * expert + half] = picked[expert * rows : (expert + 1) * rows]


def build_buckets(routes, moe_input, experts, rows):
    return pl.pallas_call(
        functools.partial(bucket_kernel, experts, rows),
        out_shape=jax.ShapeDtypeStruct((2 * experts, rows, HALF_D), BF16),
        compiler_params=params(),
        name="bucket_rows",
    )(routes, moe_input)


def combine_kernel(experts, rows, routes_ref, gates_ref, back_ref, out_ref):
    tok = routes_ref.shape[0]
    target0, target1 = slot_targets(routes_ref[...], experts, rows)
    targets = jnp.concatenate([target0, target1], axis=0)
    for half in range(2):
        total = jnp.zeros((2 * tok, HALF_D), F32)
        for expert in range(experts):
            column = lax.broadcasted_iota(jnp.int32, (2 * tok, rows), 1) + expert * rows
            chosen = jnp.where(column == targets, 1.0, 0.0).astype(BF16)
            total = total + jnp.dot(chosen, back_ref[2 * expert + half], preferred_element_type=F32)
        out_ref[:, half * HALF_D : (half + 1) * HALF_D] = (
            total[:tok] * gates_ref[:, 0:1] + total[tok:] * gates_ref[:, 1:2]
        ).astype(BF16)


def combine(routes, gates, back, experts, rows):
    return pl.pallas_call(
        functools.partial(combine_kernel, experts, rows),
        out_shape=jax.ShapeDtypeStruct((routes.shape[0], D), BF16),
        compiler_params=params(),
        name="combine_routes",
    )(routes, gates, back)


STEP = 896
STEPS = HALF_D // STEP


def first_half_kernel(core_ref, x_ref, gate_ref, up_ref, gate_sum, up_sum):
    step = pl.program_id(0)
    gate = jnp.dot(x_ref[...], gate_ref[0], preferred_element_type=F32)
    up = jnp.dot(x_ref[...], up_ref[0], preferred_element_type=F32)

    @pl.when(step == 0)
    def _():
        gate_sum[...] = gate
        up_sum[...] = up

    @pl.when(step > 0)
    def _():
        gate_sum[...] += gate
        up_sum[...] += up


def first_half(core, x, gate, up):
    count = x.shape[0]
    weights = pl.BlockSpec((1, STEP, HALF), lambda k, core: (0, core[0] * STEPS + k, 0))
    sums = pl.BlockSpec((count, HALF), lambda k, core: (0, 0))
    return pl.pallas_call(
        first_half_kernel,
        grid_spec=pltpu.PrefetchScalarGridSpec(
            num_scalar_prefetch=1,
            grid=(STEPS,),
            in_specs=[pl.BlockSpec((count, STEP), lambda k, core: (0, k)), weights, weights],
            out_specs=[sums, sums],
        ),
        out_shape=[jax.ShapeDtypeStruct((count, HALF), F32)] * 2,
        compiler_params=params(),
        cost_estimate=pl.CostEstimate(
            flops=4 * count * HALF_D * HALF, bytes_accessed=4 * HALF_D * HALF + 2 * count * HALF_D, transcendentals=0
        ),
        name="hidden_own_columns",
    )(core, x, gate, up)


def second_half_kernel(core_ref, x_ref, gate_ref, up_ref, gate_in, up_in, down_ref, hidden_ref, out_ref, gate_sum, up_sum):
    step = pl.program_id(0)
    gate = jnp.dot(x_ref[...], gate_ref[0], preferred_element_type=F32)
    up = jnp.dot(x_ref[...], up_ref[0], preferred_element_type=F32)

    @pl.when(step == 0)
    def _():
        gate_sum[...] = gate_in[...] + gate
        up_sum[...] = up_in[...] + up

    @pl.when(step > 0)
    def _():
        gate_sum[...] += gate
        up_sum[...] += up

    @pl.when(step == STEPS - 1)
    def _():
        value = gate_sum[...]
        hidden = (value / (1.0 + jnp.exp(-value)) * up_sum[...]).astype(BF16)
        hidden_ref[...] = hidden
        out_ref[...] = jnp.dot(hidden, down_ref[0], preferred_element_type=F32).astype(BF16)


def second_half(core, x, gate, up, gate_sum, up_sum, down):
    count = x.shape[0]
    weights = pl.BlockSpec((1, STEP, HALF), lambda k, core: (0, (1 - core[0]) * STEPS + k, 0))
    sums = pl.BlockSpec((count, HALF), lambda k, core: (0, 0))
    return pl.pallas_call(
        second_half_kernel,
        grid_spec=pltpu.PrefetchScalarGridSpec(
            num_scalar_prefetch=1,
            grid=(STEPS,),
            in_specs=[
                pl.BlockSpec((count, STEP), lambda k, core: (0, k)),
                weights,
                weights,
                sums,
                sums,
                pl.BlockSpec((1, HALF, HALF_D), lambda k, core: (0, 0, 1 - core[0])),
            ],
            out_specs=[sums, pl.BlockSpec((count, HALF_D), lambda k, core: (0, 0))],
            scratch_shapes=[pltpu.VMEM((count, HALF), F32)] * 2,
        ),
        out_shape=[jax.ShapeDtypeStruct((count, HALF), BF16), jax.ShapeDtypeStruct((count, HALF_D), BF16)],
        compiler_params=params(),
        cost_estimate=pl.CostEstimate(
            flops=6 * count * HALF_D * HALF, bytes_accessed=6 * HALF_D * HALF + 4 * count * HALF_D, transcendentals=count * HALF
        ),
        name="hidden_other_columns",
    )(core, x, gate, up, gate_sum, up_sum, down)


def down_kernel(core_ref, hidden_ref, down_ref, other_ref, out_ref):
    own = jnp.dot(hidden_ref[...], down_ref[0], preferred_element_type=F32).astype(BF16)
    out_ref[...] = (own.astype(F32) + other_ref[...].astype(F32)).astype(BF16)


def down_own(core, hidden, down, other):
    count = hidden.shape[0]
    whole = pl.BlockSpec((count, HALF_D), lambda k, core: (0, 0))
    return pl.pallas_call(
        down_kernel,
        grid_spec=pltpu.PrefetchScalarGridSpec(
            num_scalar_prefetch=1,
            grid=(1,),
            in_specs=[
                pl.BlockSpec((count, HALF), lambda k, core: (0, 0)),
                pl.BlockSpec((1, HALF, HALF_D), lambda k, core: (0, 0, core[0])),
                whole,
            ],
            out_specs=whole,
        ),
        out_shape=jax.ShapeDtypeStruct((count, HALF_D), BF16),
        compiler_params=params(),
        cost_estimate=pl.CostEstimate(
            flops=2 * count * HALF_D * HALF, bytes_accessed=2 * HALF_D * HALF + 4 * count * HALF_D, transcendentals=0
        ),
        name="down_own_columns",
    )(core, hidden, down, other)


def split_kernel(per_device, x_ref, out_ref):
    pieces = [x_ref[:, head * (NOPE + ROPE) : head * (NOPE + ROPE) + NOPE] for head in range(per_device)]
    pieces += [x_ref[:, head * (NOPE + ROPE) + NOPE : (head + 1) * (NOPE + ROPE)] for head in range(per_device)]
    out_ref[0] = jnp.concatenate(pieces, axis=1)


def split_queries(queries, shards):
    tok = queries.shape[0]
    width = queries.shape[1] // shards
    return pl.pallas_call(
        functools.partial(split_kernel, HEADS // shards),
        grid=(shards,),
        in_specs=[pl.BlockSpec((tok, width), lambda d: (0, d))],
        out_specs=pl.BlockSpec((1, tok, width), lambda d: (d, 0, 0)),
        out_shape=jax.ShapeDtypeStruct((shards, tok, width), BF16),
        compiler_params=params(),
        name="split_queries",
    )(queries)


BLOCK = 256
EXP_SCALE = math.log2(math.e) / math.sqrt(NOPE + ROPE)


def attention_kernel(nope_ref, rope_ref, kv_ref, key_ref, value_ref, out_ref, keys):
    head = pl.program_id(0)

    @pl.when(head == 0)
    def _():
        keys[:, : LATENT + ROPE] = kv_ref[...]
        keys[:, LATENT + ROPE :] = kv_ref[:, LATENT:]

    side = lax.broadcasted_iota(jnp.int32, (1, 2 * ROPE), 1) // ROPE == head % 2
    below = lax.broadcasted_iota(jnp.int32, (BLOCK, BLOCK), 1) <= lax.broadcasted_iota(
        jnp.int32, (BLOCK, BLOCK), 0
    )
    contract = (((1,), (1,)), ((), ()))
    for block in range(nope_ref.shape[0] // BLOCK):
        start = block * BLOCK
        rows = pl.ds(start, BLOCK)
        latent = jnp.dot(nope_ref[rows, :], key_ref[0], preferred_element_type=F32).astype(BF16)
        rope = jnp.where(side, rope_ref[rows, :], jnp.zeros((), BF16))
        query = jnp.concatenate([latent, rope], axis=1)
        diagonal = lax.dot_general(query, keys[rows, :], contract, preferred_element_type=F32)
        diagonal = jnp.where(below, diagonal, -1e30)
        top = jnp.max(diagonal, axis=1, keepdims=True)
        if block:
            past = lax.dot_general(query, keys[:start, :], contract, preferred_element_type=F32)
            top = jnp.maximum(top, jnp.max(past, axis=1, keepdims=True))
        weights = jnp.exp2((diagonal - top) * EXP_SCALE)
        total = jnp.sum(weights, axis=1, keepdims=True)
        mixed = jnp.dot(weights.astype(BF16), keys[rows, :LATENT], preferred_element_type=F32)
        if block:
            weights = jnp.exp2((past - top) * EXP_SCALE)
            total = total + jnp.sum(weights, axis=1, keepdims=True)
            mixed = mixed + jnp.dot(weights.astype(BF16), keys[:start, :LATENT], preferred_element_type=F32)
        mixed = (mixed / total).astype(BF16)
        out_ref[rows, :] = jnp.dot(mixed, value_ref[0], preferred_element_type=F32).astype(BF16)


def attention(queries, keys, key_proj, value_proj):
    length = queries.shape[0]
    heads = key_proj.shape[0]
    return pl.pallas_call(
        attention_kernel,
        grid=(heads,),
        in_specs=[
            pl.BlockSpec((length, NOPE), lambda h: (0, h)),
            pl.BlockSpec((length, 2 * ROPE), lambda h: (0, heads + h // 2)),
            pl.BlockSpec((length, LATENT + ROPE), lambda h: (0, 0)),
            pl.BlockSpec((1, NOPE, LATENT), lambda h: (h, 0, 0)),
            pl.BlockSpec((1, LATENT, VDIM), lambda h: (h, 0, 0)),
        ],
        out_specs=pl.BlockSpec((length, VDIM), lambda h: (0, h)),
        out_shape=jax.ShapeDtypeStruct((length, heads * VDIM), BF16),
        scratch_shapes=[pltpu.VMEM((length, LATENT + 2 * ROPE), BF16)],
        compiler_params=params(),
        cost_estimate=pl.CostEstimate(
            flops=2 * heads * length * length * (LATENT + ROPE),
            bytes_accessed=8 * length * LATENT,
            transcendentals=heads * length * length // 2,
        ),
        name="causal_attention",
    )(queries, queries, keys, key_proj, value_proj)


def on_device(
    queries,
    latent_kv,
    key_proj,
    value_proj,
    moe_input,
    routes,
    gates,
    expert_gate,
    expert_up,
    expert_down,
):
    shards = lax.axis_size("ctx")
    tok = queries.shape[0]
    experts = shards // 2
    capacity = 2 * ((4 * tok * TOP + 6 * experts - 1) // (6 * experts))
    rows = -(-capacity // 8) * 8
    core = (lax.axis_index("ctx") % 2).astype(jnp.int32).reshape(1)
    swap = [(i, i ^ 1) for i in range(shards)]

    keys = lax.all_gather(latent_kv, "ctx", axis=0, tiled=True)

    buckets = build_buckets(routes, moe_input, experts, rows)
    arrived = lax.all_to_all(buckets, "ctx", split_axis=0, concat_axis=0, tiled=True)
    own = arrived.reshape(shards * rows, HALF_D)
    other = lax.ppermute(own, "ctx", swap)

    sent = split_queries(queries, shards)
    held = lax.all_to_all(sent, "ctx", split_axis=0, concat_axis=0, tiled=True)

    gate_sum, up_sum = first_half(core, own, expert_gate, expert_up)
    hidden, for_other = second_half(core, other, expert_gate, expert_up, gate_sum, up_sum, expert_down)
    from_other = lax.ppermute(for_other, "ctx", swap)
    result = down_own(core, hidden, expert_down, from_other).reshape(shards, rows, HALF_D)
    back = lax.all_to_all(result, "ctx", split_axis=0, concat_axis=0, tiled=True)

    held = held.reshape(shards * tok, held.shape[2])
    values = attention(held, keys, key_proj, value_proj)
    values = lax.all_to_all(
        values.reshape(shards, tok, values.shape[1]), "ctx", split_axis=0, concat_axis=0, tiled=True
    )
    attention_out = values.transpose(1, 0, 2).reshape(tok, HEADS * VDIM)

    moe_out = combine(routes, gates, back, experts, rows)
    return (attention_out, moe_out)


def solution(mesh):
    return jax.shard_map(
        on_device,
        mesh=mesh,
        in_specs=(
            P(("groups", "ctx"), None),
            P(("groups", "ctx"), None),
            P("ctx", None, None),
            P("ctx", None, None),
            P(("groups", "ctx"), None),
            P(("groups", "ctx"), None),
            P(("groups", "ctx"), None),
            P("ctx", None, None),
            P("ctx", None, None),
            P("ctx", None, None),
        ),
        out_specs=(P(("groups", "ctx"), None), P(("groups", "ctx"), None)),
        check_vma=False,
    )
```

```python
import functools
import math

import jax
import jax.numpy as jnp
from jax import lax
from jax.experimental import pallas as pl
from jax.experimental.pallas import tpu as pltpu
from jax.sharding import PartitionSpec as P

D = 3584
HEADS = 64
NOPE = 128
ROPE = 64
LATENT = 512
VDIM = 128
TOP = 2
HALF = 512
HALF_D = D // 2
VMEM_LIMIT = 50 * 1024 * 1024
F32 = jnp.float32
BF16 = jnp.bfloat16


def params(limit=VMEM_LIMIT):
    return pltpu.CompilerParams(vmem_limit_bytes=limit)


def slot_targets(routes, experts, rows):
    tok = routes.shape[0]
    lane = lax.broadcasted_iota(jnp.int32, (tok, 128), 1)
    first = routes[:, 0:1]
    second = routes[:, 1:2]
    hot0 = jnp.where(lane == first, 1.0, 0.0)
    hot1 = jnp.where(lane == second, 1.0, 0.0)
    earlier = jnp.where(
        lax.broadcasted_iota(jnp.int32, (tok, tok), 1) < lax.broadcasted_iota(jnp.int32, (tok, tok), 0),
        1.0,
        0.0,
    )
    counts = jnp.dot(earlier.astype(BF16), (hot0 + hot1).astype(BF16), preferred_element_type=F32)
    slot0 = jnp.sum(counts * hot0, axis=1, keepdims=True).astype(jnp.int32)
    slot1 = jnp.sum(counts * hot1, axis=1, keepdims=True).astype(jnp.int32)
    return first * rows + slot0, second * rows + slot1


def bucket_kernel(experts, rows, routes_ref, x_ref, out_ref):
    tok = x_ref.shape[0]
    target0, target1 = slot_targets(routes_ref[...], experts, rows)
    column = lax.broadcasted_iota(jnp.int32, (tok, experts * rows), 1)
    chosen = jnp.where((column == target0) | (column == target1), 1.0, 0.0).astype(BF16)
    for half in range(2):
        picked = lax.dot_general(
            chosen,
            x_ref[:, half * HALF_D : (half + 1) * HALF_D],
            (((0,), (0,)), ((), ())),
            preferred_element_type=F32,
        ).astype(BF16)
        for expert in range(experts):
            out_ref[2 * expert + half] = picked[expert * rows : (expert + 1) * rows]


def build_buckets(routes, moe_input, experts, rows):
    return pl.pallas_call(
        functools.partial(bucket_kernel, experts, rows),
        out_shape=jax.ShapeDtypeStruct((2 * experts, rows, HALF_D), BF16),
        compiler_params=params(),
        name="bucket_rows",
    )(routes, moe_input)


def combine_kernel(experts, rows, routes_ref, gates_ref, back_ref, out_ref):
    tok = routes_ref.shape[0]
    target0, target1 = slot_targets(routes_ref[...], experts, rows)
    targets = jnp.concatenate([target0, target1], axis=0)
    for half in range(2):
        total = jnp.zeros((2 * tok, HALF_D), F32)
        for expert in range(experts):
            column = lax.broadcasted_iota(jnp.int32, (2 * tok, rows), 1) + expert * rows
            chosen = jnp.where(column == targets, 1.0, 0.0).astype(BF16)
            total = total + jnp.dot(chosen, back_ref[2 * expert + half], preferred_element_type=F32)
        out_ref[:, half * HALF_D : (half + 1) * HALF_D] = (
            total[:tok] * gates_ref[:, 0:1] + total[tok:] * gates_ref[:, 1:2]
        ).astype(BF16)


def combine(routes, gates, back, experts, rows):
    return pl.pallas_call(
        functools.partial(combine_kernel, experts, rows),
        out_shape=jax.ShapeDtypeStruct((routes.shape[0], D), BF16),
        compiler_params=params(),
        name="combine_routes",
    )(routes, gates, back)


STEP = 896
STEPS = HALF_D // STEP


def first_half_kernel(core_ref, x_ref, gate_ref, up_ref, gate_sum, up_sum):
    step = pl.program_id(0)
    gate = jnp.dot(x_ref[...], gate_ref[0], preferred_element_type=F32)
    up = jnp.dot(x_ref[...], up_ref[0], preferred_element_type=F32)

    @pl.when(step == 0)
    def _():
        gate_sum[...] = gate
        up_sum[...] = up

    @pl.when(step > 0)
    def _():
        gate_sum[...] += gate
        up_sum[...] += up


def first_half(core, x, gate, up):
    count = x.shape[0]
    weights = pl.BlockSpec((1, STEP, HALF), lambda k, core: (0, core[0] * STEPS + k, 0))
    sums = pl.BlockSpec((count, HALF), lambda k, core: (0, 0))
    return pl.pallas_call(
        first_half_kernel,
        grid_spec=pltpu.PrefetchScalarGridSpec(
            num_scalar_prefetch=1,
            grid=(STEPS,),
            in_specs=[pl.BlockSpec((count, STEP), lambda k, core: (0, k)), weights, weights],
            out_specs=[sums, sums],
        ),
        out_shape=[jax.ShapeDtypeStruct((count, HALF), F32)] * 2,
        compiler_params=params(),
        cost_estimate=pl.CostEstimate(
            flops=4 * count * HALF_D * HALF, bytes_accessed=4 * HALF_D * HALF + 2 * count * HALF_D, transcendentals=0
        ),
        name="hidden_own_columns",
    )(core, x, gate, up)


def second_half_kernel(core_ref, x_ref, gate_ref, up_ref, gate_in, up_in, down_ref, hidden_ref, out_ref, gate_sum, up_sum):
    step = pl.program_id(0)
    gate = jnp.dot(x_ref[...], gate_ref[0], preferred_element_type=F32)
    up = jnp.dot(x_ref[...], up_ref[0], preferred_element_type=F32)

    @pl.when(step == 0)
    def _():
        gate_sum[...] = gate_in[...] + gate
        up_sum[...] = up_in[...] + up

    @pl.when(step > 0)
    def _():
        gate_sum[...] += gate
        up_sum[...] += up

    @pl.when(step == STEPS - 1)
    def _():
        value = gate_sum[...]
        hidden = (value / (1.0 + jnp.exp(-value)) * up_sum[...]).astype(BF16)
        hidden_ref[...] = hidden
        out_ref[...] = jnp.dot(hidden, down_ref[0], preferred_element_type=F32).astype(BF16)


def second_half(core, x, gate, up, gate_sum, up_sum, down):
    count = x.shape[0]
    weights = pl.BlockSpec((1, STEP, HALF), lambda k, core: (0, (1 - core[0]) * STEPS + k, 0))
    sums = pl.BlockSpec((count, HALF), lambda k, core: (0, 0))
    return pl.pallas_call(
        second_half_kernel,
        grid_spec=pltpu.PrefetchScalarGridSpec(
            num_scalar_prefetch=1,
            grid=(STEPS,),
            in_specs=[
                pl.BlockSpec((count, STEP), lambda k, core: (0, k)),
                weights,
                weights,
                sums,
                sums,
                pl.BlockSpec((1, HALF, HALF_D), lambda k, core: (0, 0, 1 - core[0])),
            ],
            out_specs=[sums, pl.BlockSpec((count, HALF_D), lambda k, core: (0, 0))],
            scratch_shapes=[pltpu.VMEM((count, HALF), F32)] * 2,
        ),
        out_shape=[jax.ShapeDtypeStruct((count, HALF), BF16), jax.ShapeDtypeStruct((count, HALF_D), BF16)],
        compiler_params=params(),
        cost_estimate=pl.CostEstimate(
            flops=6 * count * HALF_D * HALF, bytes_accessed=6 * HALF_D * HALF + 4 * count * HALF_D, transcendentals=count * HALF
        ),
        name="hidden_other_columns",
    )(core, x, gate, up, gate_sum, up_sum, down)


def down_kernel(core_ref, hidden_ref, down_ref, other_ref, out_ref):
    own = jnp.dot(hidden_ref[...], down_ref[0], preferred_element_type=F32).astype(BF16)
    out_ref[...] = (own.astype(F32) + other_ref[...].astype(F32)).astype(BF16)


def down_own(core, hidden, down, other):
    count = hidden.shape[0]
    whole = pl.BlockSpec((count, HALF_D), lambda k, core: (0, 0))
    return pl.pallas_call(
        down_kernel,
        grid_spec=pltpu.PrefetchScalarGridSpec(
            num_scalar_prefetch=1,
            grid=(1,),
            in_specs=[
                pl.BlockSpec((count, HALF), lambda k, core: (0, 0)),
                pl.BlockSpec((1, HALF, HALF_D), lambda k, core: (0, 0, core[0])),
                whole,
            ],
            out_specs=whole,
        ),
        out_shape=jax.ShapeDtypeStruct((count, HALF_D), BF16),
        compiler_params=params(),
        cost_estimate=pl.CostEstimate(
            flops=2 * count * HALF_D * HALF, bytes_accessed=2 * HALF_D * HALF + 4 * count * HALF_D, transcendentals=0
        ),
        name="down_own_columns",
    )(core, hidden, down, other)


def split_kernel(per_device, x_ref, out_ref):
    pieces = [x_ref[:, head * (NOPE + ROPE) : head * (NOPE + ROPE) + NOPE] for head in range(per_device)]
    pieces += [x_ref[:, head * (NOPE + ROPE) + NOPE : (head + 1) * (NOPE + ROPE)] for head in range(per_device)]
    out_ref[0] = jnp.concatenate(pieces, axis=1)


def split_queries(queries, shards):
    tok = queries.shape[0]
    width = queries.shape[1] // shards
    return pl.pallas_call(
        functools.partial(split_kernel, HEADS // shards),
        grid=(shards,),
        in_specs=[pl.BlockSpec((tok, width), lambda d: (0, d))],
        out_specs=pl.BlockSpec((1, tok, width), lambda d: (d, 0, 0)),
        out_shape=jax.ShapeDtypeStruct((shards, tok, width), BF16),
        compiler_params=params(),
        name="split_queries",
    )(queries)


BLOCK = 256
EXP_SCALE = math.log2(math.e) / math.sqrt(NOPE + ROPE)


def attention_kernel(rank_ref, nope_ref, rope_ref, kv_ref, key_ref, value_ref, out_ref, keys):
    head = pl.program_id(0)
    shards, tok = kv_ref.shape[:2]

    @pl.when(head == 0)
    def _():
        for place, offset in enumerate(doubling_masks(shards)[1]):
            rows = pl.ds(pl.multiple_of((rank_ref[0] ^ offset) * tok, tok), tok)
            keys[rows, : LATENT + ROPE] = kv_ref[place]
            keys[rows, LATENT + ROPE :] = kv_ref[place, :, LATENT:]

    side = lax.broadcasted_iota(jnp.int32, (1, 2 * ROPE), 1) // ROPE == head % 2
    below = lax.broadcasted_iota(jnp.int32, (BLOCK, BLOCK), 1) <= lax.broadcasted_iota(
        jnp.int32, (BLOCK, BLOCK), 0
    )
    contract = (((1,), (1,)), ((), ()))
    for block in range(nope_ref.shape[0] // BLOCK):
        start = block * BLOCK
        rows = pl.ds(start, BLOCK)
        latent = jnp.dot(nope_ref[rows, :], key_ref[0], preferred_element_type=F32).astype(BF16)
        rope = jnp.where(side, rope_ref[rows, :], jnp.zeros((), BF16))
        query = jnp.concatenate([latent, rope], axis=1)
        diagonal = lax.dot_general(query, keys[rows, :], contract, preferred_element_type=F32)
        diagonal = jnp.where(below, diagonal, -1e30)
        top = jnp.max(diagonal, axis=1, keepdims=True)
        if block:
            past = lax.dot_general(query, keys[:start, :], contract, preferred_element_type=F32)
            top = jnp.maximum(top, jnp.max(past, axis=1, keepdims=True))
        weights = jnp.exp2((diagonal - top) * EXP_SCALE)
        total = jnp.sum(weights, axis=1, keepdims=True)
        mixed = jnp.dot(weights.astype(BF16), keys[rows, :LATENT], preferred_element_type=F32)
        if block:
            weights = jnp.exp2((past - top) * EXP_SCALE)
            total = total + jnp.sum(weights, axis=1, keepdims=True)
            mixed = mixed + jnp.dot(weights.astype(BF16), keys[:start, :LATENT], preferred_element_type=F32)
        mixed = (mixed / total).astype(BF16)
        out_ref[rows, :] = jnp.dot(mixed, value_ref[0], preferred_element_type=F32).astype(BF16)


def attention(rank, queries, keys, key_proj, value_proj):
    length = queries.shape[0]
    heads = key_proj.shape[0]
    return pl.pallas_call(
        attention_kernel,
        grid_spec=pltpu.PrefetchScalarGridSpec(
            num_scalar_prefetch=1,
            grid=(heads,),
            in_specs=[
                pl.BlockSpec((length, NOPE), lambda h, rank: (0, h)),
                pl.BlockSpec((length, 2 * ROPE), lambda h, rank: (0, heads + h // 2)),
                pl.BlockSpec(keys.shape, lambda h, rank: (0, 0, 0)),
                pl.BlockSpec((1, NOPE, LATENT), lambda h, rank: (h, 0, 0)),
                pl.BlockSpec((1, LATENT, VDIM), lambda h, rank: (h, 0, 0)),
            ],
            out_specs=pl.BlockSpec((length, VDIM), lambda h, rank: (0, h)),
            scratch_shapes=[pltpu.VMEM((length, LATENT + 2 * ROPE), BF16)],
        ),
        out_shape=jax.ShapeDtypeStruct((length, heads * VDIM), BF16),
        compiler_params=params(),
        cost_estimate=pl.CostEstimate(
            flops=2 * heads * length * length * (LATENT + ROPE),
            bytes_accessed=8 * length * LATENT,
            transcendentals=heads * length * length // 2,
        ),
        name="causal_attention",
    )(rank, queries, queries, keys, key_proj, value_proj)


def exchange(blocks, mask):
    met = lax.ppermute(blocks, "ctx", [(i, i ^ mask) for i in range(lax.axis_size("ctx"))])
    return jnp.concatenate([blocks, met], axis=0)


def doubling_masks(shards):
    steps = [1 << bit for bit in reversed(range(shards.bit_length() - 1))]
    order = [0]
    for mask in steps:
        order = order + [offset ^ mask for offset in order]
    return steps, order


def on_device(
    queries,
    latent_kv,
    key_proj,
    value_proj,
    moe_input,
    routes,
    gates,
    expert_gate,
    expert_up,
    expert_down,
):
    shards = lax.axis_size("ctx")
    tok = queries.shape[0]
    experts = shards // 2
    capacity = 2 * ((4 * tok * TOP + 6 * experts - 1) // (6 * experts))
    rows = -(-capacity // 8) * 8
    rank = lax.axis_index("ctx").astype(jnp.int32).reshape(1)
    core = rank % 2
    swap = [(i, i ^ 1) for i in range(shards)]

    keys = latent_kv[None]
    for mask in doubling_masks(shards)[0]:
        keys = exchange(keys, mask)

    buckets = build_buckets(routes, moe_input, experts, rows)
    arrived = lax.all_to_all(buckets, "ctx", split_axis=0, concat_axis=0, tiled=True)
    own = arrived.reshape(shards * rows, HALF_D)
    other = lax.ppermute(own, "ctx", swap)

    sent = split_queries(queries, shards)
    held = lax.all_to_all(sent, "ctx", split_axis=0, concat_axis=0, tiled=True)

    gate_sum, up_sum = first_half(core, own, expert_gate, expert_up)
    hidden, for_other = second_half(core, other, expert_gate, expert_up, gate_sum, up_sum, expert_down)
    from_other = lax.ppermute(for_other, "ctx", swap)
    result = down_own(core, hidden, expert_down, from_other).reshape(shards, rows, HALF_D)

    held = held.reshape(shards * tok, held.shape[2])
    result, held = lax.optimization_barrier((result, held))
    back = lax.all_to_all(result, "ctx", split_axis=0, concat_axis=0, tiled=True)
    values = attention(rank, held, keys, key_proj, value_proj)
    values = lax.all_to_all(
        values.reshape(shards, tok, values.shape[1]), "ctx", split_axis=0, concat_axis=0, tiled=True
    )
    attention_out = values.transpose(1, 0, 2).reshape(tok, HEADS * VDIM)

    moe_out = combine(routes, gates, back, experts, rows)
    return (attention_out, moe_out)


def solution(mesh):
    return jax.shard_map(
        on_device,
        mesh=mesh,
        in_specs=(
            P(("groups", "ctx"), None),
            P(("groups", "ctx"), None),
            P("ctx", None, None),
            P("ctx", None, None),
            P(("groups", "ctx"), None),
            P(("groups", "ctx"), None),
            P(("groups", "ctx"), None),
            P("ctx", None, None),
            P("ctx", None, None),
            P("ctx", None, None),
        ),
        out_specs=(P(("groups", "ctx"), None), P(("groups", "ctx"), None)),
        check_vma=False,
    )
```

```python
import functools
import math

import jax
import jax.numpy as jnp
from jax import lax
from jax.experimental import pallas as pl
from jax.experimental.pallas import tpu as pltpu
from jax.sharding import PartitionSpec as P

D = 3584
HEADS = 64
NOPE = 128
ROPE = 64
LATENT = 512
VDIM = 128
TOP = 2
HALF = 512
VMEM_LIMIT = 50 * 1024 * 1024
F32 = jnp.float32
BF16 = jnp.bfloat16


SMEM = pl.BlockSpec(memory_space=pltpu.SMEM)
VMEM = pl.BlockSpec(memory_space=pltpu.VMEM)
SMALL = pl.CostEstimate(flops=1, bytes_accessed=1, transcendentals=0)


def call(kernel, name, **options):
    return pl.pallas_call(
        kernel,
        name=name,
        cost_estimate=SMALL,
        compiler_params=pltpu.CompilerParams(vmem_limit_bytes=VMEM_LIMIT),
        **options,
    )


def slot_targets(routes, rows):
    tok = routes.shape[0]
    lane = lax.broadcasted_iota(jnp.int32, (tok, 128), 1)
    first = routes[:, 0:1]
    second = routes[:, 1:2]
    hot0 = jnp.where(lane == first, 1.0, 0.0)
    hot1 = jnp.where(lane == second, 1.0, 0.0)
    earlier = jnp.where(
        lax.broadcasted_iota(jnp.int32, (tok, tok), 1) < lax.broadcasted_iota(jnp.int32, (tok, tok), 0),
        1.0,
        0.0,
    )
    counts = jnp.dot(earlier.astype(BF16), (hot0 + hot1).astype(BF16), preferred_element_type=F32)
    slot0 = jnp.sum(counts * hot0, axis=1, keepdims=True).astype(jnp.int32)
    slot1 = jnp.sum(counts * hot1, axis=1, keepdims=True).astype(jnp.int32)
    return first * rows + slot0, second * rows + slot1


def bucket_kernel(rows, routes_ref, x_ref, out_ref):
    target0, target1 = slot_targets(routes_ref[...], rows)
    column = lax.broadcasted_iota(jnp.int32, (x_ref.shape[0], out_ref.shape[0]), 1)
    chosen = jnp.where((column == target0) | (column == target1), 1.0, 0.0).astype(BF16)
    out_ref[...] = lax.dot_general(
        chosen, x_ref[...], (((0,), (0,)), ((), ())), preferred_element_type=F32
    ).astype(BF16)


def build_buckets(routes, moe_input, experts, rows):
    return call(
        functools.partial(bucket_kernel, rows),
        "bucket_rows",
        out_shape=jax.ShapeDtypeStruct((experts * rows, D), BF16),
    )(routes, moe_input)


def combine_kernel(rows, routes_ref, gates_ref, back_ref, out_ref):
    tok = routes_ref.shape[0]
    target0, target1 = slot_targets(routes_ref[...], rows)
    targets = jnp.concatenate([target0, target1], axis=0)
    column = lax.broadcasted_iota(jnp.int32, (2 * tok, back_ref.shape[0]), 1)
    chosen = jnp.where(column == targets, 1.0, 0.0).astype(BF16)
    picked = jnp.dot(chosen, back_ref[...], preferred_element_type=F32)
    out_ref[...] = (picked[:tok] * gates_ref[:, 0:1] + picked[tok:] * gates_ref[:, 1:2]).astype(BF16)


def combine(routes, gates, back, rows):
    return call(
        functools.partial(combine_kernel, rows),
        "combine_routes",
        out_shape=jax.ShapeDtypeStruct((routes.shape[0], D), BF16),
    )(routes, gates, back)


STEP = 896
STEPS = D // STEP


def hidden_kernel(own_ref, other_ref, gate_ref, up_ref, down_ref, hidden_ref, out_ref, gate_sum, up_sum):
    step = pl.program_id(0)
    count = own_ref.shape[0]
    x = jnp.concatenate([own_ref[...], other_ref[...]], axis=0)
    gate = jnp.dot(x, gate_ref[0], preferred_element_type=F32)
    up = jnp.dot(x, up_ref[0], preferred_element_type=F32)

    @pl.when(step == 0)
    def _():
        gate_sum[...] = gate
        up_sum[...] = up

    @pl.when(step > 0)
    def _():
        gate_sum[...] += gate
        up_sum[...] += up

    @pl.when(step == STEPS - 1)
    def _():
        value = gate_sum[...]
        hidden = (value / (1.0 + jnp.exp(-value)) * up_sum[...]).astype(BF16)
        hidden_ref[...] = hidden[:count]
        out_ref[...] = jnp.dot(hidden[count:], down_ref[0], preferred_element_type=F32).astype(BF16)


def hidden_rows(own, other, gate, up, down):
    count = own.shape[0]
    part = pl.BlockSpec((count, STEP), lambda k: (0, k))
    weights = pl.BlockSpec((1, STEP, HALF), lambda k: (0, k, 0))
    return call(
        hidden_kernel,
        "expert_hidden",
        grid=(STEPS,),
        in_specs=[part, part, weights, weights, pl.BlockSpec((1, HALF, D), lambda k: (0, 0, 0))],
        out_specs=[
            pl.BlockSpec((count, HALF), lambda k: (0, 0)),
            pl.BlockSpec((count, D), lambda k: (0, 0)),
        ],
        scratch_shapes=[pltpu.VMEM((2 * count, HALF), F32)] * 2,
        out_shape=[jax.ShapeDtypeStruct((count, HALF), BF16), jax.ShapeDtypeStruct((count, D), BF16)],
    )(own, other, gate, up, down)


def down_kernel(hidden_ref, down_ref, other_ref, out_ref):
    own = jnp.dot(hidden_ref[...], down_ref[0], preferred_element_type=F32).astype(BF16)
    out_ref[...] = (own.astype(F32) + other_ref[...].astype(F32)).astype(BF16)


def down_own(hidden, down, other):
    return call(down_kernel, "down_own_rows", out_shape=jax.ShapeDtypeStruct(other.shape, BF16))(
        hidden, down, other
    )


def split_kernel(x_ref, out_ref):
    each = NOPE + ROPE
    heads = range(x_ref.shape[1] // each)
    pieces = [x_ref[:, head * each : head * each + NOPE] for head in heads]
    pieces += [x_ref[:, head * each + NOPE : (head + 1) * each] for head in heads]
    out_ref[0] = jnp.concatenate(pieces, axis=1)


def split_queries(queries, chips):
    tok = queries.shape[0]
    width = queries.shape[1] // chips
    return call(
        split_kernel,
        "split_queries",
        grid=(chips,),
        in_specs=[pl.BlockSpec((tok, width), lambda d: (0, d))],
        out_specs=pl.BlockSpec((1, tok, width), lambda d: (d, 0, 0)),
        out_shape=jax.ShapeDtypeStruct((chips, tok, width), BF16),
    )(queries)


BLOCK = 128
SPAN = 2 * BLOCK
EXP_SCALE = math.log2(math.e) / math.sqrt(NOPE + ROPE)


def attention_kernel(
    per_core,
    rank_ref,
    plain_ref,
    rope_ref,
    kv_ref,
    own_key_ref,
    other_key_ref,
    own_value_ref,
    other_value_ref,
    out_ref,
    keys,
    queries,
    mixed,
):
    pair = pl.program_id(0)
    shards, tok = kv_ref.shape[:2]
    count = plain_ref.shape[0]
    core = rank_ref[0] & 1
    mine = pair // per_core == core

    @pl.when(pair == 0)
    def _():
        for index, offset in enumerate(gather_order(shards)):
            place = pl.ds(pl.multiple_of((rank_ref[0] ^ offset) * tok, tok), tok)
            keys[place, : LATENT + ROPE] = kv_ref[index]
            keys[place, LATENT + ROPE :] = kv_ref[index, :, LATENT:]

    side = lax.broadcasted_iota(jnp.int32, (1, 2 * ROPE), 1) // ROPE
    for one in range(2):
        key = jnp.where(mine, own_key_ref[one], other_key_ref[one])
        latent = jnp.dot(plain_ref[:, one * NOPE : (one + 1) * NOPE], key, preferred_element_type=F32)
        queries[one, :, :LATENT] = latent.astype(BF16)
        queries[one, :, LATENT:] = jnp.where(side == one, rope_ref[...], jnp.zeros((), BF16))

    row = lax.broadcasted_iota(jnp.int32, (2 * BLOCK, SPAN), 0) % BLOCK
    position = (2 * (row // tok) + core) * tok + row % tok
    visible = lax.broadcasted_iota(jnp.int32, (2 * BLOCK, SPAN), 1) <= position
    contract = (((1,), (1,)), ((), ()))
    for block in range(count // BLOCK):
        start = block * SPAN
        rows = pl.ds(block * BLOCK, BLOCK)
        last = pl.ds(start, SPAN)
        query = jnp.concatenate([queries[0, rows, :], queries[1, rows, :]], axis=0)
        near = lax.dot_general(query, keys[last, :], contract, preferred_element_type=F32)
        near = jnp.where(visible, near, -1e30)
        top = jnp.max(near, axis=1, keepdims=True)
        if block:
            past = lax.dot_general(query, keys[:start, :], contract, preferred_element_type=F32)
            top = jnp.maximum(top, jnp.max(past, axis=1, keepdims=True))
        weights = jnp.exp2((near - top) * EXP_SCALE)
        total = jnp.sum(weights, axis=1, keepdims=True)
        summed = jnp.dot(weights.astype(BF16), keys[last, :LATENT], preferred_element_type=F32)
        if block:
            weights = jnp.exp2((past - top) * EXP_SCALE)
            total = total + jnp.sum(weights, axis=1, keepdims=True)
            summed = summed + jnp.dot(weights.astype(BF16), keys[:start, :LATENT], preferred_element_type=F32)
        result = (summed / total).astype(BF16)
        mixed[0, rows, :] = result[:BLOCK]
        mixed[1, rows, :] = result[BLOCK:]

    for one in range(2):
        value = jnp.where(mine, own_value_ref[one], other_value_ref[one])
        out_ref[:, one * VDIM : (one + 1) * VDIM] = jnp.dot(
            mixed[one], value, preferred_element_type=F32
        ).astype(BF16)


def attention(rank, queries, keys, key_proj, other_key, value_proj, other_value):
    count = queries.shape[0]
    pairs = key_proj.shape[0]
    per_core = pairs // 2
    key_spec = pl.BlockSpec((2, NOPE, LATENT), lambda p, rank: (p % per_core, 0, 0))
    value_spec = pl.BlockSpec((2, LATENT, VDIM), lambda p, rank: (p % per_core, 0, 0))
    return call(
        functools.partial(attention_kernel, per_core),
        "causal_attention",
        grid_spec=pltpu.PrefetchScalarGridSpec(
            num_scalar_prefetch=1,
            grid=(pairs,),
            in_specs=[
                pl.BlockSpec((count, 2 * NOPE), lambda p, rank: (0, p)),
                pl.BlockSpec((count, 2 * ROPE), lambda p, rank: (0, 2 * pairs + p)),
                pl.BlockSpec(keys.shape, lambda p, rank: (0, 0, 0)),
                key_spec,
                key_spec,
                value_spec,
                value_spec,
            ],
            out_specs=pl.BlockSpec((count, 2 * VDIM), lambda p, rank: (0, p)),
            scratch_shapes=[
                pltpu.VMEM((keys.shape[0] * keys.shape[1], LATENT + 2 * ROPE), BF16),
                pltpu.VMEM((2, count, LATENT + 2 * ROPE), BF16),
                pltpu.VMEM((2, count, LATENT), BF16),
            ],
        ),
        out_shape=jax.ShapeDtypeStruct((count, 2 * pairs * VDIM), BF16),
    )(rank, queries, queries, keys, key_proj, other_key, value_proj, other_value)


def send(array, mask):
    return lax.ppermute(array, "ctx", [(i, i ^ mask) for i in range(lax.axis_size("ctx"))])


def swap_chips(array):
    shards = lax.axis_size("ctx")
    return lax.all_to_all(
        array,
        "ctx",
        split_axis=0,
        concat_axis=0,
        axis_index_groups=[list(range(core, shards, 2)) for core in range(2)],
        tiled=True,
    )


def after(array, *others):
    return lax.optimization_barrier((array, *others))[0]


def gather_order(shards):
    top, below = shards // 2, shards // 4
    order = [0, top, below, top ^ below]
    mask = below // 2
    while mask:
        order = order + [offset ^ mask for offset in order]
        mask //= 2
    return order


def on_device(
    queries,
    latent_kv,
    key_proj,
    value_proj,
    moe_input,
    routes,
    gates,
    expert_gate,
    expert_up,
    expert_down,
):
    shards = lax.axis_size("ctx")
    tok = queries.shape[0]
    experts = shards // 2
    capacity = 2 * ((4 * tok * TOP + 6 * experts - 1) // (6 * experts))
    rows = -(-capacity // 8) * 8
    rank = lax.axis_index("ctx").astype(jnp.int32).reshape(1)

    keys = jnp.stack([latent_kv] + [send(latent_kv, offset) for offset in gather_order(shards)[1:4]])
    other_key = send(key_proj, 1)
    other_value = send(value_proj, 1)

    buckets = after(build_buckets(routes, moe_input, experts, rows), keys)
    own = swap_chips(buckets.reshape(experts, rows, D))
    sent = after(split_queries(queries, experts), own)
    held = swap_chips(sent)

    own = own.reshape(experts * rows, D)
    mask = shards // 8
    while mask:
        keys = jnp.concatenate([keys, send(keys, mask)], axis=0)
        mask //= 2
    other = send(own, 1)
    own = after(own, keys, other_key, other_value)
    hidden, for_other = hidden_rows(own, other, expert_gate, expert_up, expert_down)
    result = down_own(hidden, expert_down, send(for_other, 1))

    result, held = lax.optimization_barrier((result, held))
    back = swap_chips(result.reshape(experts, rows, D))
    values = attention(
        rank, held.reshape(experts * tok, held.shape[2]), keys, key_proj, other_key, value_proj, other_value
    )
    values, back = lax.optimization_barrier((values, back))
    values = swap_chips(values.reshape(experts, tok, values.shape[1]))
    moe_out = combine(routes, gates, back.reshape(experts * rows, D), rows)
    attention_out = values.transpose(1, 0, 2).reshape(tok, HEADS * VDIM)
    return (attention_out, moe_out)


def solution(mesh):
    return jax.shard_map(
        on_device,
        mesh=mesh,
        in_specs=(
            P(("groups", "ctx"), None),
            P(("groups", "ctx"), None),
            P("ctx", None, None),
            P("ctx", None, None),
            P(("groups", "ctx"), None),
            P(("groups", "ctx"), None),
            P(("groups", "ctx"), None),
            P("ctx", None, None),
            P("ctx", None, None),
            P("ctx", None, None),
        ),
        out_specs=(P(("groups", "ctx"), None), P(("groups", "ctx"), None)),
        check_vma=False,
    )
```

```python
import functools
import math

import jax
import jax.numpy as jnp
from jax import lax
from jax.experimental import pallas as pl
from jax.experimental.pallas import tpu as pltpu
from jax.sharding import PartitionSpec as P

D = 3584
HEADS = 64
NOPE = 128
ROPE = 64
LATENT = 512
VDIM = 128
TOP = 2
HALF = 512
VMEM_LIMIT = 50 * 1024 * 1024
F32 = jnp.float32
BF16 = jnp.bfloat16


SMEM = pl.BlockSpec(memory_space=pltpu.SMEM)
VMEM = pl.BlockSpec(memory_space=pltpu.VMEM)
SMALL = pl.CostEstimate(flops=1, bytes_accessed=1, transcendentals=0)


def call(kernel, name, **options):
    return pl.pallas_call(
        kernel,
        name=name,
        cost_estimate=SMALL,
        compiler_params=pltpu.CompilerParams(vmem_limit_bytes=VMEM_LIMIT),
        **options,
    )


def slot_targets(routes, rows):
    tok = routes.shape[0]
    lane = lax.broadcasted_iota(jnp.int32, (tok, 128), 1)
    first = routes[:, 0:1]
    second = routes[:, 1:2]
    hot0 = jnp.where(lane == first, 1.0, 0.0)
    hot1 = jnp.where(lane == second, 1.0, 0.0)
    earlier = jnp.where(
        lax.broadcasted_iota(jnp.int32, (tok, tok), 1) < lax.broadcasted_iota(jnp.int32, (tok, tok), 0),
        1.0,
        0.0,
    )
    counts = jnp.dot(earlier.astype(BF16), (hot0 + hot1).astype(BF16), preferred_element_type=F32)
    slot0 = jnp.sum(counts * hot0, axis=1, keepdims=True).astype(jnp.int32)
    slot1 = jnp.sum(counts * hot1, axis=1, keepdims=True).astype(jnp.int32)
    return first * rows + slot0, second * rows + slot1


def bucket_kernel(rows, routes_ref, x_ref, *out_refs):
    target0, target1 = slot_targets(routes_ref[...], rows)
    column = lax.broadcasted_iota(jnp.int32, (x_ref.shape[0], len(out_refs) * rows), 1)
    chosen = jnp.where((column == target0) | (column == target1), 1.0, 0.0).astype(BF16)
    found = lax.dot_general(
        chosen, x_ref[...], (((0,), (0,)), ((), ())), preferred_element_type=F32
    ).astype(BF16)
    for place, out_ref in enumerate(out_refs):
        out_ref[...] = found[place * rows : (place + 1) * rows]


def build_buckets(routes, moe_input, experts, rows):
    return call(
        functools.partial(bucket_kernel, rows),
        "bucket_rows",
        out_shape=[jax.ShapeDtypeStruct((rows, D), BF16)] * experts,
    )(routes, moe_input)


def stack(refs):
    return jnp.concatenate([ref[...] for ref in refs], axis=0)


def combine_kernel(rows, routes_ref, gates_ref, *refs):
    out_ref = refs[-1]
    back = stack(refs[:-1])
    tok = routes_ref.shape[0]
    target0, target1 = slot_targets(routes_ref[...], rows)
    targets = jnp.concatenate([target0, target1], axis=0)
    column = lax.broadcasted_iota(jnp.int32, (2 * tok, back.shape[0]), 1)
    chosen = jnp.where(column == targets, 1.0, 0.0).astype(BF16)
    picked = jnp.dot(chosen, back, preferred_element_type=F32)
    out_ref[...] = (picked[:tok] * gates_ref[:, 0:1] + picked[tok:] * gates_ref[:, 1:2]).astype(BF16)


def combine(routes, gates, back, rows):
    return call(
        functools.partial(combine_kernel, rows),
        "combine_routes",
        out_shape=jax.ShapeDtypeStruct((routes.shape[0], D), BF16),
    )(routes, gates, *back)


STEP = 896
STEPS = D // STEP


def hidden_kernel(*refs):
    gate_ref, up_ref, down_ref, hidden_ref, out_ref, gate_sum, up_sum = refs[-7:]
    step = pl.program_id(0)
    count = hidden_ref.shape[0]
    x = stack(refs[:-7])
    gate = jnp.dot(x, gate_ref[0], preferred_element_type=F32)
    up = jnp.dot(x, up_ref[0], preferred_element_type=F32)

    @pl.when(step == 0)
    def _():
        gate_sum[...] = gate
        up_sum[...] = up

    @pl.when(step > 0)
    def _():
        gate_sum[...] += gate
        up_sum[...] += up

    @pl.when(step == STEPS - 1)
    def _():
        value = gate_sum[...]
        hidden = (value / (1.0 + jnp.exp(-value)) * up_sum[...]).astype(BF16)
        hidden_ref[...] = hidden[:count]
        out_ref[...] = jnp.dot(hidden[count:], down_ref[0], preferred_element_type=F32).astype(BF16)


def hidden_rows(own, other, gate, up, down):
    rows = own[0].shape[0]
    count = len(own) * rows
    part = pl.BlockSpec((rows, STEP), lambda k: (0, k))
    weights = pl.BlockSpec((1, STEP, HALF), lambda k: (0, k, 0))
    return call(
        hidden_kernel,
        "expert_hidden",
        grid=(STEPS,),
        in_specs=[part] * (2 * len(own))
        + [weights, weights, pl.BlockSpec((1, HALF, D), lambda k: (0, 0, 0))],
        out_specs=[
            pl.BlockSpec((count, HALF), lambda k: (0, 0)),
            pl.BlockSpec((count, D), lambda k: (0, 0)),
        ],
        scratch_shapes=[pltpu.VMEM((2 * count, HALF), F32)] * 2,
        out_shape=[jax.ShapeDtypeStruct((count, HALF), BF16), jax.ShapeDtypeStruct((count, D), BF16)],
    )(*own, *other, gate, up, down)


def down_kernel(hidden_ref, down_ref, other_ref, *out_refs):
    own = jnp.dot(hidden_ref[...], down_ref[0], preferred_element_type=F32).astype(BF16)
    both = (own.astype(F32) + other_ref[...].astype(F32)).astype(BF16)
    rows = out_refs[0].shape[0]
    for place, out_ref in enumerate(out_refs):
        out_ref[...] = both[place * rows : (place + 1) * rows]


def down_own(hidden, down, other, experts):
    return call(
        down_kernel,
        "down_own_rows",
        out_shape=[jax.ShapeDtypeStruct((other.shape[0] // experts, D), BF16)] * experts,
    )(hidden, down, other)


def split_kernel(x_ref, out_ref):
    each = NOPE + ROPE
    heads = range(x_ref.shape[1] // each)
    pieces = [x_ref[:, head * each : head * each + NOPE] for head in heads]
    pieces += [x_ref[:, head * each + NOPE : (head + 1) * each] for head in heads]
    out_ref[0] = jnp.concatenate(pieces, axis=1)


def split_queries(queries, chips):
    tok = queries.shape[0]
    width = queries.shape[1] // chips
    return call(
        split_kernel,
        "split_queries",
        grid=(chips,),
        in_specs=[pl.BlockSpec((tok, width), lambda d: (0, d))],
        out_specs=pl.BlockSpec((1, tok, width), lambda d: (d, 0, 0)),
        out_shape=jax.ShapeDtypeStruct((chips, tok, width), BF16),
    )(queries)


BLOCK = 128
SPAN = 2 * BLOCK
EXP_SCALE = math.log2(math.e) / math.sqrt(NOPE + ROPE)


def attention_kernel(
    per_core,
    rank_ref,
    plain_ref,
    rope_ref,
    kv_ref,
    own_key_ref,
    other_key_ref,
    own_value_ref,
    other_value_ref,
    out_ref,
    keys,
    queries,
    mixed,
):
    pair = pl.program_id(0)
    shards, tok = kv_ref.shape[:2]
    count = plain_ref.shape[0]
    core = rank_ref[0] & 1
    mine = pair // per_core == core

    @pl.when(pair == 0)
    def _():
        for index, offset in enumerate(gather_order(shards)):
            place = pl.ds(pl.multiple_of((rank_ref[0] ^ offset) * tok, tok), tok)
            keys[place, : LATENT + ROPE] = kv_ref[index]
            keys[place, LATENT + ROPE :] = kv_ref[index, :, LATENT:]

    side = lax.broadcasted_iota(jnp.int32, (1, 2 * ROPE), 1) // ROPE
    for one in range(2):
        key = jnp.where(mine, own_key_ref[one], other_key_ref[one])
        latent = jnp.dot(plain_ref[:, one * NOPE : (one + 1) * NOPE], key, preferred_element_type=F32)
        queries[one, :, :LATENT] = latent.astype(BF16)
        queries[one, :, LATENT:] = jnp.where(side == one, rope_ref[...], jnp.zeros((), BF16))

    row = lax.broadcasted_iota(jnp.int32, (2 * BLOCK, SPAN), 0) % BLOCK
    position = (2 * (row // tok) + core) * tok + row % tok
    visible = lax.broadcasted_iota(jnp.int32, (2 * BLOCK, SPAN), 1) <= position
    contract = (((1,), (1,)), ((), ()))
    for block in range(count // BLOCK):
        start = block * SPAN
        rows = pl.ds(block * BLOCK, BLOCK)
        last = pl.ds(start, SPAN)
        query = jnp.concatenate([queries[0, rows, :], queries[1, rows, :]], axis=0)
        near = lax.dot_general(query, keys[last, :], contract, preferred_element_type=F32)
        near = jnp.where(visible, near, -1e30)
        top = jnp.max(near, axis=1, keepdims=True)
        if block:
            past = lax.dot_general(query, keys[:start, :], contract, preferred_element_type=F32)
            top = jnp.maximum(top, jnp.max(past, axis=1, keepdims=True))
        weights = jnp.exp2((near - top) * EXP_SCALE)
        total = jnp.sum(weights, axis=1, keepdims=True)
        summed = jnp.dot(weights.astype(BF16), keys[last, :LATENT], preferred_element_type=F32)
        if block:
            weights = jnp.exp2((past - top) * EXP_SCALE)
            total = total + jnp.sum(weights, axis=1, keepdims=True)
            summed = summed + jnp.dot(weights.astype(BF16), keys[:start, :LATENT], preferred_element_type=F32)
        result = (summed / total).astype(BF16)
        mixed[0, rows, :] = result[:BLOCK]
        mixed[1, rows, :] = result[BLOCK:]

    for one in range(2):
        value = jnp.where(mine, own_value_ref[one], other_value_ref[one])
        out_ref[:, one * VDIM : (one + 1) * VDIM] = jnp.dot(
            mixed[one], value, preferred_element_type=F32
        ).astype(BF16)


def attention(rank, queries, keys, key_proj, other_key, value_proj, other_value):
    count = queries.shape[0]
    pairs = key_proj.shape[0]
    per_core = pairs // 2
    key_spec = pl.BlockSpec((2, NOPE, LATENT), lambda p, rank: (p % per_core, 0, 0))
    value_spec = pl.BlockSpec((2, LATENT, VDIM), lambda p, rank: (p % per_core, 0, 0))
    return call(
        functools.partial(attention_kernel, per_core),
        "causal_attention",
        grid_spec=pltpu.PrefetchScalarGridSpec(
            num_scalar_prefetch=1,
            grid=(pairs,),
            in_specs=[
                pl.BlockSpec((count, 2 * NOPE), lambda p, rank: (0, p)),
                pl.BlockSpec((count, 2 * ROPE), lambda p, rank: (0, 2 * pairs + p)),
                pl.BlockSpec(keys.shape, lambda p, rank: (0, 0, 0)),
                key_spec,
                key_spec,
                value_spec,
                value_spec,
            ],
            out_specs=pl.BlockSpec((count, 2 * VDIM), lambda p, rank: (0, p)),
            scratch_shapes=[
                pltpu.VMEM((keys.shape[0] * keys.shape[1], LATENT + 2 * ROPE), BF16),
                pltpu.VMEM((2, count, LATENT + 2 * ROPE), BF16),
                pltpu.VMEM((2, count, LATENT), BF16),
            ],
        ),
        out_shape=jax.ShapeDtypeStruct((count, 2 * pairs * VDIM), BF16),
    )(rank, queries, queries, keys, key_proj, other_key, value_proj, other_value)


def send(array, mask):
    return lax.ppermute(array, "ctx", [(i, i ^ mask) for i in range(lax.axis_size("ctx"))])


def swap_chips(array):
    shards = lax.axis_size("ctx")
    return lax.all_to_all(
        array,
        "ctx",
        split_axis=0,
        concat_axis=0,
        axis_index_groups=[list(range(core, shards, 2)) for core in range(2)],
        tiled=True,
    )


def after(array, *others):
    return lax.optimization_barrier((array, *others))[0]


def gather_order(shards):
    top, below = shards // 2, shards // 4
    order = [0, top, below, top ^ below]
    mask = below // 2
    while mask:
        order = order + [offset ^ mask for offset in order]
        mask //= 2
    return order


def on_device(
    queries,
    latent_kv,
    key_proj,
    value_proj,
    moe_input,
    routes,
    gates,
    expert_gate,
    expert_up,
    expert_down,
):
    shards = lax.axis_size("ctx")
    tok = queries.shape[0]
    experts = shards // 2
    capacity = 2 * ((4 * tok * TOP + 6 * experts - 1) // (6 * experts))
    rows = -(-capacity // 8) * 8
    rank = lax.axis_index("ctx").astype(jnp.int32).reshape(1)

    named = routes ^ (rank // 2)
    chips = range(1, experts)

    keys = jnp.stack([latent_kv] + [send(latent_kv, offset) for offset in gather_order(shards)[1:4]])
    other_key = send(key_proj, 1)
    other_value = send(value_proj, 1)

    buckets = build_buckets(named, moe_input, experts, rows)
    own = [buckets[0]] + [send(buckets[m], 2 * m) for m in chips]
    sent = after(split_queries(queries, experts), keys, *own)
    held = swap_chips(sent)

    mask = shards // 8
    while mask:
        keys = jnp.concatenate([keys, send(keys, mask)], axis=0)
        mask //= 2
    other = [send(piece, 1) for piece in own]
    own[0] = after(own[0], keys, other_key, other_value)
    hidden, for_other = hidden_rows(own, other, expert_gate, expert_up, expert_down)
    result = down_own(hidden, expert_down, send(for_other, 1), experts)
    back = [result[0]] + [send(result[m], 2 * m) for m in chips]

    held = after(held, *result)
    values = attention(
        rank, held.reshape(experts * tok, held.shape[2]), keys, key_proj, other_key, value_proj, other_value
    )
    values, *back = lax.optimization_barrier((values, *back))
    values = swap_chips(values.reshape(experts, tok, values.shape[1]))
    moe_out = combine(named, gates, back, rows)
    attention_out = values.transpose(1, 0, 2).reshape(tok, HEADS * VDIM)
    return (attention_out, moe_out)


def solution(mesh):
    return jax.shard_map(
        on_device,
        mesh=mesh,
        in_specs=(
            P(("groups", "ctx"), None),
            P(("groups", "ctx"), None),
            P("ctx", None, None),
            P("ctx", None, None),
            P(("groups", "ctx"), None),
            P(("groups", "ctx"), None),
            P(("groups", "ctx"), None),
            P("ctx", None, None),
            P("ctx", None, None),
            P("ctx", None, None),
        ),
        out_specs=(P(("groups", "ctx"), None), P(("groups", "ctx"), None)),
        check_vma=False,
    )
```

```python
import functools
import math

import jax
import jax.numpy as jnp
from jax import lax
from jax.experimental import pallas as pl
from jax.experimental.pallas import tpu as pltpu
from jax.sharding import PartitionSpec as P

D = 3584
HEADS = 64
NOPE = 128
ROPE = 64
LATENT = 512
VDIM = 128
TOP = 2
HALF = 512
VMEM_LIMIT = 50 * 1024 * 1024
F32 = jnp.float32
BF16 = jnp.bfloat16


SMEM = pl.BlockSpec(memory_space=pltpu.SMEM)
VMEM = pl.BlockSpec(memory_space=pltpu.VMEM)
SMALL = pl.CostEstimate(flops=1, bytes_accessed=1, transcendentals=0)


def call(kernel, name, **options):
    return pl.pallas_call(
        kernel,
        name=name,
        cost_estimate=SMALL,
        compiler_params=pltpu.CompilerParams(vmem_limit_bytes=VMEM_LIMIT),
        **options,
    )


def slot_targets(routes, rows):
    tok = routes.shape[0]
    lane = lax.broadcasted_iota(jnp.int32, (tok, 128), 1)
    first = routes[:, 0:1]
    second = routes[:, 1:2]
    hot0 = jnp.where(lane == first, 1.0, 0.0)
    hot1 = jnp.where(lane == second, 1.0, 0.0)
    earlier = jnp.where(
        lax.broadcasted_iota(jnp.int32, (tok, tok), 1) < lax.broadcasted_iota(jnp.int32, (tok, tok), 0),
        1.0,
        0.0,
    )
    counts = jnp.dot(earlier.astype(BF16), (hot0 + hot1).astype(BF16), preferred_element_type=F32)
    slot0 = jnp.sum(counts * hot0, axis=1, keepdims=True).astype(jnp.int32)
    slot1 = jnp.sum(counts * hot1, axis=1, keepdims=True).astype(jnp.int32)
    return first * rows + slot0, second * rows + slot1


def bucket_kernel(rows, routes_ref, x_ref, *out_refs):
    target0, target1 = slot_targets(routes_ref[...], rows)
    column = lax.broadcasted_iota(jnp.int32, (x_ref.shape[0], len(out_refs) * rows), 1)
    chosen = jnp.where((column == target0) | (column == target1), 1.0, 0.0).astype(BF16)
    found = lax.dot_general(
        chosen, x_ref[...], (((0,), (0,)), ((), ())), preferred_element_type=F32
    ).astype(BF16)
    for place, out_ref in enumerate(out_refs):
        out_ref[...] = found[place * rows : (place + 1) * rows]


def build_buckets(routes, moe_input, experts, rows):
    return call(
        functools.partial(bucket_kernel, rows),
        "bucket_rows",
        out_shape=[jax.ShapeDtypeStruct((rows, D), BF16)] * experts,
    )(routes, moe_input)


def stack(refs):
    return jnp.concatenate([ref[...] for ref in refs], axis=0)


def combine_kernel(rows, routes_ref, gates_ref, back_ref, out_ref):
    back = back_ref[...]
    tok = routes_ref.shape[0]
    target0, target1 = slot_targets(routes_ref[...], rows)
    targets = jnp.concatenate([target0, target1], axis=0)
    column = lax.broadcasted_iota(jnp.int32, (2 * tok, back.shape[0]), 1)
    chosen = jnp.where(column == targets, 1.0, 0.0).astype(BF16)
    picked = jnp.dot(chosen, back, preferred_element_type=F32)
    out_ref[...] = (picked[:tok] * gates_ref[:, 0:1] + picked[tok:] * gates_ref[:, 1:2]).astype(BF16)


def combine(routes, gates, back, rows):
    return call(
        functools.partial(combine_kernel, rows),
        "combine_routes",
        out_shape=jax.ShapeDtypeStruct((routes.shape[0], D), BF16),
    )(routes, gates, back)


STEP = 896
STEPS = D // STEP


def hidden_kernel(*refs):
    gate_ref, up_ref, down_ref, hidden_ref, out_ref, gate_sum, up_sum = refs[-7:]
    step = pl.program_id(0)
    count = hidden_ref.shape[0]
    x = stack(refs[:-7])
    gate = jnp.dot(x, gate_ref[0], preferred_element_type=F32)
    up = jnp.dot(x, up_ref[0], preferred_element_type=F32)

    @pl.when(step == 0)
    def _():
        gate_sum[...] = gate
        up_sum[...] = up

    @pl.when(step > 0)
    def _():
        gate_sum[...] += gate
        up_sum[...] += up

    @pl.when(step == STEPS - 1)
    def _():
        value = gate_sum[...]
        hidden = (value / (1.0 + jnp.exp(-value)) * up_sum[...]).astype(BF16)
        hidden_ref[...] = hidden[:count]
        out_ref[...] = jnp.dot(hidden[count:], down_ref[0], preferred_element_type=F32).astype(BF16)


def hidden_rows(own, other, gate, up, down):
    rows = own[0].shape[0]
    count = len(own) * rows
    part = pl.BlockSpec((rows, STEP), lambda k: (0, k))
    weights = pl.BlockSpec((1, STEP, HALF), lambda k: (0, k, 0))
    return call(
        hidden_kernel,
        "expert_hidden",
        grid=(STEPS,),
        in_specs=[part] * (2 * len(own))
        + [weights, weights, pl.BlockSpec((1, HALF, D), lambda k: (0, 0, 0))],
        out_specs=[
            pl.BlockSpec((count, HALF), lambda k: (0, 0)),
            pl.BlockSpec((count, D), lambda k: (0, 0)),
        ],
        scratch_shapes=[pltpu.VMEM((2 * count, HALF), F32)] * 2,
        out_shape=[jax.ShapeDtypeStruct((count, HALF), BF16), jax.ShapeDtypeStruct((count, D), BF16)],
    )(*own, *other, gate, up, down)


def down_kernel(rank_ref, hidden_ref, down_ref, other_ref, out_ref):
    own = jnp.dot(hidden_ref[...], down_ref[0], preferred_element_type=F32).astype(BF16)
    both = (own.astype(F32) + other_ref[...].astype(F32)).astype(BF16)
    rows = out_ref.shape[1]
    for offset in range(out_ref.shape[0]):
        out_ref[(rank_ref[0] // 2) ^ offset] = both[offset * rows : (offset + 1) * rows]


def down_own(rank, hidden, down, other, experts):
    return call(
        down_kernel,
        "down_own_rows",
        in_specs=[SMEM, VMEM, VMEM, VMEM],
        out_specs=VMEM,
        out_shape=jax.ShapeDtypeStruct((experts, other.shape[0] // experts, D), BF16),
    )(rank, hidden, down, other)


class Split:
    def __init__(self, groups, shards, heads):
        self.groups, self.shards = groups, shards
        self.each = heads // shards
        self.wide = groups == 2 and self.each % (2 * groups) == 0
        self.chips = shards // 2
        self.own_pairs = self.each // 2 // (groups if self.wide else 1)
        self.holders = 2 if self.wide else 1
        self.pairs = 2 * self.holders * self.own_pairs
        self.parts = groups if self.wide else 1

    def first_head(self, rank, chip, pair):
        core, rest = divmod(pair, self.holders * self.own_pairs)
        holder, own = divmod(rest, self.own_pairs)
        if not self.wide:
            return (2 * chip + ((rank & 1) ^ core)) * self.each + 2 * own
        group, low = divmod(chip, self.shards // 4)
        top = (rank & (self.shards // 2)) ^ (holder * (self.shards // 2))
        return (top + 2 * low + ((rank & 1) ^ core)) * self.each + 2 * (group * self.own_pairs + own)

    def exchange(self, array):
        half = self.shards // 2
        if self.wide:
            tops, steps = (0, half), [g * self.shards + c for g in range(self.groups) for c in range(0, half, 2)]
            sets = [[start + core + step for step in steps] for start in tops for core in range(2)]
        else:
            starts = range(0, self.groups * self.shards, self.shards)
            sets = [[start + core + c for c in range(0, self.shards, 2)] for start in starts for core in range(2)]
        return lax.all_to_all(
            array, ("groups", "ctx"), split_axis=0, concat_axis=0, axis_index_groups=sets, tiled=True
        )


def split_kernel(split, rank_ref, x_ref, out_ref):
    each = NOPE + ROPE
    for chip in range(split.chips):
        for pair in range(split.pairs):
            start = pl.multiple_of(split.first_head(rank_ref[0], chip, pair) * each, 128)
            part = x_ref[:, pl.ds(start, 2 * each)]
            out_ref[chip, :, pair * 2 * each : (pair + 1) * 2 * each] = jnp.concatenate(
                [part[:, :NOPE], part[:, each : each + NOPE], part[:, NOPE:each], part[:, each + NOPE :]], axis=1
            )


def split_queries(split, rank, queries):
    tok = queries.shape[0]
    return call(
        functools.partial(split_kernel, split),
        "split_queries",
        in_specs=[SMEM, VMEM],
        out_specs=VMEM,
        out_shape=jax.ShapeDtypeStruct((split.chips, tok, 2 * split.pairs * (NOPE + ROPE)), BF16),
    )(rank, queries)


def join_kernel(split, rank_ref, x_ref, out_ref):
    for chip in range(split.chips):
        for pair in range(split.pairs):
            start = pl.multiple_of(split.first_head(rank_ref[0], chip, pair) * VDIM, 128)
            out_ref[:, pl.ds(start, 2 * VDIM)] = x_ref[chip, :, pair * 2 * VDIM : (pair + 1) * 2 * VDIM]


def join_values(split, rank, values):
    return call(
        functools.partial(join_kernel, split),
        "join_values",
        in_specs=[SMEM, VMEM],
        out_specs=VMEM,
        out_shape=jax.ShapeDtypeStruct((values.shape[1], HEADS * VDIM), BF16),
    )(rank, values)


BLOCK = 128
SPAN = 2 * BLOCK
EXP_SCALE = math.log2(math.e) / math.sqrt(NOPE + ROPE)


def attention_kernel(split, rank_ref, query_ref, kv_ref, weight_ref, out_ref, keys, queries, mixed):
    tok = kv_ref.shape[1]
    part_rows = query_ref.shape[0] // split.parts
    core = rank_ref[0] & 1

    @pl.when(pl.program_id(0) == 0)
    def _():
        for index, offset in enumerate(gather_order(split)):
            group, ctx = divmod(offset, split.shards)
            group = rank_ref[1] ^ group if split.wide else 0
            place = pl.ds(pl.multiple_of((rank_ref[0] ^ ctx) * tok, tok), tok)
            keys[group, place, : LATENT + ROPE] = kv_ref[index]
            keys[group, place, LATENT + ROPE :] = kv_ref[index, :, LATENT:]

    contract = (((1,), (1,)), ((), ()))
    side = lax.broadcasted_iota(jnp.int32, (1, 2 * ROPE), 1) // ROPE
    for one in range(2):
        latent = lax.dot_general(
            query_ref[:, one * NOPE : (one + 1) * NOPE], weight_ref[0, one], contract, preferred_element_type=F32
        )
        queries[one, :, :LATENT] = latent.astype(BF16)
        queries[one, :, LATENT:] = jnp.where(side == one, query_ref[:, 2 * NOPE :], jnp.zeros((), BF16))

    row = lax.broadcasted_iota(jnp.int32, (2 * BLOCK, SPAN), 0) % BLOCK
    position = (2 * (row // tok) + core) * tok + row % tok
    visible = lax.broadcasted_iota(jnp.int32, (2 * BLOCK, SPAN), 1) <= position

    def attend(part, block, before):
        start = before * SPAN
        first = part * part_rows + block * BLOCK
        rows = pl.ds(first, BLOCK)
        last = pl.ds(start, SPAN)
        query = jnp.concatenate([queries[0, rows, :], queries[1, rows, :]], axis=0)
        near = lax.dot_general(query, keys[part, last, :], contract, preferred_element_type=F32)
        near = jnp.where(visible, near, -1e30)
        top = jnp.max(near, axis=1, keepdims=True)
        if before:
            past = lax.dot_general(query, keys[part, :start, :], contract, preferred_element_type=F32)
            top = jnp.maximum(top, jnp.max(past, axis=1, keepdims=True))
        weights = jnp.exp2((near - top) * EXP_SCALE)
        total = jnp.sum(weights, axis=1, keepdims=True)
        summed = jnp.dot(weights.astype(BF16), keys[part, last, :LATENT], preferred_element_type=F32)
        if before:
            weights = jnp.exp2((past - top) * EXP_SCALE)
            total = total + jnp.sum(weights, axis=1, keepdims=True)
            summed = summed + jnp.dot(
                weights.astype(BF16), keys[part, :start, :LATENT], preferred_element_type=F32
            )
        result = (summed / total).astype(BF16)
        mixed[0, rows, :] = result[:BLOCK]
        mixed[1, rows, :] = result[BLOCK:]

    blocks = part_rows // BLOCK
    if split.wide:
        for half in range(2):

            @pl.when(rank_ref[0] // (split.shards // 2) == half)
            def _():
                for part in range(split.parts):
                    for block in range(blocks):
                        attend(part, block, half * blocks + block)

    else:
        for block in range(blocks):
            attend(0, block, block)

    for one in range(2):
        out_ref[:, one * VDIM : (one + 1) * VDIM] = jnp.dot(
            mixed[one], weight_ref[0, 2 + one], preferred_element_type=F32
        ).astype(BF16)


def attention(split, place, queries, keys, weights):
    count = queries.shape[0]
    length = keys.shape[0] * keys.shape[1] // split.parts
    return call(
        functools.partial(attention_kernel, split),
        "causal_attention",
        grid_spec=pltpu.PrefetchScalarGridSpec(
            num_scalar_prefetch=1,
            grid=(split.pairs,),
            in_specs=[
                pl.BlockSpec((count, 2 * (NOPE + ROPE)), lambda p, place: (0, p)),
                pl.BlockSpec(keys.shape, lambda p, place: (0, 0, 0)),
                pl.BlockSpec((1, 4, LATENT, VDIM), lambda p, place: (p, 0, 0, 0)),
            ],
            out_specs=pl.BlockSpec((count, 2 * VDIM), lambda p, place: (0, p)),
            scratch_shapes=[
                pltpu.VMEM((split.parts, length, LATENT + 2 * ROPE), BF16),
                pltpu.VMEM((2, count, LATENT + 2 * ROPE), BF16),
                pltpu.VMEM((2, count, LATENT), BF16),
            ],
        ),
        out_shape=jax.ShapeDtypeStruct((count, 2 * split.pairs * VDIM), BF16),
    )(place, queries, keys, weights)


def send(array, mask):
    count = lax.axis_size("groups") * lax.axis_size("ctx")
    return lax.ppermute(array, ("groups", "ctx"), [(i, i ^ mask) for i in range(count)])


def swap_chips(array):
    shards = lax.axis_size("ctx")
    return lax.all_to_all(
        array,
        "ctx",
        split_axis=0,
        concat_axis=0,
        axis_index_groups=[list(range(core, shards, 2)) for core in range(2)],
        tiled=True,
    )


def after(array, *others):
    return lax.optimization_barrier((array, *others))[0]


def gather_masks(split):
    top, below = split.shards // 2, split.shards // 4
    later = [1 << bit for bit in reversed(range(1, below.bit_length() - 1))]
    return [top, below, top ^ below], later + ([split.shards] if split.wide else []) + [1]


def gather_order(split):
    direct, later = gather_masks(split)
    order = [0] + direct
    for mask in later:
        order = order + [offset ^ mask for offset in order]
    return order


def on_device(
    queries,
    latent_kv,
    key_proj,
    value_proj,
    moe_input,
    routes,
    gates,
    expert_gate,
    expert_up,
    expert_down,
):
    shards = lax.axis_size("ctx")
    split = Split(lax.axis_size("groups"), shards, HEADS)
    tok = queries.shape[0]
    experts = shards // 2
    capacity = 2 * ((4 * tok * TOP + 6 * experts - 1) // (6 * experts))
    rows = -(-capacity // 8) * 8
    rank = lax.axis_index("ctx").astype(jnp.int32).reshape(1)
    group = lax.axis_index("groups").astype(jnp.int32).reshape(1)
    place = jnp.concatenate([rank, group])

    named = routes ^ (rank // 2)
    chips = range(1, experts)

    direct, later = gather_masks(split)
    keys = jnp.stack([latent_kv] + [send(latent_kv, offset) for offset in direct])
    for mask in later[:-1]:
        keys = jnp.concatenate([keys, send(keys, mask)], axis=0)

    buckets = build_buckets(named, moe_input, experts, rows)
    own = [buckets[0]] + [send(buckets[m], 2 * m) for m in chips]
    sent = after(split_queries(split, rank, queries), keys, *own)
    held = split.exchange(sent)

    weights = jnp.concatenate(
        [
            key_proj.swapaxes(1, 2).reshape(-1, 2, LATENT, NOPE),
            value_proj.reshape(-1, 2, LATENT, VDIM),
        ],
        axis=1,
    )
    if split.wide:
        weights = lax.dynamic_slice_in_dim(weights, group[0] * split.own_pairs, split.own_pairs, axis=0)
        weights = after(weights, *own)
        weights = jnp.concatenate([weights, send(weights, shards // 2)], axis=0)

    keys = jnp.concatenate([keys, send(keys, later[-1])], axis=0)
    other = [send(piece, 1) for piece in own]
    own[0] = after(own[0], keys)
    hidden, for_other = hidden_rows(own, other, expert_gate, expert_up, expert_down)
    result = down_own(rank, hidden, expert_down, send(for_other, 1), experts)
    weights = jnp.concatenate([weights, send(weights, 1)], axis=0)

    result, held, weights = lax.optimization_barrier((result, held, weights))
    back = swap_chips(result)
    values = attention(split, place, held.reshape(experts * tok, held.shape[2]), keys, weights)
    values, back = lax.optimization_barrier((values, back))
    values = split.exchange(values.reshape(experts, tok, values.shape[1]))
    moe_out = combine(routes, gates, back.reshape(experts * rows, D), rows)
    return (join_values(split, rank, values), moe_out)


def solution(mesh):
    return jax.shard_map(
        on_device,
        mesh=mesh,
        in_specs=(
            P(("groups", "ctx"), None),
            P(("groups", "ctx"), None),
            P("ctx", None, None),
            P("ctx", None, None),
            P(("groups", "ctx"), None),
            P(("groups", "ctx"), None),
            P(("groups", "ctx"), None),
            P("ctx", None, None),
            P("ctx", None, None),
            P("ctx", None, None),
        ),
        out_specs=(P(("groups", "ctx"), None), P(("groups", "ctx"), None)),
        check_vma=False,
    )
```

```python
import functools
import math

import jax
import jax.numpy as jnp
from jax import lax
from jax.experimental import pallas as pl
from jax.experimental.pallas import tpu as pltpu
from jax.sharding import PartitionSpec as P

D = 3584
HEADS = 64
NOPE = 128
ROPE = 64
LATENT = 512
VDIM = 128
TOP = 2
HALF = 512
VMEM_LIMIT = 50 * 1024 * 1024
F32 = jnp.float32
BF16 = jnp.bfloat16


SMEM = pl.BlockSpec(memory_space=pltpu.SMEM)
VMEM = pl.BlockSpec(memory_space=pltpu.VMEM)
SMALL = pl.CostEstimate(flops=1, bytes_accessed=1, transcendentals=0)


def call(kernel, name, **options):
    return pl.pallas_call(
        kernel,
        name=name,
        cost_estimate=SMALL,
        compiler_params=pltpu.CompilerParams(vmem_limit_bytes=VMEM_LIMIT),
        **options,
    )


def slot_targets(routes, rows):
    tok = routes.shape[0]
    lane = lax.broadcasted_iota(jnp.int32, (tok, 128), 1)
    first = routes[:, 0:1]
    second = routes[:, 1:2]
    hot0 = jnp.where(lane == first, 1.0, 0.0)
    hot1 = jnp.where(lane == second, 1.0, 0.0)
    earlier = jnp.where(
        lax.broadcasted_iota(jnp.int32, (tok, tok), 1) < lax.broadcasted_iota(jnp.int32, (tok, tok), 0),
        1.0,
        0.0,
    )
    counts = jnp.dot(earlier.astype(BF16), (hot0 + hot1).astype(BF16), preferred_element_type=F32)
    slot0 = jnp.sum(counts * hot0, axis=1, keepdims=True).astype(jnp.int32)
    slot1 = jnp.sum(counts * hot1, axis=1, keepdims=True).astype(jnp.int32)
    return first * rows + slot0, second * rows + slot1


def bucket_kernel(rows, routes_ref, x_ref, *out_refs):
    target0, target1 = slot_targets(routes_ref[...], rows)
    column = lax.broadcasted_iota(jnp.int32, (x_ref.shape[0], len(out_refs) * rows), 1)
    chosen = jnp.where((column == target0) | (column == target1), 1.0, 0.0).astype(BF16)
    found = lax.dot_general(
        chosen, x_ref[...], (((0,), (0,)), ((), ())), preferred_element_type=F32
    ).astype(BF16)
    for place, out_ref in enumerate(out_refs):
        out_ref[...] = found[place * rows : (place + 1) * rows]


def build_buckets(routes, moe_input, experts, rows):
    return call(
        functools.partial(bucket_kernel, rows),
        "bucket_rows",
        out_shape=[jax.ShapeDtypeStruct((rows, D), BF16)] * experts,
    )(routes, moe_input)


def stack(refs):
    return jnp.concatenate([ref[...] for ref in refs], axis=0)


def combine_kernel(rows, routes_ref, gates_ref, back_ref, out_ref):
    back = back_ref[...]
    tok = routes_ref.shape[0]
    target0, target1 = slot_targets(routes_ref[...], rows)
    targets = jnp.concatenate([target0, target1], axis=0)
    column = lax.broadcasted_iota(jnp.int32, (2 * tok, back.shape[0]), 1)
    chosen = jnp.where(column == targets, 1.0, 0.0).astype(BF16)
    picked = jnp.dot(chosen, back, preferred_element_type=F32)
    out_ref[...] = (picked[:tok] * gates_ref[:, 0:1] + picked[tok:] * gates_ref[:, 1:2]).astype(BF16)


def combine(routes, gates, back, rows):
    return call(
        functools.partial(combine_kernel, rows),
        "combine_routes",
        out_shape=jax.ShapeDtypeStruct((routes.shape[0], D), BF16),
    )(routes, gates, back)


STEP = 896
STEPS = D // STEP


def hidden_kernel(*refs):
    gate_ref, up_ref, down_ref, hidden_ref, out_ref, gate_sum, up_sum = refs[-7:]
    step = pl.program_id(0)
    count = hidden_ref.shape[0]
    x = stack(refs[:-7])
    gate = jnp.dot(x, gate_ref[0], preferred_element_type=F32)
    up = jnp.dot(x, up_ref[0], preferred_element_type=F32)

    @pl.when(step == 0)
    def _():
        gate_sum[...] = gate
        up_sum[...] = up

    @pl.when(step > 0)
    def _():
        gate_sum[...] += gate
        up_sum[...] += up

    @pl.when(step == STEPS - 1)
    def _():
        value = gate_sum[...]
        hidden = (value / (1.0 + jnp.exp(-value)) * up_sum[...]).astype(BF16)
        hidden_ref[...] = hidden[:count]
        out_ref[...] = jnp.dot(hidden[count:], down_ref[0], preferred_element_type=F32).astype(BF16)


def hidden_rows(own, other, gate, up, down):
    rows = own[0].shape[0]
    count = len(own) * rows
    part = pl.BlockSpec((rows, STEP), lambda k: (0, k))
    weights = pl.BlockSpec((1, STEP, HALF), lambda k: (0, k, 0))
    return call(
        hidden_kernel,
        "expert_hidden",
        grid=(STEPS,),
        in_specs=[part] * (2 * len(own))
        + [weights, weights, pl.BlockSpec((1, HALF, D), lambda k: (0, 0, 0))],
        out_specs=[
            pl.BlockSpec((count, HALF), lambda k: (0, 0)),
            pl.BlockSpec((count, D), lambda k: (0, 0)),
        ],
        scratch_shapes=[pltpu.VMEM((2 * count, HALF), F32)] * 2,
        out_shape=[jax.ShapeDtypeStruct((count, HALF), BF16), jax.ShapeDtypeStruct((count, D), BF16)],
    )(*own, *other, gate, up, down)


def down_kernel(rank_ref, hidden_ref, down_ref, other_ref, out_ref):
    own = jnp.dot(hidden_ref[...], down_ref[0], preferred_element_type=F32).astype(BF16)
    both = (own.astype(F32) + other_ref[...].astype(F32)).astype(BF16)
    rows = out_ref.shape[1]
    for offset in range(out_ref.shape[0]):
        out_ref[(rank_ref[0] // 2) ^ offset] = both[offset * rows : (offset + 1) * rows]


def down_own(rank, hidden, down, other, experts):
    return call(
        down_kernel,
        "down_own_rows",
        in_specs=[SMEM, VMEM, VMEM, VMEM],
        out_specs=VMEM,
        out_shape=jax.ShapeDtypeStruct((experts, other.shape[0] // experts, D), BF16),
    )(rank, hidden, down, other)


class Split:
    def __init__(self, groups, shards, heads):
        self.groups, self.shards = groups, shards
        self.each = heads // shards
        self.wide = groups == 2 and self.each % (2 * groups) == 0
        self.chips = shards // 2
        self.own_pairs = self.each // 2 // (groups if self.wide else 1)
        self.holders = 2 if self.wide else 1
        self.pairs = 2 * self.holders * self.own_pairs
        self.parts = groups if self.wide else 1

    def first_head(self, rank, chip, pair):
        core, rest = divmod(pair, self.holders * self.own_pairs)
        holder, own = divmod(rest, self.own_pairs)
        if not self.wide:
            return (2 * chip + ((rank & 1) ^ core)) * self.each + 2 * own
        group, low = divmod(chip, self.shards // 4)
        top = (rank & (self.shards // 2)) ^ (holder * (self.shards // 2))
        return (top + 2 * low + ((rank & 1) ^ core)) * self.each + 2 * (group * self.own_pairs + own)

    def exchange(self, array):
        half = self.shards // 2
        if self.wide:
            tops, steps = (0, half), [g * self.shards + c for g in range(self.groups) for c in range(0, half, 2)]
            sets = [[start + core + step for step in steps] for start in tops for core in range(2)]
        else:
            starts = range(0, self.groups * self.shards, self.shards)
            sets = [[start + core + c for c in range(0, self.shards, 2)] for start in starts for core in range(2)]
        return lax.all_to_all(
            array, ("groups", "ctx"), split_axis=0, concat_axis=0, axis_index_groups=sets, tiled=True
        )


def split_kernel(split, rank_ref, x_ref, out_ref):
    each = NOPE + ROPE
    for chip in range(split.chips):
        for pair in range(split.pairs):
            start = pl.multiple_of(split.first_head(rank_ref[0], chip, pair) * each, 128)
            part = x_ref[:, pl.ds(start, 2 * each)]
            out_ref[chip, :, pair * 2 * each : (pair + 1) * 2 * each] = jnp.concatenate(
                [part[:, :NOPE], part[:, each : each + NOPE], part[:, NOPE:each], part[:, each + NOPE :]], axis=1
            )


def split_queries(split, rank, queries):
    tok = queries.shape[0]
    return call(
        functools.partial(split_kernel, split),
        "split_queries",
        in_specs=[SMEM, VMEM],
        out_specs=VMEM,
        out_shape=jax.ShapeDtypeStruct((split.chips, tok, 2 * split.pairs * (NOPE + ROPE)), BF16),
    )(rank, queries)


def join_kernel(split, rank_ref, x_ref, out_ref):
    for chip in range(split.chips):
        for pair in range(split.pairs):
            start = pl.multiple_of(split.first_head(rank_ref[0], chip, pair) * VDIM, 128)
            out_ref[:, pl.ds(start, 2 * VDIM)] = x_ref[chip, :, pair * 2 * VDIM : (pair + 1) * 2 * VDIM]


def join_values(split, rank, values):
    return call(
        functools.partial(join_kernel, split),
        "join_values",
        in_specs=[SMEM, VMEM],
        out_specs=VMEM,
        out_shape=jax.ShapeDtypeStruct((values.shape[1], HEADS * VDIM), BF16),
    )(rank, values)


BLOCK = 128
SPAN = 2 * BLOCK
EXP_SCALE = math.log2(math.e) / math.sqrt(NOPE + ROPE)


def attention_kernel(
    split, rank_ref, query_ref, kv_ref, other_kv_ref, weight_ref, other_weight_ref, out_ref, keys, queries, mixed
):
    tok = kv_ref.shape[1]
    part_rows = query_ref.shape[0] // split.parts
    core = rank_ref[0] & 1

    @pl.when(pl.program_id(0) == 0)
    def _():
        for index, offset in enumerate(gather_order(split)):
            for from_ref, swapped in ((kv_ref, 0), (other_kv_ref, 1)):
                group, ctx = divmod(offset ^ swapped, split.shards)
                group = rank_ref[1] ^ group if split.wide else 0
                place = pl.ds(pl.multiple_of((rank_ref[0] ^ ctx) * tok, tok), tok)
                keys[group, place, : LATENT + ROPE] = from_ref[index]
                keys[group, place, LATENT + ROPE :] = from_ref[index, :, LATENT:]

    own_core = pl.program_id(0) < split.pairs // 2

    def weight(index):
        return jnp.where(own_core, weight_ref[0, index], other_weight_ref[0, index])

    contract = (((1,), (1,)), ((), ()))
    side = lax.broadcasted_iota(jnp.int32, (1, 2 * ROPE), 1) // ROPE
    for one in range(2):
        latent = lax.dot_general(
            query_ref[:, one * NOPE : (one + 1) * NOPE], weight(one), contract, preferred_element_type=F32
        )
        queries[one, :, :LATENT] = latent.astype(BF16)
        queries[one, :, LATENT:] = jnp.where(side == one, query_ref[:, 2 * NOPE :], jnp.zeros((), BF16))

    row = lax.broadcasted_iota(jnp.int32, (2 * BLOCK, SPAN), 0) % BLOCK
    position = (2 * (row // tok) + core) * tok + row % tok
    visible = lax.broadcasted_iota(jnp.int32, (2 * BLOCK, SPAN), 1) <= position

    def attend(part, block, before):
        start = before * SPAN
        first = part * part_rows + block * BLOCK
        rows = pl.ds(first, BLOCK)
        last = pl.ds(start, SPAN)
        query = jnp.concatenate([queries[0, rows, :], queries[1, rows, :]], axis=0)
        near = lax.dot_general(query, keys[part, last, :], contract, preferred_element_type=F32)
        near = jnp.where(visible, near, -1e30)
        top = jnp.max(near, axis=1, keepdims=True)
        if before:
            past = lax.dot_general(query, keys[part, :start, :], contract, preferred_element_type=F32)
            top = jnp.maximum(top, jnp.max(past, axis=1, keepdims=True))
        weights = jnp.exp2((near - top) * EXP_SCALE)
        total = jnp.sum(weights, axis=1, keepdims=True)
        summed = jnp.dot(weights.astype(BF16), keys[part, last, :LATENT], preferred_element_type=F32)
        if before:
            weights = jnp.exp2((past - top) * EXP_SCALE)
            total = total + jnp.sum(weights, axis=1, keepdims=True)
            summed = summed + jnp.dot(
                weights.astype(BF16), keys[part, :start, :LATENT], preferred_element_type=F32
            )
        result = (summed / total).astype(BF16)
        mixed[0, rows, :] = result[:BLOCK]
        mixed[1, rows, :] = result[BLOCK:]

    blocks = part_rows // BLOCK
    if split.wide:
        for half in range(2):

            @pl.when(rank_ref[0] // (split.shards // 2) == half)
            def _():
                for part in range(split.parts):
                    for block in range(blocks):
                        attend(part, block, half * blocks + block)

    else:
        for block in range(blocks):
            attend(0, block, block)

    for one in range(2):
        out_ref[:, one * VDIM : (one + 1) * VDIM] = jnp.dot(
            mixed[one], weight(2 + one), preferred_element_type=F32
        ).astype(BF16)


def attention(split, place, queries, keys, other_keys, weights, other_weights):
    count = queries.shape[0]
    length = 2 * keys.shape[0] * keys.shape[1] // split.parts
    whole = pl.BlockSpec(keys.shape, lambda p, place: (0, 0, 0))
    each = split.pairs // 2
    return call(
        functools.partial(attention_kernel, split),
        "causal_attention",
        grid_spec=pltpu.PrefetchScalarGridSpec(
            num_scalar_prefetch=1,
            grid=(split.pairs,),
            in_specs=[
                pl.BlockSpec((count, 2 * (NOPE + ROPE)), lambda p, place: (0, p)),
                whole,
                whole,
                pl.BlockSpec((1, 4, LATENT, VDIM), lambda p, place: (jnp.minimum(p, each - 1), 0, 0, 0)),
                pl.BlockSpec((1, 4, LATENT, VDIM), lambda p, place: (jnp.maximum(p - each, 0), 0, 0, 0)),
            ],
            out_specs=pl.BlockSpec((count, 2 * VDIM), lambda p, place: (0, p)),
            scratch_shapes=[
                pltpu.VMEM((split.parts, length, LATENT + 2 * ROPE), BF16),
                pltpu.VMEM((2, count, LATENT + 2 * ROPE), BF16),
                pltpu.VMEM((2, count, LATENT), BF16),
            ],
        ),
        out_shape=jax.ShapeDtypeStruct((count, 2 * split.pairs * VDIM), BF16),
    )(place, queries, keys, other_keys, weights, other_weights)


def send(array, mask):
    count = lax.axis_size("groups") * lax.axis_size("ctx")
    return lax.ppermute(array, ("groups", "ctx"), [(i, i ^ mask) for i in range(count)])


def swap_chips(array):
    shards = lax.axis_size("ctx")
    return lax.all_to_all(
        array,
        "ctx",
        split_axis=0,
        concat_axis=0,
        axis_index_groups=[list(range(core, shards, 2)) for core in range(2)],
        tiled=True,
    )


def after(array, *others):
    return lax.optimization_barrier((array, *others))[0]


def gather_masks(split):
    top, below = split.shards // 2, split.shards // 4
    later = [1 << bit for bit in reversed(range(1, below.bit_length() - 1))]
    return [top, below, top ^ below], later + ([split.shards] if split.wide else [])


def gather_order(split):
    direct, later = gather_masks(split)
    order = [0] + direct
    for mask in later:
        order = order + [offset ^ mask for offset in order]
    return order


def on_device(
    queries,
    latent_kv,
    key_proj,
    value_proj,
    moe_input,
    routes,
    gates,
    expert_gate,
    expert_up,
    expert_down,
):
    shards = lax.axis_size("ctx")
    split = Split(lax.axis_size("groups"), shards, HEADS)
    tok = queries.shape[0]
    experts = shards // 2
    capacity = 2 * ((4 * tok * TOP + 6 * experts - 1) // (6 * experts))
    rows = -(-capacity // 8) * 8
    rank = lax.axis_index("ctx").astype(jnp.int32).reshape(1)
    group = lax.axis_index("groups").astype(jnp.int32).reshape(1)
    place = jnp.concatenate([rank, group])

    named = routes ^ (rank // 2)
    chips = range(1, experts)

    direct, later = gather_masks(split)
    keys = jnp.stack([latent_kv] + [send(latent_kv, offset) for offset in direct])

    buckets = build_buckets(named, moe_input, experts, rows)
    own = [buckets[0]] + [send(buckets[m], 2 * m) for m in chips]
    keys = after(keys, own[1])
    for mask in later:
        keys = jnp.concatenate([keys, send(keys, mask)], axis=0)
    sent = after(split_queries(split, rank, queries), keys, *own[1 : experts // 2])
    held = split.exchange(sent)

    weights = jnp.concatenate(
        [
            key_proj.swapaxes(1, 2).reshape(-1, 2, LATENT, NOPE),
            value_proj.reshape(-1, 2, LATENT, VDIM),
        ],
        axis=1,
    )
    if split.wide:
        weights = lax.dynamic_slice_in_dim(weights, group[0] * split.own_pairs, split.own_pairs, axis=0)
        weights = after(weights, *own[1 : experts // 2])
        weights = jnp.concatenate([weights, send(weights, shards // 2)], axis=0)

    other = [send(piece, 1) for piece in own]
    hidden, for_other = hidden_rows(own, other, expert_gate, expert_up, expert_down)
    result = down_own(rank, hidden, expert_down, send(for_other, 1), experts)

    result, held, weights = lax.optimization_barrier((result, held, weights))
    back = swap_chips(result)
    held = held.reshape(experts * tok, held.shape[2])
    values = attention(split, place, held, keys, send(keys, 1), weights, send(weights, 1))
    values, back = lax.optimization_barrier((values, back))
    values = split.exchange(values.reshape(experts, tok, values.shape[1]))
    moe_out = combine(routes, gates, back.reshape(experts * rows, D), rows)
    return (join_values(split, rank, values), moe_out)


def solution(mesh):
    return jax.shard_map(
        on_device,
        mesh=mesh,
        in_specs=(
            P(("groups", "ctx"), None),
            P(("groups", "ctx"), None),
            P("ctx", None, None),
            P("ctx", None, None),
            P(("groups", "ctx"), None),
            P(("groups", "ctx"), None),
            P(("groups", "ctx"), None),
            P("ctx", None, None),
            P("ctx", None, None),
            P("ctx", None, None),
        ),
        out_specs=(P(("groups", "ctx"), None), P(("groups", "ctx"), None)),
        check_vma=False,
    )
```

```python
import functools
import math

import jax
import jax.numpy as jnp
from jax import lax
from jax.experimental import pallas as pl
from jax.experimental.pallas import tpu as pltpu
from jax.sharding import PartitionSpec as P

D = 3584
HEADS = 64
NOPE = 128
ROPE = 64
LATENT = 512
VDIM = 128
TOP = 2
HALF = 512
VMEM_LIMIT = 50 * 1024 * 1024
F32 = jnp.float32
BF16 = jnp.bfloat16


SMEM = pl.BlockSpec(memory_space=pltpu.SMEM)
VMEM = pl.BlockSpec(memory_space=pltpu.VMEM)


def call(kernel, name, flops=0, moved=0, **options):
    return pl.pallas_call(
        kernel,
        name=name,
        cost_estimate=pl.CostEstimate(flops=flops, bytes_accessed=moved, transcendentals=0),
        compiler_params=pltpu.CompilerParams(vmem_limit_bytes=VMEM_LIMIT),
        **options,
    )


def slot_targets(routes, rows):
    tok = routes.shape[0]
    lane = lax.broadcasted_iota(jnp.int32, (tok, 128), 1)
    first = routes[:, 0:1]
    second = routes[:, 1:2]
    hot0 = jnp.where(lane == first, 1.0, 0.0)
    hot1 = jnp.where(lane == second, 1.0, 0.0)
    earlier = jnp.where(
        lax.broadcasted_iota(jnp.int32, (tok, tok), 1) < lax.broadcasted_iota(jnp.int32, (tok, tok), 0),
        1.0,
        0.0,
    )
    counts = jnp.dot(earlier.astype(BF16), (hot0 + hot1).astype(BF16), preferred_element_type=F32)
    slot0 = jnp.sum(counts * hot0, axis=1, keepdims=True).astype(jnp.int32)
    slot1 = jnp.sum(counts * hot1, axis=1, keepdims=True).astype(jnp.int32)
    return first * rows + slot0, second * rows + slot1


def bucket_kernel(rows, routes_ref, x_ref, out_ref):
    target0, target1 = slot_targets(routes_ref[...], rows)
    column = lax.broadcasted_iota(jnp.int32, (x_ref.shape[0], out_ref.shape[0]), 1)
    chosen = jnp.where((column == target0) | (column == target1), 1.0, 0.0).astype(BF16)
    out_ref[...] = lax.dot_general(
        chosen, x_ref[...], (((0,), (0,)), ((), ())), preferred_element_type=F32
    ).astype(BF16)


def build_buckets(routes, moe_input, experts, rows):
    return call(
        functools.partial(bucket_kernel, rows),
        "bucket_rows",
        moved=2 * D * (moe_input.shape[0] + experts * rows),
        out_shape=jax.ShapeDtypeStruct((experts * rows, D), BF16),
    )(routes, moe_input)


def combine_kernel(rows, routes_ref, gates_ref, back_ref, out_ref):
    back = back_ref[...]
    tok = routes_ref.shape[0]
    target0, target1 = slot_targets(routes_ref[...], rows)
    targets = jnp.concatenate([target0, target1], axis=0)
    column = lax.broadcasted_iota(jnp.int32, (2 * tok, back.shape[0]), 1)
    chosen = jnp.where(column == targets, 1.0, 0.0).astype(BF16)
    picked = jnp.dot(chosen, back, preferred_element_type=F32)
    out_ref[...] = (picked[:tok] * gates_ref[:, 0:1] + picked[tok:] * gates_ref[:, 1:2]).astype(BF16)


def combine(routes, gates, back, rows):
    return call(
        functools.partial(combine_kernel, rows),
        "combine_routes",
        moved=2 * D * (routes.shape[0] + back.shape[0]),
        out_shape=jax.ShapeDtypeStruct((routes.shape[0], D), BF16),
    )(routes, gates, back)


STEP = 896
STEPS = D // STEP


def expert_kernel(x_ref, gate0, up0, gate1, up1, down0, down1, out_ref, sums, hidden):
    step = pl.program_id(0)

    @pl.when(step < STEPS)
    def _():
        x = x_ref[...]
        for index, weight_ref in enumerate((gate0, up0, gate1, up1)):
            part = jnp.dot(x, weight_ref[0], preferred_element_type=F32)
            sums[index] = jnp.where(step == 0, part, sums[index] + part)

    @pl.when(step == STEPS)
    def _():
        for half in range(2):
            value = sums[2 * half]
            hidden[half] = (value / (1.0 + jnp.exp(-value)) * sums[2 * half + 1]).astype(BF16)

    @pl.when(step >= STEPS)
    def _():
        first = jnp.dot(hidden[0], down0[0], preferred_element_type=F32).astype(BF16)
        second = jnp.dot(hidden[1], down1[0], preferred_element_type=F32).astype(BF16)
        out_ref[...] = (first.astype(F32) + second.astype(F32)).astype(BF16)


def expert_rows(x, own, other):
    count = x.shape[0]
    weights = pl.BlockSpec((1, STEP, HALF), lambda k: (0, jnp.minimum(k, STEPS - 1), 0))
    down = pl.BlockSpec((1, HALF, STEP), lambda k: (0, 0, jnp.maximum(k - STEPS, 0)))
    return call(
        expert_kernel,
        "expert_rows",
        flops=12 * count * D * HALF,
        moved=12 * D * HALF + 4 * count * D,
        grid=(2 * STEPS,),
        in_specs=[pl.BlockSpec((count, STEP), lambda k: (0, jnp.minimum(k, STEPS - 1)))] + [weights] * 4 + [down] * 2,
        out_specs=pl.BlockSpec((count, STEP), lambda k: (0, jnp.maximum(k - STEPS, 0))),
        scratch_shapes=[pltpu.VMEM((4, count, HALF), F32), pltpu.VMEM((2, count, HALF), BF16)],
        out_shape=jax.ShapeDtypeStruct((count, D), BF16),
    )(x, own[0], own[1], other[0], other[1], own[2], other[2])


class Split:
    def __init__(self, groups, shards, heads):
        self.groups, self.shards = groups, shards
        self.each = heads // shards
        self.wide = groups == 2 and self.each % (2 * groups) == 0
        self.chips = shards // 2
        self.own_pairs = self.each // 2 // (groups if self.wide else 1)
        self.holders = 2 if self.wide else 1
        self.pairs = 2 * self.holders * self.own_pairs
        self.parts = groups if self.wide else 1

    def first_head(self, rank, chip, pair):
        core, rest = divmod(pair, self.holders * self.own_pairs)
        holder, own = divmod(rest, self.own_pairs)
        if not self.wide:
            return (2 * chip + ((rank & 1) ^ core)) * self.each + 2 * own
        group, low = divmod(chip, self.shards // 4)
        top = (rank & (self.shards // 2)) ^ (holder * (self.shards // 2))
        return (top + 2 * low + ((rank & 1) ^ core)) * self.each + 2 * (group * self.own_pairs + own)

    def exchange(self, array):
        half = self.shards // 2
        if self.wide:
            tops, steps = (0, half), [g * self.shards + c for g in range(self.groups) for c in range(0, half, 2)]
            sets = [[start + core + step for step in steps] for start in tops for core in range(2)]
        else:
            starts = range(0, self.groups * self.shards, self.shards)
            sets = [[start + core + c for c in range(0, self.shards, 2)] for start in starts for core in range(2)]
        return lax.all_to_all(
            array, ("groups", "ctx"), split_axis=0, concat_axis=0, axis_index_groups=sets, tiled=True
        )


def split_kernel(split, rank_ref, x_ref, out_ref):
    each = NOPE + ROPE
    for chip in range(split.chips):
        for pair in range(split.pairs):
            start = pl.multiple_of(split.first_head(rank_ref[0], chip, pair) * each, 128)
            part = x_ref[:, pl.ds(start, 2 * each)]
            out_ref[chip, :, pair * 2 * each : (pair + 1) * 2 * each] = jnp.concatenate(
                [part[:, :NOPE], part[:, each : each + NOPE], part[:, NOPE:each], part[:, each + NOPE :]], axis=1
            )


def split_queries(split, rank, queries):
    tok = queries.shape[0]
    return call(
        functools.partial(split_kernel, split),
        "split_queries",
        moved=4 * queries.size,
        in_specs=[SMEM, VMEM],
        out_specs=VMEM,
        out_shape=jax.ShapeDtypeStruct((split.chips, tok, 2 * split.pairs * (NOPE + ROPE)), BF16),
    )(rank, queries)


def join_kernel(split, rank_ref, x_ref, out_ref):
    for chip in range(split.chips):
        for pair in range(split.pairs):
            start = pl.multiple_of(split.first_head(rank_ref[0], chip, pair) * VDIM, 128)
            out_ref[:, pl.ds(start, 2 * VDIM)] = x_ref[chip, :, pair * 2 * VDIM : (pair + 1) * 2 * VDIM]


def join_values(split, rank, values):
    return call(
        functools.partial(join_kernel, split),
        "join_values",
        moved=4 * values.size,
        in_specs=[SMEM, VMEM],
        out_specs=VMEM,
        out_shape=jax.ShapeDtypeStruct((values.shape[1], HEADS * VDIM), BF16),
    )(rank, values)


BLOCK = 128
SPAN = 2 * BLOCK
EXP_SCALE = math.log2(math.e) / math.sqrt(NOPE + ROPE)


def attention_kernel(
    split, rank_ref, query_ref, kv_ref, other_kv_ref, weight_ref, other_weight_ref, out_ref, keys, queries, mixed
):
    tok = kv_ref.shape[1]
    part_rows = query_ref.shape[0] // split.parts
    core = rank_ref[0] & 1

    @pl.when(pl.program_id(0) == 0)
    def _():
        for index, offset in enumerate(gather_order(split)):
            for from_ref, swapped in ((kv_ref, 0), (other_kv_ref, 1)):
                group, ctx = divmod(offset ^ swapped, split.shards)
                group = rank_ref[1] ^ group if split.wide else 0
                place = pl.ds(pl.multiple_of((rank_ref[0] ^ ctx) * tok, tok), tok)
                keys[group, place, : LATENT + ROPE] = from_ref[index]
                keys[group, place, LATENT + ROPE :] = from_ref[index, :, LATENT:]

    own_core = pl.program_id(0) < split.pairs // 2

    def weight(index):
        return jnp.where(own_core, weight_ref[0, index], other_weight_ref[0, index])

    contract = (((1,), (1,)), ((), ()))
    side = lax.broadcasted_iota(jnp.int32, (1, 2 * ROPE), 1) // ROPE
    for one in range(2):
        latent = lax.dot_general(
            query_ref[:, one * NOPE : (one + 1) * NOPE], weight(one), contract, preferred_element_type=F32
        )
        queries[one, :, :LATENT] = latent.astype(BF16)
        queries[one, :, LATENT:] = jnp.where(side == one, query_ref[:, 2 * NOPE :], jnp.zeros((), BF16))

    row = lax.broadcasted_iota(jnp.int32, (2 * BLOCK, SPAN), 0) % BLOCK
    position = (2 * (row // tok) + core) * tok + row % tok
    visible = lax.broadcasted_iota(jnp.int32, (2 * BLOCK, SPAN), 1) <= position

    def attend(part, block, before):
        start = before * SPAN
        first = part * part_rows + block * BLOCK
        rows = pl.ds(first, BLOCK)
        last = pl.ds(start, SPAN)
        query = jnp.concatenate([queries[0, rows, :], queries[1, rows, :]], axis=0)
        near = lax.dot_general(query, keys[part, last, :], contract, preferred_element_type=F32)
        near = jnp.where(visible, near, -1e30)
        top = jnp.max(near, axis=1, keepdims=True)
        if before:
            past = lax.dot_general(query, keys[part, :start, :], contract, preferred_element_type=F32)
            top = jnp.maximum(top, jnp.max(past, axis=1, keepdims=True))
        weights = jnp.exp2((near - top) * EXP_SCALE)
        total = jnp.sum(weights, axis=1, keepdims=True)
        summed = jnp.dot(weights.astype(BF16), keys[part, last, :LATENT], preferred_element_type=F32)
        if before:
            weights = jnp.exp2((past - top) * EXP_SCALE)
            total = total + jnp.sum(weights, axis=1, keepdims=True)
            summed = summed + jnp.dot(
                weights.astype(BF16), keys[part, :start, :LATENT], preferred_element_type=F32
            )
        result = (summed / total).astype(BF16)
        mixed[0, rows, :] = result[:BLOCK]
        mixed[1, rows, :] = result[BLOCK:]

    blocks = part_rows // BLOCK
    if split.wide:
        for half in range(2):

            @pl.when(rank_ref[0] // (split.shards // 2) == half)
            def _():
                for part in range(split.parts):
                    for block in range(blocks):
                        attend(part, block, half * blocks + block)

    else:
        for block in range(blocks):
            attend(0, block, block)

    for one in range(2):
        out_ref[:, one * VDIM : (one + 1) * VDIM] = jnp.dot(
            mixed[one], weight(2 + one), preferred_element_type=F32
        ).astype(BF16)


def attention(split, place, queries, keys, other_keys, weights, other_weights):
    count = queries.shape[0]
    length = 2 * keys.shape[0] * keys.shape[1] // split.parts
    whole = pl.BlockSpec(keys.shape, lambda p, place: (0, 0, 0))
    each = split.pairs // 2
    return call(
        functools.partial(attention_kernel, split),
        "causal_attention",
        flops=4 * count * length * split.pairs * (2 * LATENT + ROPE),
        moved=4 * (queries.size + keys.size + weights.size),
        grid_spec=pltpu.PrefetchScalarGridSpec(
            num_scalar_prefetch=1,
            grid=(split.pairs,),
            in_specs=[
                pl.BlockSpec((count, 2 * (NOPE + ROPE)), lambda p, place: (0, p)),
                whole,
                whole,
                pl.BlockSpec((1, 4, LATENT, VDIM), lambda p, place: (jnp.minimum(p, each - 1), 0, 0, 0)),
                pl.BlockSpec((1, 4, LATENT, VDIM), lambda p, place: (jnp.maximum(p - each, 0), 0, 0, 0)),
            ],
            out_specs=pl.BlockSpec((count, 2 * VDIM), lambda p, place: (0, p)),
            scratch_shapes=[
                pltpu.VMEM((split.parts, length, LATENT + 2 * ROPE), BF16),
                pltpu.VMEM((2, count, LATENT + 2 * ROPE), BF16),
                pltpu.VMEM((2, count, LATENT), BF16),
            ],
        ),
        out_shape=jax.ShapeDtypeStruct((count, 2 * split.pairs * VDIM), BF16),
    )(place, queries, keys, other_keys, weights, other_weights)


def send(array, mask):
    count = lax.axis_size("groups") * lax.axis_size("ctx")
    return lax.ppermute(array, ("groups", "ctx"), [(i, i ^ mask) for i in range(count)])


def swap_chips(array):
    shards = lax.axis_size("ctx")
    return lax.all_to_all(
        array,
        "ctx",
        split_axis=0,
        concat_axis=0,
        axis_index_groups=[list(range(core, shards, 2)) for core in range(2)],
        tiled=True,
    )


def after(array, *others):
    return lax.optimization_barrier((array, *others))[0]


def gather_masks(split):
    top, below = split.shards // 2, split.shards // 4
    later = [1 << bit for bit in reversed(range(1, below.bit_length() - 1))]
    return [top, below, top ^ below], later + ([split.shards] if split.wide else [])


def gather_order(split):
    direct, later = gather_masks(split)
    order = [0] + direct
    for mask in later:
        order = order + [offset ^ mask for offset in order]
    return order


def on_device(
    queries,
    latent_kv,
    key_proj,
    value_proj,
    moe_input,
    routes,
    gates,
    expert_gate,
    expert_up,
    expert_down,
):
    shards = lax.axis_size("ctx")
    split = Split(lax.axis_size("groups"), shards, HEADS)
    tok = queries.shape[0]
    experts = shards // 2
    capacity = 2 * ((4 * tok * TOP + 6 * experts - 1) // (6 * experts))
    rows = -(-capacity // 8) * 8
    rank = lax.axis_index("ctx").astype(jnp.int32).reshape(1)
    group = lax.axis_index("groups").astype(jnp.int32).reshape(1)
    place = jnp.concatenate([rank, group])

    direct, later = gather_masks(split)
    keys = jnp.stack([latent_kv] + [send(latent_kv, offset) for offset in direct])

    buckets = after(build_buckets(routes, moe_input, experts, rows), keys)
    arrived = swap_chips(buckets.reshape(experts, rows, D)).reshape(experts * rows, D)

    for mask in later:
        keys = jnp.concatenate([keys, send(keys, mask)], axis=0)
    own_half = [expert_gate, expert_up, expert_down]
    other_half = [send(part, 1) for part in own_half]
    sent = after(split_queries(split, rank, queries), keys, arrived, *other_half)
    held = split.exchange(sent).reshape(experts * tok, -1)

    weights = jnp.concatenate(
        [
            key_proj.swapaxes(1, 2).reshape(-1, 2, LATENT, NOPE),
            value_proj.reshape(-1, 2, LATENT, VDIM),
        ],
        axis=1,
    )
    if split.wide:
        weights = lax.dynamic_slice_in_dim(weights, group[0] * split.own_pairs, split.own_pairs, axis=0)
        weights = after(weights, arrived)
        weights = jnp.concatenate([weights, send(weights, shards // 2)], axis=0)

    result = expert_rows(arrived, own_half, other_half)
    result, held, weights = lax.optimization_barrier((result, held, weights))
    back = swap_chips(result.reshape(experts, rows, D))
    values = attention(split, place, held, keys, send(keys, 1), weights, send(weights, 1))
    values, back = lax.optimization_barrier((values, back))
    values = split.exchange(values.reshape(experts, tok, values.shape[1]))
    moe_out = combine(routes, gates, back.reshape(experts * rows, D), rows)
    return (join_values(split, rank, values), moe_out)


def solution(mesh):
    return jax.shard_map(
        on_device,
        mesh=mesh,
        in_specs=(
            P(("groups", "ctx"), None),
            P(("groups", "ctx"), None),
            P("ctx", None, None),
            P("ctx", None, None),
            P(("groups", "ctx"), None),
            P(("groups", "ctx"), None),
            P(("groups", "ctx"), None),
            P("ctx", None, None),
            P("ctx", None, None),
            P("ctx", None, None),
        ),
        out_specs=(P(("groups", "ctx"), None), P(("groups", "ctx"), None)),
        check_vma=False,
    )
```

```python
import functools
import math

import jax
import jax.numpy as jnp
from jax import lax
from jax.experimental import pallas as pl
from jax.experimental.pallas import tpu as pltpu
from jax.sharding import PartitionSpec as P

D = 3584
HEADS = 64
NOPE = 128
ROPE = 64
LATENT = 512
VDIM = 128
TOP = 2
HALF = 512
VMEM_LIMIT = 50 * 1024 * 1024
F32 = jnp.float32
BF16 = jnp.bfloat16


SMEM = pl.BlockSpec(memory_space=pltpu.SMEM)
VMEM = pl.BlockSpec(memory_space=pltpu.VMEM)


def call(kernel, name, flops=0, moved=0, **options):
    return pl.pallas_call(
        kernel,
        name=name,
        cost_estimate=pl.CostEstimate(flops=flops, bytes_accessed=moved, transcendentals=0),
        compiler_params=pltpu.CompilerParams(vmem_limit_bytes=VMEM_LIMIT),
        **options,
    )


def slot_targets(routes, rows):
    tok = routes.shape[0]
    lane = lax.broadcasted_iota(jnp.int32, (tok, 128), 1)
    first = routes[:, 0:1]
    second = routes[:, 1:2]
    hot0 = jnp.where(lane == first, 1.0, 0.0)
    hot1 = jnp.where(lane == second, 1.0, 0.0)
    earlier = jnp.where(
        lax.broadcasted_iota(jnp.int32, (tok, tok), 1) < lax.broadcasted_iota(jnp.int32, (tok, tok), 0),
        1.0,
        0.0,
    )
    counts = jnp.dot(earlier.astype(BF16), (hot0 + hot1).astype(BF16), preferred_element_type=F32)
    slot0 = jnp.sum(counts * hot0, axis=1, keepdims=True).astype(jnp.int32)
    slot1 = jnp.sum(counts * hot1, axis=1, keepdims=True).astype(jnp.int32)
    return first * rows + slot0, second * rows + slot1


def bucket_kernel(rows, routes_ref, x_ref, out_ref):
    target0, target1 = slot_targets(routes_ref[...], rows)
    column = lax.broadcasted_iota(jnp.int32, (x_ref.shape[0], out_ref.shape[0]), 1)
    chosen = jnp.where((column == target0) | (column == target1), 1.0, 0.0).astype(BF16)
    out_ref[...] = lax.dot_general(
        chosen, x_ref[...], (((0,), (0,)), ((), ())), preferred_element_type=F32
    ).astype(BF16)


def build_buckets(routes, moe_input, experts, rows):
    return call(
        functools.partial(bucket_kernel, rows),
        "bucket_rows",
        moved=2 * D * (moe_input.shape[0] + experts * rows),
        out_shape=jax.ShapeDtypeStruct((experts * rows, D), BF16),
    )(routes, moe_input)


def combine_kernel(rows, routes_ref, gates_ref, back_ref, out_ref):
    back = back_ref[...]
    tok = routes_ref.shape[0]
    target0, target1 = slot_targets(routes_ref[...], rows)
    targets = jnp.concatenate([target0, target1], axis=0)
    column = lax.broadcasted_iota(jnp.int32, (2 * tok, back.shape[0]), 1)
    chosen = jnp.where(column == targets, 1.0, 0.0).astype(BF16)
    picked = jnp.dot(chosen, back, preferred_element_type=F32)
    out_ref[...] = (picked[:tok] * gates_ref[:, 0:1] + picked[tok:] * gates_ref[:, 1:2]).astype(BF16)


def combine(routes, gates, back, rows):
    return call(
        functools.partial(combine_kernel, rows),
        "combine_routes",
        moved=2 * D * (routes.shape[0] + back.shape[0]),
        out_shape=jax.ShapeDtypeStruct((routes.shape[0], D), BF16),
    )(routes, gates, back)


STEP = 896
STEPS = D // STEP


def expert_kernel(x_ref, gate0, up0, gate1, up1, down0, down1, out_ref, sums, hidden):
    step = pl.program_id(0)

    @pl.when(step < STEPS)
    def _():
        x = x_ref[...]
        for index, weight_ref in enumerate((gate0, up0, gate1, up1)):
            part = jnp.dot(x, weight_ref[0], preferred_element_type=F32)
            sums[index] = jnp.where(step == 0, part, sums[index] + part)

    @pl.when(step == STEPS)
    def _():
        for half in range(2):
            value = sums[2 * half]
            hidden[half] = (value / (1.0 + jnp.exp(-value)) * sums[2 * half + 1]).astype(BF16)

    @pl.when(step >= STEPS)
    def _():
        first = jnp.dot(hidden[0], down0[0], preferred_element_type=F32).astype(BF16)
        second = jnp.dot(hidden[1], down1[0], preferred_element_type=F32).astype(BF16)
        out_ref[...] = (first.astype(F32) + second.astype(F32)).astype(BF16)


def expert_rows(x, own, other):
    count = x.shape[0]
    weights = pl.BlockSpec((1, STEP, HALF), lambda k: (0, jnp.minimum(k, STEPS - 1), 0))
    down = pl.BlockSpec((1, HALF, STEP), lambda k: (0, 0, jnp.maximum(k - STEPS, 0)))
    return call(
        expert_kernel,
        "expert_rows",
        flops=12 * count * D * HALF,
        moved=12 * D * HALF + 4 * count * D,
        grid=(2 * STEPS,),
        in_specs=[pl.BlockSpec((count, STEP), lambda k: (0, jnp.minimum(k, STEPS - 1)))] + [weights] * 4 + [down] * 2,
        out_specs=pl.BlockSpec((count, STEP), lambda k: (0, jnp.maximum(k - STEPS, 0))),
        scratch_shapes=[pltpu.VMEM((4, count, HALF), F32), pltpu.VMEM((2, count, HALF), BF16)],
        out_shape=jax.ShapeDtypeStruct((count, D), BF16),
    )(x, own[0], own[1], other[0], other[1], own[2], other[2])


class Split:
    def __init__(self, groups, shards, heads):
        self.groups, self.shards = groups, shards
        self.each = heads // shards
        self.wide = groups == 2 and self.each % (2 * groups) == 0
        self.chips = shards // 2
        self.own_pairs = self.each // 2 // (groups if self.wide else 1)
        self.holders = 2 if self.wide else 1
        self.pairs = 2 * self.holders * self.own_pairs
        self.parts = groups if self.wide else 1

    def first_head(self, rank, chip, pair):
        core, rest = divmod(pair, self.holders * self.own_pairs)
        holder, own = divmod(rest, self.own_pairs)
        if not self.wide:
            return (2 * chip + ((rank & 1) ^ core)) * self.each + 2 * own
        group, low = divmod(chip, self.shards // 4)
        top = (rank & (self.shards // 2)) ^ (holder * (self.shards // 2))
        return (top + 2 * low + ((rank & 1) ^ core)) * self.each + 2 * (group * self.own_pairs + own)

    def exchange(self, array):
        half = self.shards // 2
        if self.wide:
            tops, steps = (0, half), [g * self.shards + c for g in range(self.groups) for c in range(0, half, 2)]
            sets = [[start + core + step for step in steps] for start in tops for core in range(2)]
        else:
            starts = range(0, self.groups * self.shards, self.shards)
            sets = [[start + core + c for c in range(0, self.shards, 2)] for start in starts for core in range(2)]
        return lax.all_to_all(
            array, ("groups", "ctx"), split_axis=0, concat_axis=0, axis_index_groups=sets, tiled=True
        )


def split_kernel(split, rank_ref, x_ref, out_ref):
    each = NOPE + ROPE
    for chip in range(split.chips):
        for pair in range(split.pairs):
            start = pl.multiple_of(split.first_head(rank_ref[0], chip, pair) * each, 128)
            part = x_ref[:, pl.ds(start, 2 * each)]
            out_ref[chip, :, pair * 2 * each : (pair + 1) * 2 * each] = jnp.concatenate(
                [part[:, :NOPE], part[:, each : each + NOPE], part[:, NOPE:each], part[:, each + NOPE :]], axis=1
            )


def split_queries(split, rank, queries):
    tok = queries.shape[0]
    return call(
        functools.partial(split_kernel, split),
        "split_queries",
        moved=4 * queries.size,
        in_specs=[SMEM, VMEM],
        out_specs=VMEM,
        out_shape=jax.ShapeDtypeStruct((split.chips, tok, 2 * split.pairs * (NOPE + ROPE)), BF16),
    )(rank, queries)


def join_kernel(split, rank_ref, x_ref, out_ref):
    for chip in range(split.chips):
        for pair in range(split.pairs):
            start = pl.multiple_of(split.first_head(rank_ref[0], chip, pair) * VDIM, 128)
            out_ref[:, pl.ds(start, 2 * VDIM)] = x_ref[chip, :, pair * 2 * VDIM : (pair + 1) * 2 * VDIM]


def join_values(split, rank, values):
    return call(
        functools.partial(join_kernel, split),
        "join_values",
        moved=4 * values.size,
        in_specs=[SMEM, VMEM],
        out_specs=VMEM,
        out_shape=jax.ShapeDtypeStruct((values.shape[1], HEADS * VDIM), BF16),
    )(rank, values)


BLOCK = 128
SPAN = 2 * BLOCK
EXP_SCALE = math.log2(math.e) / math.sqrt(NOPE + ROPE)


def attention_kernel(
    split, rank_ref, query_ref, kv_ref, other_kv_ref, weight_ref, other_weight_ref, out_ref, keys, queries, mixed
):
    tok = kv_ref.shape[1]
    part_rows = query_ref.shape[0] // split.parts
    core = rank_ref[0] & 1

    @pl.when(pl.program_id(0) == 0)
    def _():
        for index, offset in enumerate(gather_order(split)):
            for from_ref, swapped in ((kv_ref, 0), (other_kv_ref, 1)):
                group, ctx = divmod(offset ^ swapped, split.shards)
                group = rank_ref[1] ^ group if split.wide else 0
                place = pl.ds(pl.multiple_of((rank_ref[0] ^ ctx) * tok, tok), tok)
                keys[group, place, : LATENT + ROPE] = from_ref[index]
                keys[group, place, LATENT + ROPE :] = from_ref[index, :, LATENT:]

    own_core = pl.program_id(0) < split.pairs // 2

    def weight(index):
        return jnp.where(own_core, weight_ref[0, index], other_weight_ref[0, index])

    contract = (((1,), (1,)), ((), ()))
    side = lax.broadcasted_iota(jnp.int32, (1, 2 * ROPE), 1) // ROPE
    for one in range(2):
        latent = lax.dot_general(
            query_ref[:, one * NOPE : (one + 1) * NOPE], weight(one), contract, preferred_element_type=F32
        )
        queries[one, :, :LATENT] = latent.astype(BF16)
        queries[one, :, LATENT:] = jnp.where(side == one, query_ref[:, 2 * NOPE :], jnp.zeros((), BF16))

    row = lax.broadcasted_iota(jnp.int32, (2 * BLOCK, SPAN), 0) % BLOCK
    position = (2 * (row // tok) + core) * tok + row % tok
    visible = lax.broadcasted_iota(jnp.int32, (2 * BLOCK, SPAN), 1) <= position

    def attend(part, block, before):
        start = before * SPAN
        first = part * part_rows + block * BLOCK
        rows = pl.ds(first, BLOCK)
        last = pl.ds(start, SPAN)
        query = jnp.concatenate([queries[0, rows, :], queries[1, rows, :]], axis=0)
        near = lax.dot_general(query, keys[part, last, :], contract, preferred_element_type=F32)
        near = jnp.where(visible, near, -1e30)
        top = jnp.max(near, axis=1, keepdims=True)
        if before:
            past = lax.dot_general(query, keys[part, :start, :], contract, preferred_element_type=F32)
            top = jnp.maximum(top, jnp.max(past, axis=1, keepdims=True))
        weights = jnp.exp2((near - top) * EXP_SCALE)
        total = jnp.sum(weights, axis=1, keepdims=True)
        summed = jnp.dot(weights.astype(BF16), keys[part, last, :LATENT], preferred_element_type=F32)
        if before:
            weights = jnp.exp2((past - top) * EXP_SCALE)
            total = total + jnp.sum(weights, axis=1, keepdims=True)
            summed = summed + jnp.dot(
                weights.astype(BF16), keys[part, :start, :LATENT], preferred_element_type=F32
            )
        result = (summed / total).astype(BF16)
        mixed[0, rows, :] = result[:BLOCK]
        mixed[1, rows, :] = result[BLOCK:]

    blocks = part_rows // BLOCK
    if split.wide:
        for half in range(2):

            @pl.when(rank_ref[0] // (split.shards // 2) == half)
            def _():
                for part in range(split.parts):
                    for block in range(blocks):
                        attend(part, block, half * blocks + block)

    else:
        for block in range(blocks):
            attend(0, block, block)

    for one in range(2):
        out_ref[:, one * VDIM : (one + 1) * VDIM] = jnp.dot(
            mixed[one], weight(2 + one), preferred_element_type=F32
        ).astype(BF16)


def attention(split, place, queries, keys, other_keys, weights, other_weights):
    count = queries.shape[0]
    length = 2 * keys.shape[0] * keys.shape[1] // split.parts
    whole = pl.BlockSpec(keys.shape, lambda p, place: (0, 0, 0))
    each = split.pairs // 2
    return call(
        functools.partial(attention_kernel, split),
        "causal_attention",
        flops=4 * count * length * split.pairs * (2 * LATENT + ROPE),
        moved=4 * (queries.size + keys.size + weights.size),
        grid_spec=pltpu.PrefetchScalarGridSpec(
            num_scalar_prefetch=1,
            grid=(split.pairs,),
            in_specs=[
                pl.BlockSpec((count, 2 * (NOPE + ROPE)), lambda p, place: (0, p)),
                whole,
                whole,
                pl.BlockSpec((1, 4, LATENT, VDIM), lambda p, place: (jnp.minimum(p, each - 1), 0, 0, 0)),
                pl.BlockSpec((1, 4, LATENT, VDIM), lambda p, place: (jnp.maximum(p - each, 0), 0, 0, 0)),
            ],
            out_specs=pl.BlockSpec((count, 2 * VDIM), lambda p, place: (0, p)),
            scratch_shapes=[
                pltpu.VMEM((split.parts, length, LATENT + 2 * ROPE), BF16),
                pltpu.VMEM((2, count, LATENT + 2 * ROPE), BF16),
                pltpu.VMEM((2, count, LATENT), BF16),
            ],
        ),
        out_shape=jax.ShapeDtypeStruct((count, 2 * split.pairs * VDIM), BF16),
    )(place, queries, keys, other_keys, weights, other_weights)


def send(array, mask):
    count = lax.axis_size("groups") * lax.axis_size("ctx")
    return lax.ppermute(array, ("groups", "ctx"), [(i, i ^ mask) for i in range(count)])


def swap_chips(array):
    shards = lax.axis_size("ctx")
    return lax.all_to_all(
        array,
        "ctx",
        split_axis=0,
        concat_axis=0,
        axis_index_groups=[list(range(core, shards, 2)) for core in range(2)],
        tiled=True,
    )


def after(array, *others):
    return lax.optimization_barrier((array, *others))[0]


def gather_masks(split):
    top, below = split.shards // 2, split.shards // 4
    later = [1 << bit for bit in reversed(range(1, below.bit_length() - 1))]
    return [top, below, top ^ below], ([split.shards] if split.wide else []) + later


def gather_order(split):
    direct, later = gather_masks(split)
    order = [0] + direct
    for mask in later:
        order = order + [offset ^ mask for offset in order]
    return order


def on_device(
    queries,
    latent_kv,
    key_proj,
    value_proj,
    moe_input,
    routes,
    gates,
    expert_gate,
    expert_up,
    expert_down,
):
    shards = lax.axis_size("ctx")
    split = Split(lax.axis_size("groups"), shards, HEADS)
    tok = queries.shape[0]
    experts = shards // 2
    capacity = 2 * ((4 * tok * TOP + 6 * experts - 1) // (6 * experts))
    rows = -(-capacity // 8) * 8
    rank = lax.axis_index("ctx").astype(jnp.int32).reshape(1)
    group = lax.axis_index("groups").astype(jnp.int32).reshape(1)
    place = jnp.concatenate([rank, group])

    direct, later = gather_masks(split)
    keys = jnp.stack([latent_kv] + [send(latent_kv, offset) for offset in direct])

    buckets = after(build_buckets(routes, moe_input, experts, rows), keys)
    arrived = swap_chips(buckets.reshape(experts, rows, D)).reshape(experts * rows, D)

    for mask in later:
        keys = jnp.concatenate([keys, send(keys, mask)], axis=0)
    other_keys = send(keys, 1)
    own_half = [expert_gate, expert_up, expert_down]
    other_half = [send(part, 1) for part in own_half]
    sent = after(split_queries(split, rank, queries), other_keys, arrived, *other_half)
    held = split.exchange(sent).reshape(experts * tok, -1)

    weights = jnp.concatenate(
        [
            key_proj.swapaxes(1, 2).reshape(-1, 2, LATENT, NOPE),
            value_proj.reshape(-1, 2, LATENT, VDIM),
        ],
        axis=1,
    )
    if split.wide:
        weights = lax.dynamic_slice_in_dim(weights, group[0] * split.own_pairs, split.own_pairs, axis=0)
        weights = after(weights, arrived)
        weights = jnp.concatenate([weights, send(weights, shards // 2)], axis=0)

    result = expert_rows(arrived, own_half, other_half)
    other_weights = send(after(weights, result), 1)
    result, held = lax.optimization_barrier((result, held))
    back = swap_chips(result.reshape(experts, rows, D))
    values = attention(split, place, held, keys, other_keys, weights, other_weights)
    values, back = lax.optimization_barrier((values, back))
    values = split.exchange(values.reshape(experts, tok, values.shape[1]))
    moe_out = combine(routes, gates, back.reshape(experts * rows, D), rows)
    return (join_values(split, rank, values), moe_out)


def solution(mesh):
    return jax.shard_map(
        on_device,
        mesh=mesh,
        in_specs=(
            P(("groups", "ctx"), None),
            P(("groups", "ctx"), None),
            P("ctx", None, None),
            P("ctx", None, None),
            P(("groups", "ctx"), None),
            P(("groups", "ctx"), None),
            P(("groups", "ctx"), None),
            P("ctx", None, None),
            P("ctx", None, None),
            P("ctx", None, None),
        ),
        out_specs=(P(("groups", "ctx"), None), P(("groups", "ctx"), None)),
        check_vma=False,
    )
```

```python
import functools
import math

import jax
import jax.numpy as jnp
from jax import lax
from jax.experimental import pallas as pl
from jax.experimental.pallas import tpu as pltpu
from jax.sharding import PartitionSpec as P

D = 3584
HEADS = 64
NOPE = 128
ROPE = 64
LATENT = 512
VDIM = 128
TOP = 2
HALF = 512
VMEM_LIMIT = 50 * 1024 * 1024
F32 = jnp.float32
BF16 = jnp.bfloat16


SMEM = pl.BlockSpec(memory_space=pltpu.SMEM)
VMEM = pl.BlockSpec(memory_space=pltpu.VMEM)


def call(kernel, name, flops=0, moved=0, **options):
    return pl.pallas_call(
        kernel,
        name=name,
        cost_estimate=pl.CostEstimate(flops=flops, bytes_accessed=moved, transcendentals=0),
        compiler_params=pltpu.CompilerParams(vmem_limit_bytes=VMEM_LIMIT),
        **options,
    )


def slot_targets(routes, rows):
    tok = routes.shape[0]
    lane = lax.broadcasted_iota(jnp.int32, (tok, 128), 1)
    first = routes[:, 0:1]
    second = routes[:, 1:2]
    hot0 = jnp.where(lane == first, 1.0, 0.0)
    hot1 = jnp.where(lane == second, 1.0, 0.0)
    earlier = jnp.where(
        lax.broadcasted_iota(jnp.int32, (tok, tok), 1) < lax.broadcasted_iota(jnp.int32, (tok, tok), 0),
        1.0,
        0.0,
    )
    counts = jnp.dot(earlier.astype(BF16), (hot0 + hot1).astype(BF16), preferred_element_type=F32)
    slot0 = jnp.sum(counts * hot0, axis=1, keepdims=True).astype(jnp.int32)
    slot1 = jnp.sum(counts * hot1, axis=1, keepdims=True).astype(jnp.int32)
    return first * rows + slot0, second * rows + slot1


def bucket_kernel(rows, routes_ref, x_ref, out_ref):
    target0, target1 = slot_targets(routes_ref[...], rows)
    column = lax.broadcasted_iota(jnp.int32, (x_ref.shape[0], out_ref.shape[0]), 1)
    chosen = jnp.where((column == target0) | (column == target1), 1.0, 0.0).astype(BF16)
    out_ref[...] = lax.dot_general(
        chosen, x_ref[...], (((0,), (0,)), ((), ())), preferred_element_type=F32
    ).astype(BF16)


def build_buckets(routes, moe_input, experts, rows):
    return call(
        functools.partial(bucket_kernel, rows),
        "bucket_rows",
        moved=2 * D * (moe_input.shape[0] + experts * rows),
        out_shape=jax.ShapeDtypeStruct((experts * rows, D), BF16),
    )(routes, moe_input)


def combine_kernel(rows, routes_ref, gates_ref, *refs):
    out_ref = refs[-1]
    back = jnp.concatenate([ref[...] for ref in refs[:-1]], axis=0)
    tok = routes_ref.shape[0]
    target0, target1 = slot_targets(routes_ref[...], rows)
    targets = jnp.concatenate([target0, target1], axis=0)
    column = lax.broadcasted_iota(jnp.int32, (2 * tok, back.shape[0]), 1)
    chosen = jnp.where(column == targets, 1.0, 0.0).astype(BF16)
    picked = jnp.dot(chosen, back, preferred_element_type=F32)
    out_ref[...] = (picked[:tok] * gates_ref[:, 0:1] + picked[tok:] * gates_ref[:, 1:2]).astype(BF16)


def combine(routes, gates, back, rows):
    return call(
        functools.partial(combine_kernel, rows),
        "combine_routes",
        moved=2 * D * (routes.shape[0] + len(back) * rows),
        out_shape=jax.ShapeDtypeStruct((routes.shape[0], D), BF16),
    )(routes, gates, *back)


STEP = 896
STEPS = D // STEP


def expert_kernel(rank_ref, x_ref, gate0, up0, gate1, up1, down0, down1, *refs):
    out_refs = refs[:-3]
    sums, hidden, result = refs[-3:]
    rows = result.shape[1]
    step = pl.program_id(0)

    @pl.when(step < STEPS)
    def _():
        x = x_ref[...]
        for index, weight_ref in enumerate((gate0, up0, gate1, up1)):
            part = jnp.dot(x, weight_ref[0], preferred_element_type=F32)
            sums[index] = jnp.where(step == 0, part, sums[index] + part)

    @pl.when(step == STEPS)
    def _():
        for half in range(2):
            value = sums[2 * half]
            hidden[half] = (value / (1.0 + jnp.exp(-value)) * sums[2 * half + 1]).astype(BF16)

    @pl.when(step >= STEPS)
    def _():
        first = jnp.dot(hidden[0], down0[0], preferred_element_type=F32).astype(BF16)
        second = jnp.dot(hidden[1], down1[0], preferred_element_type=F32).astype(BF16)
        both = (first.astype(F32) + second.astype(F32)).astype(BF16)
        for chip in range(len(out_refs)):
            result[chip] = both[chip * rows : (chip + 1) * rows]
        for offset, out_ref in enumerate(out_refs):
            out_ref[...] = result[(rank_ref[0] // 2) ^ offset]


def expert_rows(rank, x, own, other, experts):
    count = x.shape[0]
    rows = count // experts
    weights = pl.BlockSpec((1, STEP, HALF), lambda k, rank: (0, jnp.minimum(k, STEPS - 1), 0))
    down = pl.BlockSpec((1, HALF, STEP), lambda k, rank: (0, 0, jnp.maximum(k - STEPS, 0)))
    columns = pl.BlockSpec((count, STEP), lambda k, rank: (0, jnp.minimum(k, STEPS - 1)))
    return call(
        expert_kernel,
        "expert_rows",
        flops=12 * count * D * HALF,
        moved=12 * D * HALF + 4 * count * D,
        grid_spec=pltpu.PrefetchScalarGridSpec(
            num_scalar_prefetch=1,
            grid=(2 * STEPS,),
            in_specs=[columns] + [weights] * 4 + [down] * 2,
            out_specs=[pl.BlockSpec((rows, STEP), lambda k, rank: (0, jnp.maximum(k - STEPS, 0)))] * experts,
            scratch_shapes=[
                pltpu.VMEM((4, count, HALF), F32),
                pltpu.VMEM((2, count, HALF), BF16),
                pltpu.VMEM((experts, rows, STEP), BF16),
            ],
        ),
        out_shape=[jax.ShapeDtypeStruct((rows, D), BF16)] * experts,
    )(rank, x, own[0], own[1], other[0], other[1], own[2], other[2])


class Split:
    def __init__(self, groups, shards, heads):
        self.groups, self.shards = groups, shards
        self.each = heads // shards
        self.wide = groups == 2 and self.each % (2 * groups) == 0
        self.chips = shards // 2
        self.own_pairs = self.each // 2 // (groups if self.wide else 1)
        self.holders = 2 if self.wide else 1
        self.pairs = 2 * self.holders * self.own_pairs
        self.parts = groups if self.wide else 1

    def first_head(self, rank, chip, pair):
        core, rest = divmod(pair, self.holders * self.own_pairs)
        holder, own = divmod(rest, self.own_pairs)
        if not self.wide:
            return (2 * chip + ((rank & 1) ^ core)) * self.each + 2 * own
        group, low = divmod(chip, self.shards // 4)
        top = (rank & (self.shards // 2)) ^ (holder * (self.shards // 2))
        return (top + 2 * low + ((rank & 1) ^ core)) * self.each + 2 * (group * self.own_pairs + own)

    def exchange(self, array):
        half = self.shards // 2
        if self.wide:
            tops, steps = (0, half), [g * self.shards + c for g in range(self.groups) for c in range(0, half, 2)]
            sets = [[start + core + step for step in steps] for start in tops for core in range(2)]
        else:
            starts = range(0, self.groups * self.shards, self.shards)
            sets = [[start + core + c for c in range(0, self.shards, 2)] for start in starts for core in range(2)]
        return lax.all_to_all(
            array, ("groups", "ctx"), split_axis=0, concat_axis=0, axis_index_groups=sets, tiled=True
        )


def split_kernel(split, rank_ref, x_ref, out_ref):
    each = NOPE + ROPE
    for chip in range(split.chips):
        for pair in range(split.pairs):
            start = pl.multiple_of(split.first_head(rank_ref[0], chip, pair) * each, 128)
            part = x_ref[:, pl.ds(start, 2 * each)]
            out_ref[chip, :, pair * 2 * each : (pair + 1) * 2 * each] = jnp.concatenate(
                [part[:, :NOPE], part[:, each : each + NOPE], part[:, NOPE:each], part[:, each + NOPE :]], axis=1
            )


def split_queries(split, rank, queries):
    tok = queries.shape[0]
    return call(
        functools.partial(split_kernel, split),
        "split_queries",
        moved=4 * queries.size,
        in_specs=[SMEM, VMEM],
        out_specs=VMEM,
        out_shape=jax.ShapeDtypeStruct((split.chips, tok, 2 * split.pairs * (NOPE + ROPE)), BF16),
    )(rank, queries)


def join_kernel(split, rank_ref, x_ref, out_ref):
    for chip in range(split.chips):
        for pair in range(split.pairs):
            start = pl.multiple_of(split.first_head(rank_ref[0], chip, pair) * VDIM, 128)
            out_ref[:, pl.ds(start, 2 * VDIM)] = x_ref[chip, :, pair * 2 * VDIM : (pair + 1) * 2 * VDIM]


def join_values(split, rank, values):
    return call(
        functools.partial(join_kernel, split),
        "join_values",
        moved=4 * values.size,
        in_specs=[SMEM, VMEM],
        out_specs=VMEM,
        out_shape=jax.ShapeDtypeStruct((values.shape[1], HEADS * VDIM), BF16),
    )(rank, values)


BLOCK = 128
SPAN = 2 * BLOCK
EXP_SCALE = math.log2(math.e) / math.sqrt(NOPE + ROPE)


def attention_kernel(
    split, rank_ref, query_ref, kv_ref, other_kv_ref, weight_ref, other_weight_ref, out_ref, keys, queries, mixed
):
    tok = kv_ref.shape[1]
    part_rows = query_ref.shape[0] // split.parts
    core = rank_ref[0] & 1

    @pl.when(pl.program_id(0) == 0)
    def _():
        for index, offset in enumerate(gather_order(split)):
            for from_ref, swapped in ((kv_ref, 0), (other_kv_ref, 1)):
                group, ctx = divmod(offset ^ swapped, split.shards)
                group = rank_ref[1] ^ group if split.wide else 0
                place = pl.ds(pl.multiple_of((rank_ref[0] ^ ctx) * tok, tok), tok)
                keys[group, place, : LATENT + ROPE] = from_ref[index]
                keys[group, place, LATENT + ROPE :] = from_ref[index, :, LATENT:]

    own_core = pl.program_id(0) < split.pairs // 2

    def weight(index):
        return jnp.where(own_core, weight_ref[0, index], other_weight_ref[0, index])

    contract = (((1,), (1,)), ((), ()))
    side = lax.broadcasted_iota(jnp.int32, (1, 2 * ROPE), 1) // ROPE
    for one in range(2):
        latent = lax.dot_general(
            query_ref[:, one * NOPE : (one + 1) * NOPE], weight(one), contract, preferred_element_type=F32
        )
        queries[one, :, :LATENT] = latent.astype(BF16)
        queries[one, :, LATENT:] = jnp.where(side == one, query_ref[:, 2 * NOPE :], jnp.zeros((), BF16))

    row = lax.broadcasted_iota(jnp.int32, (2 * BLOCK, SPAN), 0) % BLOCK
    position = (2 * (row // tok) + core) * tok + row % tok
    visible = lax.broadcasted_iota(jnp.int32, (2 * BLOCK, SPAN), 1) <= position

    def attend(part, block, before):
        start = before * SPAN
        first = part * part_rows + block * BLOCK
        rows = pl.ds(first, BLOCK)
        last = pl.ds(start, SPAN)
        query = jnp.concatenate([queries[0, rows, :], queries[1, rows, :]], axis=0)
        near = lax.dot_general(query, keys[part, last, :], contract, preferred_element_type=F32)
        near = jnp.where(visible, near, -1e30)
        top = jnp.max(near, axis=1, keepdims=True)
        if before:
            past = lax.dot_general(query, keys[part, :start, :], contract, preferred_element_type=F32)
            top = jnp.maximum(top, jnp.max(past, axis=1, keepdims=True))
        weights = jnp.exp2((near - top) * EXP_SCALE)
        total = jnp.sum(weights, axis=1, keepdims=True)
        summed = jnp.dot(weights.astype(BF16), keys[part, last, :LATENT], preferred_element_type=F32)
        if before:
            weights = jnp.exp2((past - top) * EXP_SCALE)
            total = total + jnp.sum(weights, axis=1, keepdims=True)
            summed = summed + jnp.dot(
                weights.astype(BF16), keys[part, :start, :LATENT], preferred_element_type=F32
            )
        result = (summed / total).astype(BF16)
        mixed[0, rows, :] = result[:BLOCK]
        mixed[1, rows, :] = result[BLOCK:]

    blocks = part_rows // BLOCK
    if split.wide:
        for half in range(2):

            @pl.when(rank_ref[0] // (split.shards // 2) == half)
            def _():
                for part in range(split.parts):
                    for block in range(blocks):
                        attend(part, block, half * blocks + block)

    else:
        for block in range(blocks):
            attend(0, block, block)

    for one in range(2):
        out_ref[:, one * VDIM : (one + 1) * VDIM] = jnp.dot(
            mixed[one], weight(2 + one), preferred_element_type=F32
        ).astype(BF16)


def attention(split, place, queries, keys, other_keys, weights, other_weights):
    count = queries.shape[0]
    length = 2 * keys.shape[0] * keys.shape[1] // split.parts
    whole = pl.BlockSpec(keys.shape, lambda p, place: (0, 0, 0))
    each = split.pairs // 2
    return call(
        functools.partial(attention_kernel, split),
        "causal_attention",
        flops=4 * count * length * split.pairs * (2 * LATENT + ROPE),
        moved=4 * (queries.size + keys.size + weights.size),
        grid_spec=pltpu.PrefetchScalarGridSpec(
            num_scalar_prefetch=1,
            grid=(split.pairs,),
            in_specs=[
                pl.BlockSpec((count, 2 * (NOPE + ROPE)), lambda p, place: (0, p)),
                whole,
                whole,
                pl.BlockSpec((1, 4, LATENT, VDIM), lambda p, place: (jnp.minimum(p, each - 1), 0, 0, 0)),
                pl.BlockSpec((1, 4, LATENT, VDIM), lambda p, place: (jnp.maximum(p - each, 0), 0, 0, 0)),
            ],
            out_specs=pl.BlockSpec((count, 2 * VDIM), lambda p, place: (0, p)),
            scratch_shapes=[
                pltpu.VMEM((split.parts, length, LATENT + 2 * ROPE), BF16),
                pltpu.VMEM((2, count, LATENT + 2 * ROPE), BF16),
                pltpu.VMEM((2, count, LATENT), BF16),
            ],
        ),
        out_shape=jax.ShapeDtypeStruct((count, 2 * split.pairs * VDIM), BF16),
    )(place, queries, keys, other_keys, weights, other_weights)


def send(array, mask):
    count = lax.axis_size("groups") * lax.axis_size("ctx")
    return lax.ppermute(array, ("groups", "ctx"), [(i, i ^ mask) for i in range(count)])


def swap_chips(array):
    shards = lax.axis_size("ctx")
    return lax.all_to_all(
        array,
        "ctx",
        split_axis=0,
        concat_axis=0,
        axis_index_groups=[list(range(core, shards, 2)) for core in range(2)],
        tiled=True,
    )


def after(array, *others):
    return lax.optimization_barrier((array, *others))[0]


def gather_masks(split):
    top, below = split.shards // 2, split.shards // 4
    later = [1 << bit for bit in reversed(range(1, below.bit_length() - 1))]
    return [top, below, top ^ below], ([split.shards] if split.wide else []) + later


def gather_order(split):
    direct, later = gather_masks(split)
    order = [0] + direct
    for mask in later:
        order = order + [offset ^ mask for offset in order]
    return order


def on_device(
    queries,
    latent_kv,
    key_proj,
    value_proj,
    moe_input,
    routes,
    gates,
    expert_gate,
    expert_up,
    expert_down,
):
    shards = lax.axis_size("ctx")
    split = Split(lax.axis_size("groups"), shards, HEADS)
    tok = queries.shape[0]
    experts = shards // 2
    capacity = 2 * ((4 * tok * TOP + 6 * experts - 1) // (6 * experts))
    rows = -(-capacity // 8) * 8
    rank = lax.axis_index("ctx").astype(jnp.int32).reshape(1)
    group = lax.axis_index("groups").astype(jnp.int32).reshape(1)
    place = jnp.concatenate([rank, group])

    direct, later = gather_masks(split)
    keys = [latent_kv] + [send(latent_kv, offset) for offset in direct]

    buckets = after(build_buckets(routes, moe_input, experts, rows), *keys)
    arrived = swap_chips(buckets.reshape(experts, rows, D)).reshape(experts * rows, D)

    keys = jnp.stack(keys)
    for mask in later:
        keys = jnp.concatenate([keys, send(keys, mask)], axis=0)
    other_keys = send(keys, 1)
    own_half = [expert_gate, expert_up, expert_down]
    other_half = [send(after(part, buckets), 1) for part in own_half]
    sent = after(split_queries(split, rank, queries), other_keys, arrived, *other_half)
    held = split.exchange(sent).reshape(experts * tok, -1)

    weights = jnp.concatenate(
        [
            key_proj.swapaxes(1, 2).reshape(-1, 2, LATENT, NOPE),
            value_proj.reshape(-1, 2, LATENT, VDIM),
        ],
        axis=1,
    )
    if split.wide:
        weights = lax.dynamic_slice_in_dim(weights, group[0] * split.own_pairs, split.own_pairs, axis=0)
        weights = after(weights, arrived)
        weights = jnp.concatenate([weights, send(weights, shards // 2)], axis=0)

    result = expert_rows(rank, arrived, own_half, other_half, experts)
    back = [result[0]] + [send(result[m], 2 * m) for m in range(1, experts)]
    other_weights = send(after(weights, result[0]), 1)
    held = after(held, result[0])
    values = attention(split, place, held, keys, other_keys, weights, other_weights)
    values, *back = lax.optimization_barrier((values, *back))
    values = split.exchange(values.reshape(experts, tok, values.shape[1]))
    moe_out = combine(routes ^ (rank // 2), gates, back, rows)
    return (join_values(split, rank, values), moe_out)


def solution(mesh):
    return jax.shard_map(
        on_device,
        mesh=mesh,
        in_specs=(
            P(("groups", "ctx"), None),
            P(("groups", "ctx"), None),
            P("ctx", None, None),
            P("ctx", None, None),
            P(("groups", "ctx"), None),
            P(("groups", "ctx"), None),
            P(("groups", "ctx"), None),
            P("ctx", None, None),
            P("ctx", None, None),
            P("ctx", None, None),
        ),
        out_specs=(P(("groups", "ctx"), None), P(("groups", "ctx"), None)),
        check_vma=False,
    )
```

```python
import functools
import math

import jax
import jax.numpy as jnp
from jax import lax
from jax.experimental import pallas as pl
from jax.experimental.pallas import tpu as pltpu
from jax.sharding import PartitionSpec as P

D = 3584
HEADS = 64
NOPE = 128
ROPE = 64
LATENT = 512
VDIM = 128
TOP = 2
HALF = 512
VMEM_LIMIT = 50 * 1024 * 1024
F32 = jnp.float32
BF16 = jnp.bfloat16


SMEM = pl.BlockSpec(memory_space=pltpu.SMEM)
VMEM = pl.BlockSpec(memory_space=pltpu.VMEM)


def call(kernel, name, flops=0, moved=0, **options):
    return pl.pallas_call(
        kernel,
        name=name,
        cost_estimate=pl.CostEstimate(flops=flops, bytes_accessed=moved, transcendentals=0),
        compiler_params=pltpu.CompilerParams(vmem_limit_bytes=VMEM_LIMIT),
        **options,
    )


def slot_targets(routes, rows):
    tok = routes.shape[0]
    lane = lax.broadcasted_iota(jnp.int32, (tok, 128), 1)
    first = routes[:, 0:1]
    second = routes[:, 1:2]
    hot0 = jnp.where(lane == first, 1.0, 0.0)
    hot1 = jnp.where(lane == second, 1.0, 0.0)
    earlier = jnp.where(
        lax.broadcasted_iota(jnp.int32, (tok, tok), 1) < lax.broadcasted_iota(jnp.int32, (tok, tok), 0),
        1.0,
        0.0,
    )
    counts = jnp.dot(earlier.astype(BF16), (hot0 + hot1).astype(BF16), preferred_element_type=F32)
    slot0 = jnp.sum(counts * hot0, axis=1, keepdims=True).astype(jnp.int32)
    slot1 = jnp.sum(counts * hot1, axis=1, keepdims=True).astype(jnp.int32)
    return first * rows + slot0, second * rows + slot1


def bucket_kernel(rows, routes_ref, x_ref, out_ref):
    target0, target1 = slot_targets(routes_ref[...], rows)
    column = lax.broadcasted_iota(jnp.int32, (x_ref.shape[0], out_ref.shape[0]), 1)
    chosen = jnp.where((column == target0) | (column == target1), 1.0, 0.0).astype(BF16)
    out_ref[...] = lax.dot_general(
        chosen, x_ref[...], (((0,), (0,)), ((), ())), preferred_element_type=F32
    ).astype(BF16)


def build_buckets(routes, moe_input, experts, rows):
    return call(
        functools.partial(bucket_kernel, rows),
        "bucket_rows",
        moved=2 * D * (moe_input.shape[0] + experts * rows),
        out_shape=jax.ShapeDtypeStruct((experts * rows, D), BF16),
    )(routes, moe_input)


def combine_kernel(rows, routes_ref, gates_ref, *refs):
    out_ref = refs[-1]
    back = jnp.concatenate([ref[...] for ref in refs[:-1]], axis=0)
    tok = routes_ref.shape[0]
    target0, target1 = slot_targets(routes_ref[...], rows)
    targets = jnp.concatenate([target0, target1], axis=0)
    column = lax.broadcasted_iota(jnp.int32, (2 * tok, back.shape[0]), 1)
    chosen = jnp.where(column == targets, 1.0, 0.0).astype(BF16)
    picked = jnp.dot(chosen, back, preferred_element_type=F32)
    out_ref[...] = (picked[:tok] * gates_ref[:, 0:1] + picked[tok:] * gates_ref[:, 1:2]).astype(BF16)


def combine(routes, gates, back, rows):
    return call(
        functools.partial(combine_kernel, rows),
        "combine_routes",
        moved=2 * D * (routes.shape[0] + len(back) * rows),
        out_shape=jax.ShapeDtypeStruct((routes.shape[0], D), BF16),
    )(routes, gates, *back)


STEP = 896
STEPS = D // STEP


def expert_kernel(rank_ref, x_ref, gate0, up0, gate1, up1, down0, down1, *refs):
    out_refs = refs[:-3]
    sums, hidden, result = refs[-3:]
    rows = result.shape[1]
    step = pl.program_id(0)

    @pl.when(step < STEPS)
    def _():
        x = x_ref[...]
        for index, weight_ref in enumerate((gate0, up0, gate1, up1)):
            part = jnp.dot(x, weight_ref[0], preferred_element_type=F32)
            sums[index] = jnp.where(step == 0, part, sums[index] + part)

    @pl.when(step == STEPS)
    def _():
        for half in range(2):
            value = sums[2 * half]
            hidden[half] = (value / (1.0 + jnp.exp(-value)) * sums[2 * half + 1]).astype(BF16)

    @pl.when(step >= STEPS)
    def _():
        first = jnp.dot(hidden[0], down0[0], preferred_element_type=F32).astype(BF16)
        second = jnp.dot(hidden[1], down1[0], preferred_element_type=F32).astype(BF16)
        both = (first.astype(F32) + second.astype(F32)).astype(BF16)
        for chip in range(len(out_refs)):
            result[chip] = both[chip * rows : (chip + 1) * rows]
        for offset, out_ref in enumerate(out_refs):
            out_ref[...] = result[(rank_ref[0] // 2) ^ offset]


def expert_rows(rank, x, own, other, experts):
    count = x.shape[0]
    rows = count // experts
    weights = pl.BlockSpec((1, STEP, HALF), lambda k, rank: (0, jnp.minimum(k, STEPS - 1), 0))
    down = pl.BlockSpec((1, HALF, STEP), lambda k, rank: (0, 0, jnp.maximum(k - STEPS, 0)))
    columns = pl.BlockSpec((count, STEP), lambda k, rank: (0, jnp.minimum(k, STEPS - 1)))
    return call(
        expert_kernel,
        "expert_rows",
        flops=12 * count * D * HALF,
        moved=12 * D * HALF + 4 * count * D,
        grid_spec=pltpu.PrefetchScalarGridSpec(
            num_scalar_prefetch=1,
            grid=(2 * STEPS,),
            in_specs=[columns] + [weights] * 4 + [down] * 2,
            out_specs=[pl.BlockSpec((rows, STEP), lambda k, rank: (0, jnp.maximum(k - STEPS, 0)))] * experts,
            scratch_shapes=[
                pltpu.VMEM((4, count, HALF), F32),
                pltpu.VMEM((2, count, HALF), BF16),
                pltpu.VMEM((experts, rows, STEP), BF16),
            ],
        ),
        out_shape=[jax.ShapeDtypeStruct((rows, D), BF16)] * experts,
    )(rank, x, own[0], own[1], other[0], other[1], own[2], other[2])


class Split:
    def __init__(self, groups, shards, heads):
        self.groups, self.shards = groups, shards
        self.each = heads // shards
        self.wide = groups == 2 and self.each % (2 * groups) == 0
        self.chips = shards // 2
        self.own_pairs = self.each // 2 // (groups if self.wide else 1)
        self.holders = 2 if self.wide else 1
        self.pairs = 2 * self.holders * self.own_pairs
        self.parts = groups if self.wide else 1

    def first_head(self, rank, chip, pair):
        core, rest = divmod(pair, self.holders * self.own_pairs)
        holder, own = divmod(rest, self.own_pairs)
        if not self.wide:
            return (2 * chip + ((rank & 1) ^ core)) * self.each + 2 * own
        group, low = divmod(chip, self.shards // 4)
        top = (rank & (self.shards // 2)) ^ (holder * (self.shards // 2))
        return (top + 2 * low + ((rank & 1) ^ core)) * self.each + 2 * (group * self.own_pairs + own)

    def exchange(self, array):
        half = self.shards // 2
        if self.wide:
            tops, steps = (0, half), [g * self.shards + c for g in range(self.groups) for c in range(0, half, 2)]
            sets = [[start + core + step for step in steps] for start in tops for core in range(2)]
        else:
            starts = range(0, self.groups * self.shards, self.shards)
            sets = [[start + core + c for c in range(0, self.shards, 2)] for start in starts for core in range(2)]
        return lax.all_to_all(
            array, ("groups", "ctx"), split_axis=0, concat_axis=0, axis_index_groups=sets, tiled=True
        )


def split_kernel(split, rank_ref, x_ref, out_ref):
    each = NOPE + ROPE
    for chip in range(split.chips):
        for pair in range(split.pairs):
            start = pl.multiple_of(split.first_head(rank_ref[0], chip, pair) * each, 128)
            part = x_ref[:, pl.ds(start, 2 * each)]
            out_ref[chip, :, pair * 2 * each : (pair + 1) * 2 * each] = jnp.concatenate(
                [part[:, :NOPE], part[:, each : each + NOPE], part[:, NOPE:each], part[:, each + NOPE :]], axis=1
            )


def split_queries(split, rank, queries):
    tok = queries.shape[0]
    return call(
        functools.partial(split_kernel, split),
        "split_queries",
        moved=4 * queries.size,
        in_specs=[SMEM, VMEM],
        out_specs=VMEM,
        out_shape=jax.ShapeDtypeStruct((split.chips, tok, 2 * split.pairs * (NOPE + ROPE)), BF16),
    )(rank, queries)


def join_kernel(split, rank_ref, x_ref, out_ref):
    for chip in range(split.chips):
        for pair in range(split.pairs):
            start = pl.multiple_of(split.first_head(rank_ref[0], chip, pair) * VDIM, 128)
            out_ref[:, pl.ds(start, 2 * VDIM)] = x_ref[chip, :, pair * 2 * VDIM : (pair + 1) * 2 * VDIM]


def join_values(split, rank, values):
    return call(
        functools.partial(join_kernel, split),
        "join_values",
        moved=4 * values.size,
        in_specs=[SMEM, VMEM],
        out_specs=VMEM,
        out_shape=jax.ShapeDtypeStruct((values.shape[1], HEADS * VDIM), BF16),
    )(rank, values)


BLOCK = 128
SPAN = 2 * BLOCK
EXP_SCALE = math.log2(math.e) / math.sqrt(NOPE + ROPE)


def attention_kernel(split, rank_ref, query_ref, kv_ref, other_kv_ref, *refs):
    weight_refs = refs[:-4]
    out_ref, keys, queries, mixed = refs[-4:]
    tok = kv_ref.shape[1]
    part_rows = query_ref.shape[0] // split.parts
    core = rank_ref[0] & 1

    @pl.when(pl.program_id(0) == 0)
    def _():
        for index, offset in enumerate(gather_order(split)):
            for from_ref, swapped in ((kv_ref, 0), (other_kv_ref, 1)):
                group, ctx = divmod(offset ^ swapped, split.shards)
                group = rank_ref[1] ^ group if split.wide else 0
                place = pl.ds(pl.multiple_of((rank_ref[0] ^ ctx) * tok, tok), tok)
                keys[group, place, : LATENT + ROPE] = from_ref[index]
                keys[group, place, LATENT + ROPE :] = from_ref[index, :, LATENT:]

    piece = pl.program_id(0) // split.own_pairs

    def weight(index):
        value = weight_refs[0][0, index]
        for number in range(1, len(weight_refs)):
            value = jnp.where(piece == number, weight_refs[number][0, index], value)
        return value

    contract = (((1,), (1,)), ((), ()))
    side = lax.broadcasted_iota(jnp.int32, (1, 2 * ROPE), 1) // ROPE
    for one in range(2):
        latent = lax.dot_general(
            query_ref[:, one * NOPE : (one + 1) * NOPE], weight(one), contract, preferred_element_type=F32
        )
        queries[one, :, :LATENT] = latent.astype(BF16)
        queries[one, :, LATENT:] = jnp.where(side == one, query_ref[:, 2 * NOPE :], jnp.zeros((), BF16))

    row = lax.broadcasted_iota(jnp.int32, (2 * BLOCK, SPAN), 0) % BLOCK
    position = (2 * (row // tok) + core) * tok + row % tok
    visible = lax.broadcasted_iota(jnp.int32, (2 * BLOCK, SPAN), 1) <= position

    def attend(part, block, before):
        start = before * SPAN
        first = part * part_rows + block * BLOCK
        rows = pl.ds(first, BLOCK)
        last = pl.ds(start, SPAN)
        query = jnp.concatenate([queries[0, rows, :], queries[1, rows, :]], axis=0)
        near = lax.dot_general(query, keys[part, last, :], contract, preferred_element_type=F32)
        near = jnp.where(visible, near, -1e30)
        top = jnp.max(near, axis=1, keepdims=True)
        if before:
            past = lax.dot_general(query, keys[part, :start, :], contract, preferred_element_type=F32)
            top = jnp.maximum(top, jnp.max(past, axis=1, keepdims=True))
        weights = jnp.exp2((near - top) * EXP_SCALE)
        total = jnp.sum(weights, axis=1, keepdims=True)
        summed = jnp.dot(weights.astype(BF16), keys[part, last, :LATENT], preferred_element_type=F32)
        if before:
            weights = jnp.exp2((past - top) * EXP_SCALE)
            total = total + jnp.sum(weights, axis=1, keepdims=True)
            summed = summed + jnp.dot(
                weights.astype(BF16), keys[part, :start, :LATENT], preferred_element_type=F32
            )
        result = (summed / total).astype(BF16)
        mixed[0, rows, :] = result[:BLOCK]
        mixed[1, rows, :] = result[BLOCK:]

    blocks = part_rows // BLOCK
    if split.wide:
        for half in range(2):

            @pl.when(rank_ref[0] // (split.shards // 2) == half)
            def _():
                for part in range(split.parts):
                    for block in range(blocks):
                        attend(part, block, half * blocks + block)

    else:
        for block in range(blocks):
            attend(0, block, block)

    for one in range(2):
        out_ref[:, one * VDIM : (one + 1) * VDIM] = jnp.dot(
            mixed[one], weight(2 + one), preferred_element_type=F32
        ).astype(BF16)


def attention(split, place, queries, keys, other_keys, weights):
    count = queries.shape[0]
    length = 2 * keys.shape[0] * keys.shape[1] // split.parts
    whole = pl.BlockSpec(keys.shape, lambda p, place: (0, 0, 0))
    each = split.own_pairs

    def pair_of(piece):
        return lambda p, place: (jnp.clip(p - piece * each, 0, each - 1), 0, 0, 0)

    return call(
        functools.partial(attention_kernel, split),
        "causal_attention",
        flops=4 * count * length * split.pairs * (2 * LATENT + ROPE),
        moved=4 * (queries.size + keys.size + weights[0].size * len(weights)),
        grid_spec=pltpu.PrefetchScalarGridSpec(
            num_scalar_prefetch=1,
            grid=(split.pairs,),
            in_specs=[
                pl.BlockSpec((count, 2 * (NOPE + ROPE)), lambda p, place: (0, p)),
                whole,
                whole,
            ]
            + [pl.BlockSpec((1, 4, LATENT, VDIM), pair_of(piece)) for piece in range(len(weights))],
            out_specs=pl.BlockSpec((count, 2 * VDIM), lambda p, place: (0, p)),
            scratch_shapes=[
                pltpu.VMEM((split.parts, length, LATENT + 2 * ROPE), BF16),
                pltpu.VMEM((2, count, LATENT + 2 * ROPE), BF16),
                pltpu.VMEM((2, count, LATENT), BF16),
            ],
        ),
        out_shape=jax.ShapeDtypeStruct((count, 2 * split.pairs * VDIM), BF16),
    )(place, queries, keys, other_keys, *weights)


def send(array, mask):
    count = lax.axis_size("groups") * lax.axis_size("ctx")
    return lax.ppermute(array, ("groups", "ctx"), [(i, i ^ mask) for i in range(count)])


def swap_chips(array):
    shards = lax.axis_size("ctx")
    return lax.all_to_all(
        array,
        "ctx",
        split_axis=0,
        concat_axis=0,
        axis_index_groups=[list(range(core, shards, 2)) for core in range(2)],
        tiled=True,
    )


def after(array, *others):
    return lax.optimization_barrier((array, *others))[0]


def gather_masks(split):
    top, below = split.shards // 2, split.shards // 4
    later = [1 << bit for bit in reversed(range(1, below.bit_length() - 1))]
    return [top, below, top ^ below], ([split.shards] if split.wide else []) + later


def gather_order(split):
    direct, later = gather_masks(split)
    order = [0] + direct
    for mask in later:
        order = order + [offset ^ mask for offset in order]
    return order


def on_device(
    queries,
    latent_kv,
    key_proj,
    value_proj,
    moe_input,
    routes,
    gates,
    expert_gate,
    expert_up,
    expert_down,
):
    shards = lax.axis_size("ctx")
    split = Split(lax.axis_size("groups"), shards, HEADS)
    tok = queries.shape[0]
    experts = shards // 2
    capacity = 2 * ((4 * tok * TOP + 6 * experts - 1) // (6 * experts))
    rows = -(-capacity // 8) * 8
    rank = lax.axis_index("ctx").astype(jnp.int32).reshape(1)
    group = lax.axis_index("groups").astype(jnp.int32).reshape(1)
    place = jnp.concatenate([rank, group])

    direct, later = gather_masks(split)
    keys = [latent_kv] + [send(latent_kv, offset) for offset in direct]

    buckets = after(build_buckets(routes, moe_input, experts, rows), *keys)
    arrived = swap_chips(buckets.reshape(experts, rows, D)).reshape(experts * rows, D)

    sent = split_queries(split, rank, queries)
    keys = after(jnp.stack(keys), sent)
    for mask in later:
        keys = jnp.concatenate([keys, send(keys, mask)], axis=0)
    other_keys = send(keys, 1)

    near = jnp.concatenate(
        [
            key_proj.swapaxes(1, 2).reshape(-1, 2, LATENT, NOPE),
            value_proj.reshape(-1, 2, LATENT, VDIM),
        ],
        axis=1,
    )
    if split.wide:
        near = lax.dynamic_slice_in_dim(near, group[0] * split.own_pairs, split.own_pairs, axis=0)
    near = after(near, buckets)
    other_near = send(near, 1)

    own_half = [expert_gate, expert_up, expert_down]
    other_half = [send(after(part, buckets), 1) for part in own_half]
    held = split.exchange(after(sent, other_keys, other_near, arrived, *other_half)).reshape(experts * tok, -1)
    weights = [near, other_near]
    if split.wide:
        far = send(after(near, arrived), shards // 2)

    result = expert_rows(rank, arrived, own_half, other_half, experts)
    back = [result[0]] + [send(result[m], 2 * m) for m in range(1, experts)]
    if split.wide:
        weights = [near, far, other_near, send(after(far, back[1]), 1)]
    held = after(held, back[1])
    values = attention(split, place, held, keys, other_keys, weights)
    values, *back = lax.optimization_barrier((values, *back))
    values = split.exchange(values.reshape(experts, tok, values.shape[1]))
    moe_out = combine(routes ^ (rank // 2), gates, back, rows)
    return (join_values(split, rank, values), moe_out)


def solution(mesh):
    return jax.shard_map(
        on_device,
        mesh=mesh,
        in_specs=(
            P(("groups", "ctx"), None),
            P(("groups", "ctx"), None),
            P("ctx", None, None),
            P("ctx", None, None),
            P(("groups", "ctx"), None),
            P(("groups", "ctx"), None),
            P(("groups", "ctx"), None),
            P("ctx", None, None),
            P("ctx", None, None),
            P("ctx", None, None),
        ),
        out_specs=(P(("groups", "ctx"), None), P(("groups", "ctx"), None)),
        check_vma=False,
    )
```

```python
import functools
import math

import jax
import jax.numpy as jnp
from jax import lax
from jax.experimental import pallas as pl
from jax.experimental.pallas import tpu as pltpu
from jax.sharding import PartitionSpec as P

D = 3584
HEADS = 64
NOPE = 128
ROPE = 64
LATENT = 512
VDIM = 128
TOP = 2
HALF = 512
VMEM_LIMIT = 50 * 1024 * 1024
F32 = jnp.float32
BF16 = jnp.bfloat16


SMEM = pl.BlockSpec(memory_space=pltpu.SMEM)
VMEM = pl.BlockSpec(memory_space=pltpu.VMEM)


def call(kernel, name, flops=0, moved=0, **options):
    return pl.pallas_call(
        kernel,
        name=name,
        cost_estimate=pl.CostEstimate(flops=flops, bytes_accessed=moved, transcendentals=0),
        compiler_params=pltpu.CompilerParams(vmem_limit_bytes=VMEM_LIMIT),
        **options,
    )


def slot_targets(routes, rows):
    tok = routes.shape[0]
    lane = lax.broadcasted_iota(jnp.int32, (tok, 128), 1)
    first = routes[:, 0:1]
    second = routes[:, 1:2]
    hot0 = jnp.where(lane == first, 1.0, 0.0)
    hot1 = jnp.where(lane == second, 1.0, 0.0)
    earlier = jnp.where(
        lax.broadcasted_iota(jnp.int32, (tok, tok), 1) < lax.broadcasted_iota(jnp.int32, (tok, tok), 0),
        1.0,
        0.0,
    )
    counts = jnp.dot(earlier.astype(BF16), (hot0 + hot1).astype(BF16), preferred_element_type=F32)
    slot0 = jnp.sum(counts * hot0, axis=1, keepdims=True).astype(jnp.int32)
    slot1 = jnp.sum(counts * hot1, axis=1, keepdims=True).astype(jnp.int32)
    return first * rows + slot0, second * rows + slot1


def bucket_kernel(rows, routes_ref, x_ref, out_ref):
    target0, target1 = slot_targets(routes_ref[...], rows)
    column = lax.broadcasted_iota(jnp.int32, (x_ref.shape[0], out_ref.shape[0]), 1)
    chosen = jnp.where((column == target0) | (column == target1), 1.0, 0.0).astype(BF16)
    out_ref[...] = lax.dot_general(
        chosen, x_ref[...], (((0,), (0,)), ((), ())), preferred_element_type=F32
    ).astype(BF16)


def build_buckets(routes, moe_input, experts, rows):
    return call(
        functools.partial(bucket_kernel, rows),
        "bucket_rows",
        moved=2 * D * (moe_input.shape[0] + experts * rows),
        out_shape=jax.ShapeDtypeStruct((experts * rows, D), BF16),
    )(routes, moe_input)


def combine_kernel(rows, routes_ref, gates_ref, back_ref, out_ref):
    back = back_ref[...]
    tok = routes_ref.shape[0]
    target0, target1 = slot_targets(routes_ref[...], rows)
    targets = jnp.concatenate([target0, target1], axis=0)
    column = lax.broadcasted_iota(jnp.int32, (2 * tok, back.shape[0]), 1)
    chosen = jnp.where(column == targets, 1.0, 0.0).astype(BF16)
    picked = jnp.dot(chosen, back, preferred_element_type=F32)
    out_ref[...] = (picked[:tok] * gates_ref[:, 0:1] + picked[tok:] * gates_ref[:, 1:2]).astype(BF16)


def combine(routes, gates, back, rows):
    return call(
        functools.partial(combine_kernel, rows),
        "combine_routes",
        moved=2 * D * (routes.shape[0] + back.shape[0]),
        out_shape=jax.ShapeDtypeStruct((routes.shape[0], D), BF16),
    )(routes, gates, back)


STEP = 896
STEPS = D // STEP


def expert_kernel(x_ref, gate0, up0, gate1, up1, down0, down1, out_ref, sums, hidden):
    step = pl.program_id(0)

    @pl.when(step < STEPS)
    def _():
        x = x_ref[...]
        for index, weight_ref in enumerate((gate0, up0, gate1, up1)):
            part = jnp.dot(x, weight_ref[0], preferred_element_type=F32)
            sums[index] = jnp.where(step == 0, part, sums[index] + part)

    @pl.when(step == STEPS)
    def _():
        for half in range(2):
            value = sums[2 * half]
            hidden[half] = (value / (1.0 + jnp.exp(-value)) * sums[2 * half + 1]).astype(BF16)

    @pl.when(step >= STEPS)
    def _():
        first = jnp.dot(hidden[0], down0[0], preferred_element_type=F32).astype(BF16)
        second = jnp.dot(hidden[1], down1[0], preferred_element_type=F32).astype(BF16)
        out_ref[...] = (first.astype(F32) + second.astype(F32)).astype(BF16)


def expert_rows(x, own, other):
    count = x.shape[0]
    weights = pl.BlockSpec((1, STEP, HALF), lambda k: (0, jnp.minimum(k, STEPS - 1), 0))
    down = pl.BlockSpec((1, HALF, STEP), lambda k: (0, 0, jnp.maximum(k - STEPS, 0)))
    return call(
        expert_kernel,
        "expert_rows",
        flops=12 * count * D * HALF,
        moved=12 * D * HALF + 4 * count * D,
        grid=(2 * STEPS,),
        in_specs=[pl.BlockSpec((count, STEP), lambda k: (0, jnp.minimum(k, STEPS - 1)))] + [weights] * 4 + [down] * 2,
        out_specs=pl.BlockSpec((count, STEP), lambda k: (0, jnp.maximum(k - STEPS, 0))),
        scratch_shapes=[pltpu.VMEM((4, count, HALF), F32), pltpu.VMEM((2, count, HALF), BF16)],
        out_shape=jax.ShapeDtypeStruct((count, D), BF16),
    )(x, own[0], own[1], other[0], other[1], own[2], other[2])


class Split:
    def __init__(self, groups, shards, heads):
        self.groups, self.shards = groups, shards
        self.each = heads // shards
        self.wide = groups == 2 and self.each % (2 * groups) == 0
        self.chips = shards // 2
        self.own_pairs = self.each // 2 // (groups if self.wide else 1)
        self.holders = 2 if self.wide else 1
        self.pairs = 2 * self.holders * self.own_pairs
        self.parts = groups if self.wide else 1

    def first_head(self, rank, chip, pair):
        core, rest = divmod(pair, self.holders * self.own_pairs)
        holder, own = divmod(rest, self.own_pairs)
        if not self.wide:
            return (2 * chip + ((rank & 1) ^ core)) * self.each + 2 * own
        group, low = divmod(chip, self.shards // 4)
        top = (rank & (self.shards // 2)) ^ (holder * (self.shards // 2))
        return (top + 2 * low + ((rank & 1) ^ core)) * self.each + 2 * (group * self.own_pairs + own)

    def exchange(self, array):
        half = self.shards // 2
        if self.wide:
            tops, steps = (0, half), [g * self.shards + c for g in range(self.groups) for c in range(0, half, 2)]
            sets = [[start + core + step for step in steps] for start in tops for core in range(2)]
        else:
            starts = range(0, self.groups * self.shards, self.shards)
            sets = [[start + core + c for c in range(0, self.shards, 2)] for start in starts for core in range(2)]
        return lax.all_to_all(
            array, ("groups", "ctx"), split_axis=0, concat_axis=0, axis_index_groups=sets, tiled=True
        )


def split_kernel(split, rank_ref, x_ref, out_ref):
    each = NOPE + ROPE
    for chip in range(split.chips):
        for pair in range(split.pairs):
            start = pl.multiple_of(split.first_head(rank_ref[0], chip, pair) * each, 128)
            part = x_ref[:, pl.ds(start, 2 * each)]
            out_ref[chip, :, pair * 2 * each : (pair + 1) * 2 * each] = jnp.concatenate(
                [part[:, :NOPE], part[:, each : each + NOPE], part[:, NOPE:each], part[:, each + NOPE :]], axis=1
            )


def split_queries(split, rank, queries):
    tok = queries.shape[0]
    return call(
        functools.partial(split_kernel, split),
        "split_queries",
        moved=4 * queries.size,
        in_specs=[SMEM, VMEM],
        out_specs=VMEM,
        out_shape=jax.ShapeDtypeStruct((split.chips, tok, 2 * split.pairs * (NOPE + ROPE)), BF16),
    )(rank, queries)


def join_kernel(split, rank_ref, x_ref, out_ref):
    for chip in range(split.chips):
        for pair in range(split.pairs):
            start = pl.multiple_of(split.first_head(rank_ref[0], chip, pair) * VDIM, 128)
            out_ref[:, pl.ds(start, 2 * VDIM)] = x_ref[chip, :, pair * 2 * VDIM : (pair + 1) * 2 * VDIM]


def join_values(split, rank, values):
    return call(
        functools.partial(join_kernel, split),
        "join_values",
        moved=4 * values.size,
        in_specs=[SMEM, VMEM],
        out_specs=VMEM,
        out_shape=jax.ShapeDtypeStruct((values.shape[1], HEADS * VDIM), BF16),
    )(rank, values)


BLOCK = 128
SPAN = 2 * BLOCK
EXP_SCALE = math.log2(math.e) / math.sqrt(NOPE + ROPE)


def attention_kernel(split, rank_ref, query_ref, kv_ref, other_kv_ref, *refs):
    weight_refs = refs[:-4]
    out_ref, keys, queries, mixed = refs[-4:]
    tok = kv_ref.shape[1]
    part_rows = query_ref.shape[0] // split.parts
    core = rank_ref[0] & 1

    @pl.when(pl.program_id(0) == 0)
    def _():
        for index, offset in enumerate(gather_order(split)):
            for from_ref, swapped in ((kv_ref, 0), (other_kv_ref, 1)):
                group, ctx = divmod(offset ^ swapped, split.shards)
                group = rank_ref[1] ^ group if split.wide else 0
                place = pl.ds(pl.multiple_of((rank_ref[0] ^ ctx) * tok, tok), tok)
                keys[group, place, : LATENT + ROPE] = from_ref[index]
                keys[group, place, LATENT + ROPE :] = from_ref[index, :, LATENT:]

    piece = pl.program_id(0) // split.own_pairs

    def weight(index):
        value = weight_refs[0][0, index]
        for number in range(1, len(weight_refs)):
            value = jnp.where(piece == number, weight_refs[number][0, index], value)
        return value

    contract = (((1,), (1,)), ((), ()))
    side = lax.broadcasted_iota(jnp.int32, (1, 2 * ROPE), 1) // ROPE
    for one in range(2):
        latent = lax.dot_general(
            query_ref[:, one * NOPE : (one + 1) * NOPE], weight(one), contract, preferred_element_type=F32
        )
        queries[one, :, :LATENT] = latent.astype(BF16)
        queries[one, :, LATENT:] = jnp.where(side == one, query_ref[:, 2 * NOPE :], jnp.zeros((), BF16))

    row = lax.broadcasted_iota(jnp.int32, (2 * BLOCK, SPAN), 0) % BLOCK
    position = (2 * (row // tok) + core) * tok + row % tok
    visible = lax.broadcasted_iota(jnp.int32, (2 * BLOCK, SPAN), 1) <= position

    def attend(part, block, before):
        start = before * SPAN
        first = part * part_rows + block * BLOCK
        rows = pl.ds(first, BLOCK)
        last = pl.ds(start, SPAN)
        query = jnp.concatenate([queries[0, rows, :], queries[1, rows, :]], axis=0)
        near = lax.dot_general(query, keys[part, last, :], contract, preferred_element_type=F32)
        near = jnp.where(visible, near, -1e30)
        top = jnp.max(near, axis=1, keepdims=True)
        if before:
            past = lax.dot_general(query, keys[part, :start, :], contract, preferred_element_type=F32)
            top = jnp.maximum(top, jnp.max(past, axis=1, keepdims=True))
        weights = jnp.exp2((near - top) * EXP_SCALE)
        total = jnp.sum(weights, axis=1, keepdims=True)
        summed = jnp.dot(weights.astype(BF16), keys[part, last, :LATENT], preferred_element_type=F32)
        if before:
            weights = jnp.exp2((past - top) * EXP_SCALE)
            total = total + jnp.sum(weights, axis=1, keepdims=True)
            summed = summed + jnp.dot(
                weights.astype(BF16), keys[part, :start, :LATENT], preferred_element_type=F32
            )
        result = (summed / total).astype(BF16)
        mixed[0, rows, :] = result[:BLOCK]
        mixed[1, rows, :] = result[BLOCK:]

    blocks = part_rows // BLOCK
    if split.wide:
        for half in range(2):

            @pl.when(rank_ref[0] // (split.shards // 2) == half)
            def _():
                for part in range(split.parts):
                    for block in range(blocks):
                        attend(part, block, half * blocks + block)

    else:
        for block in range(blocks):
            attend(0, block, block)

    for one in range(2):
        out_ref[:, one * VDIM : (one + 1) * VDIM] = jnp.dot(
            mixed[one], weight(2 + one), preferred_element_type=F32
        ).astype(BF16)


def attention(split, place, queries, keys, other_keys, weights):
    count = queries.shape[0]
    length = 2 * keys.shape[0] * keys.shape[1] // split.parts
    whole = pl.BlockSpec(keys.shape, lambda p, place: (0, 0, 0))
    each = split.own_pairs

    def pair_of(piece):
        return lambda p, place: (jnp.clip(p - piece * each, 0, each - 1), 0, 0, 0)

    return call(
        functools.partial(attention_kernel, split),
        "causal_attention",
        flops=4 * count * length * split.pairs * (2 * LATENT + ROPE),
        moved=4 * (queries.size + keys.size + weights[0].size * len(weights)),
        grid_spec=pltpu.PrefetchScalarGridSpec(
            num_scalar_prefetch=1,
            grid=(split.pairs,),
            in_specs=[
                pl.BlockSpec((count, 2 * (NOPE + ROPE)), lambda p, place: (0, p)),
                whole,
                whole,
            ]
            + [pl.BlockSpec((1, 4, LATENT, VDIM), pair_of(piece)) for piece in range(len(weights))],
            out_specs=pl.BlockSpec((count, 2 * VDIM), lambda p, place: (0, p)),
            scratch_shapes=[
                pltpu.VMEM((split.parts, length, LATENT + 2 * ROPE), BF16),
                pltpu.VMEM((2, count, LATENT + 2 * ROPE), BF16),
                pltpu.VMEM((2, count, LATENT), BF16),
            ],
        ),
        out_shape=jax.ShapeDtypeStruct((count, 2 * split.pairs * VDIM), BF16),
    )(place, queries, keys, other_keys, *weights)


def send(array, mask):
    count = lax.axis_size("groups") * lax.axis_size("ctx")
    return lax.ppermute(array, ("groups", "ctx"), [(i, i ^ mask) for i in range(count)])


def swap_chips(array):
    shards = lax.axis_size("ctx")
    return lax.all_to_all(
        array,
        "ctx",
        split_axis=0,
        concat_axis=0,
        axis_index_groups=[list(range(core, shards, 2)) for core in range(2)],
        tiled=True,
    )


def after(array, *others):
    return lax.optimization_barrier((array, *others))[0]


def gather_masks(split):
    top, below = split.shards // 2, split.shards // 4
    later = [1 << bit for bit in reversed(range(1, below.bit_length() - 1))]
    return [top, below, top ^ below], ([split.shards] if split.wide else []) + later


def gather_order(split):
    direct, later = gather_masks(split)
    order = [0] + direct
    for mask in later:
        order = order + [offset ^ mask for offset in order]
    return order


def on_device(
    queries,
    latent_kv,
    key_proj,
    value_proj,
    moe_input,
    routes,
    gates,
    expert_gate,
    expert_up,
    expert_down,
):
    shards = lax.axis_size("ctx")
    split = Split(lax.axis_size("groups"), shards, HEADS)
    tok = queries.shape[0]
    experts = shards // 2
    capacity = 2 * ((4 * tok * TOP + 6 * experts - 1) // (6 * experts))
    rows = -(-capacity // 8) * 8
    rank = lax.axis_index("ctx").astype(jnp.int32).reshape(1)
    group = lax.axis_index("groups").astype(jnp.int32).reshape(1)
    place = jnp.concatenate([rank, group])

    near = jnp.concatenate(
        [
            key_proj.swapaxes(1, 2).reshape(-1, 2, LATENT, NOPE),
            value_proj.reshape(-1, 2, LATENT, VDIM),
        ],
        axis=1,
    )
    if split.wide:
        near = lax.dynamic_slice_in_dim(near, group[0] * split.own_pairs, split.own_pairs, axis=0)

    direct, later = gather_masks(split)
    keys = [latent_kv] + [send(latent_kv, offset) for offset in direct]
    held = split.exchange(split_queries(split, rank, queries)).reshape(experts * tok, -1)
    pieces = [near, send(near, shards // 2)] if split.wide else [near]
    own_half = [expert_gate, expert_up, expert_down]
    other_half = [send(after(part, *keys), 1) for part in own_half]
    keys = jnp.stack(keys)
    for mask in later:
        keys = jnp.concatenate([keys, send(keys, mask)], axis=0)

    buckets = after(build_buckets(routes, moe_input, experts, rows), held, keys, *pieces)
    arrived = swap_chips(buckets.reshape(experts, rows, D)).reshape(experts * rows, D)

    weights = pieces + [send(piece, 1) for piece in pieces]
    values = attention(split, place, held, keys, send(keys, 1), weights)
    values = after(values, arrived)
    values = split.exchange(values.reshape(experts, tok, values.shape[1]))

    result = after(expert_rows(arrived, own_half, other_half), values)
    back = swap_chips(result.reshape(experts, rows, D))
    moe_out = combine(routes, gates, back.reshape(experts * rows, D), rows)
    return (join_values(split, rank, values), moe_out)


def solution(mesh):
    return jax.shard_map(
        on_device,
        mesh=mesh,
        in_specs=(
            P(("groups", "ctx"), None),
            P(("groups", "ctx"), None),
            P("ctx", None, None),
            P("ctx", None, None),
            P(("groups", "ctx"), None),
            P(("groups", "ctx"), None),
            P(("groups", "ctx"), None),
            P("ctx", None, None),
            P("ctx", None, None),
            P("ctx", None, None),
        ),
        out_specs=(P(("groups", "ctx"), None), P(("groups", "ctx"), None)),
        check_vma=False,
    )
```

```python
import functools
import math

import jax
import jax.numpy as jnp
from jax import lax
from jax.experimental import pallas as pl
from jax.experimental.pallas import tpu as pltpu
from jax.sharding import PartitionSpec as P

D = 3584
HEADS = 64
NOPE = 128
ROPE = 64
LATENT = 512
VDIM = 128
TOP = 2
HALF = 512
VMEM_LIMIT = 50 * 1024 * 1024
F32 = jnp.float32
BF16 = jnp.bfloat16


SMEM = pl.BlockSpec(memory_space=pltpu.SMEM)
VMEM = pl.BlockSpec(memory_space=pltpu.VMEM)


def call(kernel, name, flops=0, moved=0, **options):
    return pl.pallas_call(
        kernel,
        name=name,
        cost_estimate=pl.CostEstimate(flops=flops, bytes_accessed=moved, transcendentals=0),
        compiler_params=pltpu.CompilerParams(vmem_limit_bytes=VMEM_LIMIT),
        **options,
    )


def slot_targets(routes, rows):
    tok = routes.shape[0]
    lane = lax.broadcasted_iota(jnp.int32, (tok, 128), 1)
    first = routes[:, 0:1]
    second = routes[:, 1:2]
    hot0 = jnp.where(lane == first, 1.0, 0.0)
    hot1 = jnp.where(lane == second, 1.0, 0.0)
    earlier = jnp.where(
        lax.broadcasted_iota(jnp.int32, (tok, tok), 1) < lax.broadcasted_iota(jnp.int32, (tok, tok), 0),
        1.0,
        0.0,
    )
    counts = jnp.dot(earlier.astype(BF16), (hot0 + hot1).astype(BF16), preferred_element_type=F32)
    slot0 = jnp.sum(counts * hot0, axis=1, keepdims=True).astype(jnp.int32)
    slot1 = jnp.sum(counts * hot1, axis=1, keepdims=True).astype(jnp.int32)
    return first * rows + slot0, second * rows + slot1


def bucket_kernel(rows, routes_ref, x_ref, out_ref):
    target0, target1 = slot_targets(routes_ref[...], rows)
    column = lax.broadcasted_iota(jnp.int32, (x_ref.shape[0], out_ref.shape[0]), 1)
    chosen = jnp.where((column == target0) | (column == target1), 1.0, 0.0).astype(BF16)
    out_ref[...] = lax.dot_general(
        chosen, x_ref[...], (((0,), (0,)), ((), ())), preferred_element_type=F32
    ).astype(BF16)


def build_buckets(routes, moe_input, experts, rows):
    return call(
        functools.partial(bucket_kernel, rows),
        "bucket_rows",
        moved=2 * D * (moe_input.shape[0] + experts * rows),
        out_shape=jax.ShapeDtypeStruct((experts * rows, D), BF16),
    )(routes, moe_input)


def combine_kernel(rows, routes_ref, gates_ref, back_ref, out_ref):
    back = back_ref[...]
    tok = routes_ref.shape[0]
    target0, target1 = slot_targets(routes_ref[...], rows)
    targets = jnp.concatenate([target0, target1], axis=0)
    column = lax.broadcasted_iota(jnp.int32, (2 * tok, back.shape[0]), 1)
    chosen = jnp.where(column == targets, 1.0, 0.0).astype(BF16)
    picked = jnp.dot(chosen, back, preferred_element_type=F32)
    out_ref[...] = (picked[:tok] * gates_ref[:, 0:1] + picked[tok:] * gates_ref[:, 1:2]).astype(BF16)


def combine(routes, gates, back, rows):
    return call(
        functools.partial(combine_kernel, rows),
        "combine_routes",
        moved=2 * D * (routes.shape[0] + back.shape[0]),
        out_shape=jax.ShapeDtypeStruct((routes.shape[0], D), BF16),
    )(routes, gates, back)


STEP = 896
STEPS = D // STEP


def expert_kernel(x_ref, gate0, up0, gate1, up1, down0, down1, out_ref, sums, hidden):
    step = pl.program_id(0)

    @pl.when(step < STEPS)
    def _():
        x = x_ref[...]
        for index, weight_ref in enumerate((gate0, up0, gate1, up1)):
            part = jnp.dot(x, weight_ref[0], preferred_element_type=F32)
            sums[index] = jnp.where(step == 0, part, sums[index] + part)

    @pl.when(step == STEPS)
    def _():
        for half in range(2):
            value = sums[2 * half]
            hidden[half] = (value / (1.0 + jnp.exp(-value)) * sums[2 * half + 1]).astype(BF16)

    @pl.when(step >= STEPS)
    def _():
        first = jnp.dot(hidden[0], down0[0], preferred_element_type=F32).astype(BF16)
        second = jnp.dot(hidden[1], down1[0], preferred_element_type=F32).astype(BF16)
        out_ref[...] = (first.astype(F32) + second.astype(F32)).astype(BF16)


def expert_rows(x, own, other):
    count = x.shape[0]
    weights = pl.BlockSpec((1, STEP, HALF), lambda k: (0, jnp.minimum(k, STEPS - 1), 0))
    down = pl.BlockSpec((1, HALF, STEP), lambda k: (0, 0, jnp.maximum(k - STEPS, 0)))
    return call(
        expert_kernel,
        "expert_rows",
        flops=12 * count * D * HALF,
        moved=12 * D * HALF + 4 * count * D,
        grid=(2 * STEPS,),
        in_specs=[pl.BlockSpec((count, STEP), lambda k: (0, jnp.minimum(k, STEPS - 1)))] + [weights] * 4 + [down] * 2,
        out_specs=pl.BlockSpec((count, STEP), lambda k: (0, jnp.maximum(k - STEPS, 0))),
        scratch_shapes=[pltpu.VMEM((4, count, HALF), F32), pltpu.VMEM((2, count, HALF), BF16)],
        out_shape=jax.ShapeDtypeStruct((count, D), BF16),
    )(x, own[0], own[1], other[0], other[1], own[2], other[2])


class Split:
    def __init__(self, groups, shards, heads):
        self.groups, self.shards = groups, shards
        self.each = heads // shards
        self.wide = groups == 2 and self.each % (2 * groups) == 0
        self.chips = shards // 2
        self.own_pairs = self.each // 2 // (groups if self.wide else 1)
        self.holders = 2 if self.wide else 1
        self.pairs = 2 * self.holders * self.own_pairs
        self.parts = groups if self.wide else 1

    def first_head(self, rank, chip, pair):
        core, rest = divmod(pair, self.holders * self.own_pairs)
        holder, own = divmod(rest, self.own_pairs)
        if not self.wide:
            return (2 * chip + ((rank & 1) ^ core)) * self.each + 2 * own
        group, low = divmod(chip, self.shards // 4)
        top = (rank & (self.shards // 2)) ^ (holder * (self.shards // 2))
        return (top + 2 * low + ((rank & 1) ^ core)) * self.each + 2 * (group * self.own_pairs + own)

    def exchange(self, array):
        half = self.shards // 2
        if self.wide:
            tops, steps = (0, half), [g * self.shards + c for g in range(self.groups) for c in range(0, half, 2)]
            sets = [[start + core + step for step in steps] for start in tops for core in range(2)]
        else:
            starts = range(0, self.groups * self.shards, self.shards)
            sets = [[start + core + c for c in range(0, self.shards, 2)] for start in starts for core in range(2)]
        return lax.all_to_all(
            array, ("groups", "ctx"), split_axis=0, concat_axis=0, axis_index_groups=sets, tiled=True
        )


def split_kernel(split, rank_ref, x_ref, out_ref):
    each = NOPE + ROPE
    for chip in range(split.chips):
        for pair in range(split.pairs):
            start = pl.multiple_of(split.first_head(rank_ref[0], chip, pair) * each, 128)
            part = x_ref[:, pl.ds(start, 2 * each)]
            out_ref[chip, :, pair * 2 * each : (pair + 1) * 2 * each] = jnp.concatenate(
                [part[:, :NOPE], part[:, each : each + NOPE], part[:, NOPE:each], part[:, each + NOPE :]], axis=1
            )


def split_queries(split, rank, queries):
    tok = queries.shape[0]
    return call(
        functools.partial(split_kernel, split),
        "split_queries",
        moved=4 * queries.size,
        in_specs=[SMEM, VMEM],
        out_specs=VMEM,
        out_shape=jax.ShapeDtypeStruct((split.chips, tok, 2 * split.pairs * (NOPE + ROPE)), BF16),
    )(rank, queries)


def join_kernel(split, rank_ref, x_ref, out_ref):
    for chip in range(split.chips):
        for pair in range(split.pairs):
            start = pl.multiple_of(split.first_head(rank_ref[0], chip, pair) * VDIM, 128)
            out_ref[:, pl.ds(start, 2 * VDIM)] = x_ref[chip, :, pair * 2 * VDIM : (pair + 1) * 2 * VDIM]


def join_values(split, rank, values):
    return call(
        functools.partial(join_kernel, split),
        "join_values",
        moved=4 * values.size,
        in_specs=[SMEM, VMEM],
        out_specs=VMEM,
        out_shape=jax.ShapeDtypeStruct((values.shape[1], HEADS * VDIM), BF16),
    )(rank, values)


BLOCK = 128
SPAN = 2 * BLOCK
EXP_SCALE = math.log2(math.e) / math.sqrt(NOPE + ROPE)


def attention_kernel(split, rank_ref, query_ref, kv_ref, other_kv_ref, *refs):
    weight_refs = refs[:-4]
    out_ref, keys, queries, mixed = refs[-4:]
    tok = kv_ref.shape[1]
    part_rows = query_ref.shape[0] // split.parts
    core = rank_ref[0] & 1

    @pl.when(pl.program_id(0) == 0)
    def _():
        for index, offset in enumerate(gather_order(split)):
            for from_ref, swapped in ((kv_ref, 0), (other_kv_ref, 1)):
                group, ctx = divmod(offset ^ swapped, split.shards)
                group = rank_ref[1] ^ group if split.wide else 0
                place = pl.ds(pl.multiple_of((rank_ref[0] ^ ctx) * tok, tok), tok)
                keys[group, place, : LATENT + ROPE] = from_ref[index]
                keys[group, place, LATENT + ROPE :] = from_ref[index, :, LATENT:]

    piece = pl.program_id(0) // split.own_pairs

    def weight(index):
        value = weight_refs[0][0, index]
        for number in range(1, len(weight_refs)):
            value = jnp.where(piece == number, weight_refs[number][0, index], value)
        return value

    contract = (((1,), (1,)), ((), ()))
    side = lax.broadcasted_iota(jnp.int32, (1, 2 * ROPE), 1) // ROPE
    for one in range(2):
        latent = lax.dot_general(
            query_ref[:, one * NOPE : (one + 1) * NOPE], weight(one), contract, preferred_element_type=F32
        )
        queries[one, :, :LATENT] = latent.astype(BF16)
        queries[one, :, LATENT:] = jnp.where(side == one, query_ref[:, 2 * NOPE :], jnp.zeros((), BF16))

    row = lax.broadcasted_iota(jnp.int32, (2 * BLOCK, SPAN), 0) % BLOCK
    position = (2 * (row // tok) + core) * tok + row % tok
    visible = lax.broadcasted_iota(jnp.int32, (2 * BLOCK, SPAN), 1) <= position

    def attend(part, block, before):
        start = before * SPAN
        first = part * part_rows + block * BLOCK
        rows = pl.ds(first, BLOCK)
        last = pl.ds(start, SPAN)
        query = jnp.concatenate([queries[0, rows, :], queries[1, rows, :]], axis=0)
        near = lax.dot_general(query, keys[part, last, :], contract, preferred_element_type=F32)
        near = jnp.where(visible, near, -1e30)
        top = jnp.max(near, axis=1, keepdims=True)
        if before:
            past = lax.dot_general(query, keys[part, :start, :], contract, preferred_element_type=F32)
            top = jnp.maximum(top, jnp.max(past, axis=1, keepdims=True))
        weights = jnp.exp2((near - top) * EXP_SCALE)
        total = jnp.sum(weights, axis=1, keepdims=True)
        summed = jnp.dot(weights.astype(BF16), keys[part, last, :LATENT], preferred_element_type=F32)
        if before:
            weights = jnp.exp2((past - top) * EXP_SCALE)
            total = total + jnp.sum(weights, axis=1, keepdims=True)
            summed = summed + jnp.dot(
                weights.astype(BF16), keys[part, :start, :LATENT], preferred_element_type=F32
            )
        result = (summed / total).astype(BF16)
        mixed[0, rows, :] = result[:BLOCK]
        mixed[1, rows, :] = result[BLOCK:]

    blocks = part_rows // BLOCK
    if split.wide:
        for half in range(2):

            @pl.when(rank_ref[0] // (split.shards // 2) == half)
            def _():
                for part in range(split.parts):
                    for block in range(blocks):
                        attend(part, block, half * blocks + block)

    else:
        for block in range(blocks):
            attend(0, block, block)

    for one in range(2):
        out_ref[:, one * VDIM : (one + 1) * VDIM] = jnp.dot(
            mixed[one], weight(2 + one), preferred_element_type=F32
        ).astype(BF16)


def attention(split, place, queries, keys, other_keys, weights):
    count = queries.shape[0]
    length = 2 * keys.shape[0] * keys.shape[1] // split.parts
    whole = pl.BlockSpec(keys.shape, lambda p, place: (0, 0, 0))
    each = split.own_pairs

    def pair_of(piece):
        return lambda p, place: (jnp.clip(p - piece * each, 0, each - 1), 0, 0, 0)

    return call(
        functools.partial(attention_kernel, split),
        "causal_attention",
        flops=4 * count * length * split.pairs * (2 * LATENT + ROPE),
        moved=4 * (queries.size + keys.size + weights[0].size * len(weights)),
        grid_spec=pltpu.PrefetchScalarGridSpec(
            num_scalar_prefetch=1,
            grid=(split.pairs,),
            in_specs=[
                pl.BlockSpec((count, 2 * (NOPE + ROPE)), lambda p, place: (0, p)),
                whole,
                whole,
            ]
            + [pl.BlockSpec((1, 4, LATENT, VDIM), pair_of(piece)) for piece in range(len(weights))],
            out_specs=pl.BlockSpec((count, 2 * VDIM), lambda p, place: (0, p)),
            scratch_shapes=[
                pltpu.VMEM((split.parts, length, LATENT + 2 * ROPE), BF16),
                pltpu.VMEM((2, count, LATENT + 2 * ROPE), BF16),
                pltpu.VMEM((2, count, LATENT), BF16),
            ],
        ),
        out_shape=jax.ShapeDtypeStruct((count, 2 * split.pairs * VDIM), BF16),
    )(place, queries, keys, other_keys, *weights)


def send(array, mask):
    count = lax.axis_size("groups") * lax.axis_size("ctx")
    return lax.ppermute(array, ("groups", "ctx"), [(i, i ^ mask) for i in range(count)])


def swap_chips(array):
    shards = lax.axis_size("ctx")
    return lax.all_to_all(
        array,
        "ctx",
        split_axis=0,
        concat_axis=0,
        axis_index_groups=[list(range(core, shards, 2)) for core in range(2)],
        tiled=True,
    )


def after(array, *others):
    return lax.optimization_barrier((array, *others))[0]


def gather_masks(split):
    top, below = split.shards // 2, split.shards // 4
    later = [1 << bit for bit in reversed(range(1, below.bit_length() - 1))]
    return [top, below, top ^ below], ([split.shards] if split.wide else []) + later


def gather_order(split):
    direct, later = gather_masks(split)
    order = [0] + direct
    for mask in later:
        order = order + [offset ^ mask for offset in order]
    return order


def on_device(
    queries,
    latent_kv,
    key_proj,
    value_proj,
    moe_input,
    routes,
    gates,
    expert_gate,
    expert_up,
    expert_down,
):
    shards = lax.axis_size("ctx")
    split = Split(lax.axis_size("groups"), shards, HEADS)
    tok = queries.shape[0]
    experts = shards // 2
    capacity = 2 * ((4 * tok * TOP + 6 * experts - 1) // (6 * experts))
    rows = -(-capacity // 8) * 8
    rank = lax.axis_index("ctx").astype(jnp.int32).reshape(1)
    group = lax.axis_index("groups").astype(jnp.int32).reshape(1)
    place = jnp.concatenate([rank, group])

    direct, later = gather_masks(split)
    keys = [latent_kv] + [send(latent_kv, offset) for offset in direct]

    buckets = after(build_buckets(routes, moe_input, experts, rows), *keys)
    arrived = swap_chips(buckets.reshape(experts, rows, D)).reshape(experts * rows, D)

    sent = split_queries(split, rank, queries)
    keys = after(jnp.stack(keys), sent)
    for mask in later:
        keys = jnp.concatenate([keys, send(keys, mask)], axis=0)
    other_keys = send(keys, 1)

    near = jnp.concatenate(
        [
            key_proj.swapaxes(1, 2).reshape(-1, 2, LATENT, NOPE),
            value_proj.reshape(-1, 2, LATENT, VDIM),
        ],
        axis=1,
    )
    if split.wide:
        near = lax.dynamic_slice_in_dim(near, group[0] * split.own_pairs, split.own_pairs, axis=0)
    near = after(near, buckets)

    own_half = [expert_gate, expert_up, expert_down]
    other_half = [send(after(part, buckets), 1) for part in own_half]
    held = split.exchange(after(sent, near, arrived, *other_half)).reshape(experts * tok, -1)
    pieces = [near, send(after(near, arrived), shards // 2)] if split.wide else [near]

    result = expert_rows(arrived, own_half, other_half)
    weights = pieces + [send(after(piece, result), 1) for piece in pieces]
    result, held, keys, other_keys = lax.optimization_barrier((result, held, keys, other_keys))
    back = swap_chips(result.reshape(experts, rows, D))
    values = attention(split, place, held, keys, other_keys, weights)
    values, back = lax.optimization_barrier((values, back))
    values = split.exchange(values.reshape(experts, tok, values.shape[1]))
    moe_out = combine(routes, gates, back.reshape(experts * rows, D), rows)
    return (join_values(split, rank, values), moe_out)


def solution(mesh):
    return jax.shard_map(
        on_device,
        mesh=mesh,
        in_specs=(
            P(("groups", "ctx"), None),
            P(("groups", "ctx"), None),
            P("ctx", None, None),
            P("ctx", None, None),
            P(("groups", "ctx"), None),
            P(("groups", "ctx"), None),
            P(("groups", "ctx"), None),
            P("ctx", None, None),
            P("ctx", None, None),
            P("ctx", None, None),
        ),
        out_specs=(P(("groups", "ctx"), None), P(("groups", "ctx"), None)),
        check_vma=False,
    )
```

```python
import functools
import math

import jax
import jax.numpy as jnp
from jax import lax
from jax.experimental import pallas as pl
from jax.experimental.pallas import tpu as pltpu
from jax.sharding import PartitionSpec as P

D = 3584
HEADS = 64
NOPE = 128
ROPE = 64
LATENT = 512
VDIM = 128
TOP = 2
HALF = 512
VMEM_LIMIT = 50 * 1024 * 1024
F32 = jnp.float32
BF16 = jnp.bfloat16


SMEM = pl.BlockSpec(memory_space=pltpu.SMEM)
VMEM = pl.BlockSpec(memory_space=pltpu.VMEM)


def call(kernel, name, flops=0, moved=0, **options):
    return pl.pallas_call(
        kernel,
        name=name,
        cost_estimate=pl.CostEstimate(flops=flops, bytes_accessed=moved, transcendentals=0),
        compiler_params=pltpu.CompilerParams(vmem_limit_bytes=VMEM_LIMIT),
        **options,
    )


def slot_targets(routes, rows):
    tok = routes.shape[0]
    lane = lax.broadcasted_iota(jnp.int32, (tok, 128), 1)
    first = routes[:, 0:1]
    second = routes[:, 1:2]
    hot0 = jnp.where(lane == first, 1.0, 0.0)
    hot1 = jnp.where(lane == second, 1.0, 0.0)
    earlier = jnp.where(
        lax.broadcasted_iota(jnp.int32, (tok, tok), 1) < lax.broadcasted_iota(jnp.int32, (tok, tok), 0),
        1.0,
        0.0,
    )
    counts = jnp.dot(earlier.astype(BF16), (hot0 + hot1).astype(BF16), preferred_element_type=F32)
    slot0 = jnp.sum(counts * hot0, axis=1, keepdims=True).astype(jnp.int32)
    slot1 = jnp.sum(counts * hot1, axis=1, keepdims=True).astype(jnp.int32)
    return first * rows + slot0, second * rows + slot1


def bucket_kernel(rows, routes_ref, x_ref, out_ref):
    target0, target1 = slot_targets(routes_ref[...], rows)
    column = lax.broadcasted_iota(jnp.int32, (x_ref.shape[0], out_ref.shape[0]), 1)
    chosen = jnp.where((column == target0) | (column == target1), 1.0, 0.0).astype(BF16)
    out_ref[...] = lax.dot_general(
        chosen, x_ref[...], (((0,), (0,)), ((), ())), preferred_element_type=F32
    ).astype(BF16)


def build_buckets(routes, moe_input, experts, rows):
    return call(
        functools.partial(bucket_kernel, rows),
        "bucket_rows",
        moved=2 * D * (moe_input.shape[0] + experts * rows),
        out_shape=jax.ShapeDtypeStruct((experts * rows, D), BF16),
    )(routes, moe_input)


def combine_kernel(rows, routes_ref, gates_ref, back_ref, out_ref):
    back = back_ref[...]
    tok = routes_ref.shape[0]
    target0, target1 = slot_targets(routes_ref[...], rows)
    targets = jnp.concatenate([target0, target1], axis=0)
    column = lax.broadcasted_iota(jnp.int32, (2 * tok, back.shape[0]), 1)
    chosen = jnp.where(column == targets, 1.0, 0.0).astype(BF16)
    picked = jnp.dot(chosen, back, preferred_element_type=F32)
    out_ref[...] = (picked[:tok] * gates_ref[:, 0:1] + picked[tok:] * gates_ref[:, 1:2]).astype(BF16)


def combine(routes, gates, back, rows):
    return call(
        functools.partial(combine_kernel, rows),
        "combine_routes",
        moved=2 * D * (routes.shape[0] + back.shape[0]),
        out_shape=jax.ShapeDtypeStruct((routes.shape[0], D), BF16),
    )(routes, gates, back)


STEP = 896
STEPS = D // STEP


def expert_kernel(x_ref, gate0, up0, gate1, up1, down0, down1, out_ref, sums, hidden):
    step = pl.program_id(0)

    @pl.when(step < STEPS)
    def _():
        x = x_ref[...]
        for index, weight_ref in enumerate((gate0, up0, gate1, up1)):
            part = jnp.dot(x, weight_ref[0], preferred_element_type=F32)
            sums[index] = jnp.where(step == 0, part, sums[index] + part)

    @pl.when(step == STEPS)
    def _():
        for half in range(2):
            value = sums[2 * half]
            hidden[half] = (value / (1.0 + jnp.exp(-value)) * sums[2 * half + 1]).astype(BF16)

    @pl.when(step >= STEPS)
    def _():
        first = jnp.dot(hidden[0], down0[0], preferred_element_type=F32).astype(BF16)
        second = jnp.dot(hidden[1], down1[0], preferred_element_type=F32).astype(BF16)
        out_ref[...] = (first.astype(F32) + second.astype(F32)).astype(BF16)


def expert_rows(x, own, other):
    count = x.shape[0]
    weights = pl.BlockSpec((1, STEP, HALF), lambda k: (0, jnp.minimum(k, STEPS - 1), 0))
    down = pl.BlockSpec((1, HALF, STEP), lambda k: (0, 0, jnp.maximum(k - STEPS, 0)))
    return call(
        expert_kernel,
        "expert_rows",
        flops=12 * count * D * HALF,
        moved=12 * D * HALF + 4 * count * D,
        grid=(2 * STEPS,),
        in_specs=[pl.BlockSpec((count, STEP), lambda k: (0, jnp.minimum(k, STEPS - 1)))] + [weights] * 4 + [down] * 2,
        out_specs=pl.BlockSpec((count, STEP), lambda k: (0, jnp.maximum(k - STEPS, 0))),
        scratch_shapes=[pltpu.VMEM((4, count, HALF), F32), pltpu.VMEM((2, count, HALF), BF16)],
        out_shape=jax.ShapeDtypeStruct((count, D), BF16),
    )(x, own[0], own[1], other[0], other[1], own[2], other[2])


class Split:
    def __init__(self, groups, shards, heads):
        self.groups, self.shards = groups, shards
        self.each = heads // shards
        self.wide = groups == 2 and self.each % (2 * groups) == 0
        self.chips = shards // 2
        self.own_pairs = self.each // 2 // (groups if self.wide else 1)
        self.holders = 2 if self.wide else 1
        self.pairs = 2 * self.holders * self.own_pairs
        self.parts = groups if self.wide else 1

    def first_head(self, rank, chip, pair):
        core, rest = divmod(pair, self.holders * self.own_pairs)
        holder, own = divmod(rest, self.own_pairs)
        if not self.wide:
            return (2 * chip + ((rank & 1) ^ core)) * self.each + 2 * own
        group, low = divmod(chip, self.shards // 4)
        top = (rank & (self.shards // 2)) ^ (holder * (self.shards // 2))
        return (top + 2 * low + ((rank & 1) ^ core)) * self.each + 2 * (group * self.own_pairs + own)

    def exchange(self, array):
        half = self.shards // 2
        if self.wide:
            tops, steps = (0, half), [g * self.shards + c for g in range(self.groups) for c in range(0, half, 2)]
            sets = [[start + core + step for step in steps] for start in tops for core in range(2)]
        else:
            starts = range(0, self.groups * self.shards, self.shards)
            sets = [[start + core + c for c in range(0, self.shards, 2)] for start in starts for core in range(2)]
        return lax.all_to_all(
            array, ("groups", "ctx"), split_axis=0, concat_axis=0, axis_index_groups=sets, tiled=True
        )


def split_kernel(split, rank_ref, x_ref, out_ref):
    each = NOPE + ROPE
    for chip in range(split.chips):
        for pair in range(split.pairs):
            start = pl.multiple_of(split.first_head(rank_ref[0], chip, pair) * each, 128)
            part = x_ref[:, pl.ds(start, 2 * each)]
            out_ref[chip, :, pair * 2 * each : (pair + 1) * 2 * each] = jnp.concatenate(
                [part[:, :NOPE], part[:, each : each + NOPE], part[:, NOPE:each], part[:, each + NOPE :]], axis=1
            )


def split_queries(split, rank, queries):
    tok = queries.shape[0]
    return call(
        functools.partial(split_kernel, split),
        "split_queries",
        moved=4 * queries.size,
        in_specs=[SMEM, VMEM],
        out_specs=VMEM,
        out_shape=jax.ShapeDtypeStruct((split.chips, tok, 2 * split.pairs * (NOPE + ROPE)), BF16),
    )(rank, queries)


def join_kernel(split, rank_ref, x_ref, out_ref):
    for chip in range(split.chips):
        for pair in range(split.pairs):
            start = pl.multiple_of(split.first_head(rank_ref[0], chip, pair) * VDIM, 128)
            out_ref[:, pl.ds(start, 2 * VDIM)] = x_ref[chip, :, pair * 2 * VDIM : (pair + 1) * 2 * VDIM]


def join_values(split, rank, values):
    return call(
        functools.partial(join_kernel, split),
        "join_values",
        moved=4 * values.size,
        in_specs=[SMEM, VMEM],
        out_specs=VMEM,
        out_shape=jax.ShapeDtypeStruct((values.shape[1], HEADS * VDIM), BF16),
    )(rank, values)


BLOCK = 128
SPAN = 2 * BLOCK
EXP_SCALE = math.log2(math.e) / math.sqrt(NOPE + ROPE)


def attention_kernel(split, rank_ref, query_ref, kv_ref, other_kv_ref, *refs):
    weight_refs = refs[:-4]
    out_ref, keys, queries, mixed = refs[-4:]
    tok = kv_ref.shape[1]
    part_rows = query_ref.shape[0] // split.parts
    core = rank_ref[0] & 1

    @pl.when(pl.program_id(0) == 0)
    def _():
        for index, offset in enumerate(gather_order(split)):
            for from_ref, swapped in ((kv_ref, 0), (other_kv_ref, 1)):
                group, ctx = divmod(offset ^ swapped, split.shards)
                group = rank_ref[1] ^ group if split.wide else 0
                place = pl.ds(pl.multiple_of((rank_ref[0] ^ ctx) * tok, tok), tok)
                keys[group, place, : LATENT + ROPE] = from_ref[index]
                keys[group, place, LATENT + ROPE :] = from_ref[index, :, LATENT:]

    piece = pl.program_id(0) // split.own_pairs

    def weight(index):
        value = weight_refs[0][0, index]
        for number in range(1, len(weight_refs)):
            value = jnp.where(piece == number, weight_refs[number][0, index], value)
        return value

    contract = (((1,), (1,)), ((), ()))
    side = lax.broadcasted_iota(jnp.int32, (1, 2 * ROPE), 1) // ROPE
    for one in range(2):
        latent = lax.dot_general(
            query_ref[:, one * NOPE : (one + 1) * NOPE], weight(one), contract, preferred_element_type=F32
        )
        queries[one, :, :LATENT] = latent.astype(BF16)
        queries[one, :, LATENT:] = jnp.where(side == one, query_ref[:, 2 * NOPE :], jnp.zeros((), BF16))

    row = lax.broadcasted_iota(jnp.int32, (2 * BLOCK, SPAN), 0) % BLOCK
    position = (2 * (row // tok) + core) * tok + row % tok
    visible = lax.broadcasted_iota(jnp.int32, (2 * BLOCK, SPAN), 1) <= position

    def attend(part, block, before):
        start = before * SPAN
        first = part * part_rows + block * BLOCK
        rows = pl.ds(first, BLOCK)
        last = pl.ds(start, SPAN)
        query = jnp.concatenate([queries[0, rows, :], queries[1, rows, :]], axis=0)
        near = lax.dot_general(query, keys[part, last, :], contract, preferred_element_type=F32)
        near = jnp.where(visible, near, -1e30)
        top = jnp.max(near, axis=1, keepdims=True)
        if before:
            past = lax.dot_general(query, keys[part, :start, :], contract, preferred_element_type=F32)
            top = jnp.maximum(top, jnp.max(past, axis=1, keepdims=True))
        weights = jnp.exp2((near - top) * EXP_SCALE)
        total = jnp.sum(weights, axis=1, keepdims=True)
        summed = jnp.dot(weights.astype(BF16), keys[part, last, :LATENT], preferred_element_type=F32)
        if before:
            weights = jnp.exp2((past - top) * EXP_SCALE)
            total = total + jnp.sum(weights, axis=1, keepdims=True)
            summed = summed + jnp.dot(
                weights.astype(BF16), keys[part, :start, :LATENT], preferred_element_type=F32
            )
        result = (summed / total).astype(BF16)
        mixed[0, rows, :] = result[:BLOCK]
        mixed[1, rows, :] = result[BLOCK:]

    blocks = part_rows // BLOCK
    if split.wide:
        for half in range(2):

            @pl.when(rank_ref[0] // (split.shards // 2) == half)
            def _():
                for part in range(split.parts):
                    for block in range(blocks):
                        attend(part, block, half * blocks + block)

    else:
        for block in range(blocks):
            attend(0, block, block)

    for one in range(2):
        out_ref[:, one * VDIM : (one + 1) * VDIM] = jnp.dot(
            mixed[one], weight(2 + one), preferred_element_type=F32
        ).astype(BF16)


def attention(split, place, queries, keys, other_keys, weights):
    count = queries.shape[0]
    length = 2 * keys.shape[0] * keys.shape[1] // split.parts
    whole = pl.BlockSpec(keys.shape, lambda p, place: (0, 0, 0))
    each = split.own_pairs

    def pair_of(piece):
        return lambda p, place: (jnp.clip(p - piece * each, 0, each - 1), 0, 0, 0)

    return call(
        functools.partial(attention_kernel, split),
        "causal_attention",
        flops=4 * count * length * split.pairs * (2 * LATENT + ROPE),
        moved=4 * (queries.size + keys.size + weights[0].size * len(weights)),
        grid_spec=pltpu.PrefetchScalarGridSpec(
            num_scalar_prefetch=1,
            grid=(split.pairs,),
            in_specs=[
                pl.BlockSpec((count, 2 * (NOPE + ROPE)), lambda p, place: (0, p)),
                whole,
                whole,
            ]
            + [pl.BlockSpec((1, 4, LATENT, VDIM), pair_of(piece)) for piece in range(len(weights))],
            out_specs=pl.BlockSpec((count, 2 * VDIM), lambda p, place: (0, p)),
            scratch_shapes=[
                pltpu.VMEM((split.parts, length, LATENT + 2 * ROPE), BF16),
                pltpu.VMEM((2, count, LATENT + 2 * ROPE), BF16),
                pltpu.VMEM((2, count, LATENT), BF16),
            ],
        ),
        out_shape=jax.ShapeDtypeStruct((count, 2 * split.pairs * VDIM), BF16),
    )(place, queries, keys, other_keys, *weights)


def send(array, mask):
    count = lax.axis_size("groups") * lax.axis_size("ctx")
    return lax.ppermute(array, ("groups", "ctx"), [(i, i ^ mask) for i in range(count)])


def swap_chips(array):
    shards = lax.axis_size("ctx")
    return lax.all_to_all(
        array,
        "ctx",
        split_axis=0,
        concat_axis=0,
        axis_index_groups=[list(range(core, shards, 2)) for core in range(2)],
        tiled=True,
    )


def after(array, *others):
    return lax.optimization_barrier((array, *others))[0]


def gather_masks(split):
    top, below = split.shards // 2, split.shards // 4
    later = [1 << bit for bit in reversed(range(1, below.bit_length() - 1))]
    return [top, below, top ^ below], ([split.shards] if split.wide else []) + later


def gather_order(split):
    direct, later = gather_masks(split)
    order = [0] + direct
    for mask in later:
        order = order + [offset ^ mask for offset in order]
    return order


def on_device(
    queries,
    latent_kv,
    key_proj,
    value_proj,
    moe_input,
    routes,
    gates,
    expert_gate,
    expert_up,
    expert_down,
):
    shards = lax.axis_size("ctx")
    split = Split(lax.axis_size("groups"), shards, HEADS)
    tok = queries.shape[0]
    experts = shards // 2
    capacity = 2 * ((4 * tok * TOP + 6 * experts - 1) // (6 * experts))
    rows = -(-capacity // 8) * 8
    rank = lax.axis_index("ctx").astype(jnp.int32).reshape(1)
    group = lax.axis_index("groups").astype(jnp.int32).reshape(1)
    place = jnp.concatenate([rank, group])

    direct, later = gather_masks(split)
    keys = [latent_kv] + [send(latent_kv, offset) for offset in direct]

    buckets = after(build_buckets(routes, moe_input, experts, rows), *keys)
    arrived = swap_chips(buckets.reshape(experts, rows, D)).reshape(experts * rows, D)

    sent = split_queries(split, rank, queries)
    keys = after(jnp.stack(keys), sent)
    for mask in later:
        keys = jnp.concatenate([keys, send(keys, mask)], axis=0)

    near = jnp.concatenate(
        [
            key_proj.swapaxes(1, 2).reshape(-1, 2, LATENT, NOPE),
            value_proj.reshape(-1, 2, LATENT, VDIM),
        ],
        axis=1,
    )
    if split.wide:
        near = lax.dynamic_slice_in_dim(near, group[0] * split.own_pairs, split.own_pairs, axis=0)
    near = after(near, buckets)

    own_half = [expert_gate, expert_up, expert_down]
    other_half = [send(after(part, buckets), 1) for part in own_half]
    held = split.exchange(after(sent, keys, near, arrived, *other_half)).reshape(experts * tok, -1)

    result = expert_rows(arrived, own_half, other_half)
    other_keys = send(after(keys, result), 1)
    other_near = send(after(near, result), 1)
    weights = [near, other_near]
    if split.wide:
        far = after(send(after(near, arrived), shards // 2), other_near)
        result = after(result, far)
        weights = [near, far, other_near, send(far, 1)]
    result, held, other_keys = lax.optimization_barrier((result, held, other_keys))
    back = swap_chips(result.reshape(experts, rows, D))
    values = attention(split, place, held, keys, other_keys, weights)
    values, back = lax.optimization_barrier((values, back))
    values = split.exchange(values.reshape(experts, tok, values.shape[1]))
    moe_out = combine(routes, gates, back.reshape(experts * rows, D), rows)
    return (join_values(split, rank, values), moe_out)


def solution(mesh):
    return jax.shard_map(
        on_device,
        mesh=mesh,
        in_specs=(
            P(("groups", "ctx"), None),
            P(("groups", "ctx"), None),
            P("ctx", None, None),
            P("ctx", None, None),
            P(("groups", "ctx"), None),
            P(("groups", "ctx"), None),
            P(("groups", "ctx"), None),
            P("ctx", None, None),
            P("ctx", None, None),
            P("ctx", None, None),
        ),
        out_specs=(P(("groups", "ctx"), None), P(("groups", "ctx"), None)),
        check_vma=False,
    )
```

```python
import functools
import math

import jax
import jax.numpy as jnp
from jax import lax
from jax.experimental import pallas as pl
from jax.experimental.pallas import tpu as pltpu
from jax.sharding import PartitionSpec as P

D = 3584
HEADS = 64
NOPE = 128
ROPE = 64
LATENT = 512
VDIM = 128
TOP = 2
HALF = 512
VMEM_LIMIT = 50 * 1024 * 1024
F32 = jnp.float32
BF16 = jnp.bfloat16


SMEM = pl.BlockSpec(memory_space=pltpu.SMEM)
VMEM = pl.BlockSpec(memory_space=pltpu.VMEM)


def call(kernel, name, flops=0, moved=0, **options):
    return pl.pallas_call(
        kernel,
        name=name,
        cost_estimate=pl.CostEstimate(flops=flops, bytes_accessed=moved, transcendentals=0),
        compiler_params=pltpu.CompilerParams(vmem_limit_bytes=VMEM_LIMIT),
        **options,
    )


def slot_targets(routes, rows):
    tok = routes.shape[0]
    lane = lax.broadcasted_iota(jnp.int32, (tok, 128), 1)
    first = routes[:, 0:1]
    second = routes[:, 1:2]
    hot0 = jnp.where(lane == first, 1.0, 0.0)
    hot1 = jnp.where(lane == second, 1.0, 0.0)
    earlier = jnp.where(
        lax.broadcasted_iota(jnp.int32, (tok, tok), 1) < lax.broadcasted_iota(jnp.int32, (tok, tok), 0),
        1.0,
        0.0,
    )
    counts = jnp.dot(earlier.astype(BF16), (hot0 + hot1).astype(BF16), preferred_element_type=F32)
    slot0 = jnp.sum(counts * hot0, axis=1, keepdims=True).astype(jnp.int32)
    slot1 = jnp.sum(counts * hot1, axis=1, keepdims=True).astype(jnp.int32)
    return first * rows + slot0, second * rows + slot1


def bucket_kernel(rows, routes_ref, x_ref, out_ref):
    target0, target1 = slot_targets(routes_ref[...], rows)
    column = lax.broadcasted_iota(jnp.int32, (x_ref.shape[0], out_ref.shape[0]), 1)
    chosen = jnp.where((column == target0) | (column == target1), 1.0, 0.0).astype(BF16)
    out_ref[...] = lax.dot_general(
        chosen, x_ref[...], (((0,), (0,)), ((), ())), preferred_element_type=F32
    ).astype(BF16)


def build_buckets(routes, moe_input, experts, rows):
    return call(
        functools.partial(bucket_kernel, rows),
        "bucket_rows",
        moved=2 * D * (moe_input.shape[0] + experts * rows),
        out_shape=jax.ShapeDtypeStruct((experts * rows, D), BF16),
    )(routes, moe_input)


def combine_kernel(rows, routes_ref, gates_ref, back_ref, out_ref):
    back = back_ref[...]
    tok = routes_ref.shape[0]
    target0, target1 = slot_targets(routes_ref[...], rows)
    targets = jnp.concatenate([target0, target1], axis=0)
    column = lax.broadcasted_iota(jnp.int32, (2 * tok, back.shape[0]), 1)
    chosen = jnp.where(column == targets, 1.0, 0.0).astype(BF16)
    picked = jnp.dot(chosen, back, preferred_element_type=F32)
    out_ref[...] = (picked[:tok] * gates_ref[:, 0:1] + picked[tok:] * gates_ref[:, 1:2]).astype(BF16)


def combine(routes, gates, back, rows):
    return call(
        functools.partial(combine_kernel, rows),
        "combine_routes",
        moved=2 * D * (routes.shape[0] + back.shape[0]),
        out_shape=jax.ShapeDtypeStruct((routes.shape[0], D), BF16),
    )(routes, gates, back)


STEP = 896
STEPS = D // STEP


def expert_kernel(x_ref, gate0, up0, gate1, up1, down0, down1, out_ref, sums, hidden):
    step = pl.program_id(0)

    @pl.when(step < STEPS)
    def _():
        x = x_ref[...]
        for index, weight_ref in enumerate((gate0, up0, gate1, up1)):
            part = jnp.dot(x, weight_ref[0], preferred_element_type=F32)
            sums[index] = jnp.where(step == 0, part, sums[index] + part)

    @pl.when(step == STEPS)
    def _():
        for half in range(2):
            value = sums[2 * half]
            hidden[half] = (value / (1.0 + jnp.exp(-value)) * sums[2 * half + 1]).astype(BF16)

    @pl.when(step >= STEPS)
    def _():
        first = jnp.dot(hidden[0], down0[0], preferred_element_type=F32).astype(BF16)
        second = jnp.dot(hidden[1], down1[0], preferred_element_type=F32).astype(BF16)
        out_ref[...] = (first.astype(F32) + second.astype(F32)).astype(BF16)


def expert_rows(x, own, other):
    count = x.shape[0]
    weights = pl.BlockSpec((1, STEP, HALF), lambda k: (0, jnp.minimum(k, STEPS - 1), 0))
    down = pl.BlockSpec((1, HALF, STEP), lambda k: (0, 0, jnp.maximum(k - STEPS, 0)))
    return call(
        expert_kernel,
        "expert_rows",
        flops=12 * count * D * HALF,
        moved=12 * D * HALF + 4 * count * D,
        grid=(2 * STEPS,),
        in_specs=[pl.BlockSpec((count, STEP), lambda k: (0, jnp.minimum(k, STEPS - 1)))] + [weights] * 4 + [down] * 2,
        out_specs=pl.BlockSpec((count, STEP), lambda k: (0, jnp.maximum(k - STEPS, 0))),
        scratch_shapes=[pltpu.VMEM((4, count, HALF), F32), pltpu.VMEM((2, count, HALF), BF16)],
        out_shape=jax.ShapeDtypeStruct((count, D), BF16),
    )(x, own[0], own[1], other[0], other[1], own[2], other[2])


class Split:
    def __init__(self, groups, shards, heads):
        self.groups, self.shards = groups, shards
        self.each = heads // shards
        self.wide = groups == 2 and self.each % (2 * groups) == 0
        self.chips = shards // 2
        self.own_pairs = self.each // 2 // (groups if self.wide else 1)
        self.holders = 2 if self.wide else 1
        self.pairs = 2 * self.holders * self.own_pairs
        self.parts = groups if self.wide else 1

    def first_head(self, rank, chip, pair):
        core, rest = divmod(pair, self.holders * self.own_pairs)
        holder, own = divmod(rest, self.own_pairs)
        if not self.wide:
            return (2 * chip + ((rank & 1) ^ core)) * self.each + 2 * own
        group, low = divmod(chip, self.shards // 4)
        top = (rank & (self.shards // 2)) ^ (holder * (self.shards // 2))
        return (top + 2 * low + ((rank & 1) ^ core)) * self.each + 2 * (group * self.own_pairs + own)

    def exchange(self, array):
        half = self.shards // 2
        if self.wide:
            tops, steps = (0, half), [g * self.shards + c for g in range(self.groups) for c in range(0, half, 2)]
            sets = [[start + core + step for step in steps] for start in tops for core in range(2)]
        else:
            starts = range(0, self.groups * self.shards, self.shards)
            sets = [[start + core + c for c in range(0, self.shards, 2)] for start in starts for core in range(2)]
        return lax.all_to_all(
            array, ("groups", "ctx"), split_axis=0, concat_axis=0, axis_index_groups=sets, tiled=True
        )


def split_kernel(split, rank_ref, x_ref, out_ref):
    each = NOPE + ROPE
    for chip in range(split.chips):
        for pair in range(split.pairs):
            start = pl.multiple_of(split.first_head(rank_ref[0], chip, pair) * each, 128)
            part = x_ref[:, pl.ds(start, 2 * each)]
            out_ref[chip, :, pair * 2 * each : (pair + 1) * 2 * each] = jnp.concatenate(
                [part[:, :NOPE], part[:, each : each + NOPE], part[:, NOPE:each], part[:, each + NOPE :]], axis=1
            )


def split_queries(split, rank, queries):
    tok = queries.shape[0]
    return call(
        functools.partial(split_kernel, split),
        "split_queries",
        moved=4 * queries.size,
        in_specs=[SMEM, VMEM],
        out_specs=VMEM,
        out_shape=jax.ShapeDtypeStruct((split.chips, tok, 2 * split.pairs * (NOPE + ROPE)), BF16),
    )(rank, queries)


def join_kernel(split, rank_ref, x_ref, out_ref):
    for chip in range(split.chips):
        for pair in range(split.pairs):
            start = pl.multiple_of(split.first_head(rank_ref[0], chip, pair) * VDIM, 128)
            out_ref[:, pl.ds(start, 2 * VDIM)] = x_ref[chip, :, pair * 2 * VDIM : (pair + 1) * 2 * VDIM]


def join_values(split, rank, values):
    return call(
        functools.partial(join_kernel, split),
        "join_values",
        moved=4 * values.size,
        in_specs=[SMEM, VMEM],
        out_specs=VMEM,
        out_shape=jax.ShapeDtypeStruct((values.shape[1], HEADS * VDIM), BF16),
    )(rank, values)


BLOCK = 128
SPAN = 2 * BLOCK
EXP_SCALE = math.log2(math.e) / math.sqrt(NOPE + ROPE)


def attention_kernel(
    split, rank_ref, query_ref, kv_ref, other_kv_ref, weight_ref, other_weight_ref, out_ref, keys, queries, mixed
):
    tok = kv_ref.shape[1]
    part_rows = query_ref.shape[0] // split.parts
    core = rank_ref[0] & 1

    @pl.when(pl.program_id(0) == 0)
    def _():
        for index, offset in enumerate(gather_order(split)):
            for from_ref, swapped in ((kv_ref, 0), (other_kv_ref, 1)):
                group, ctx = divmod(offset ^ swapped, split.shards)
                group = rank_ref[1] ^ group if split.wide else 0
                place = pl.ds(pl.multiple_of((rank_ref[0] ^ ctx) * tok, tok), tok)
                keys[group, place, : LATENT + ROPE] = from_ref[index]
                keys[group, place, LATENT + ROPE :] = from_ref[index, :, LATENT:]

    own_core = pl.program_id(0) < split.pairs // 2

    def weight(index):
        return jnp.where(own_core, weight_ref[0, index], other_weight_ref[0, index])

    contract = (((1,), (1,)), ((), ()))
    side = lax.broadcasted_iota(jnp.int32, (1, 2 * ROPE), 1) // ROPE
    for one in range(2):
        latent = lax.dot_general(
            query_ref[:, one * NOPE : (one + 1) * NOPE], weight(one), contract, preferred_element_type=F32
        )
        queries[one, :, :LATENT] = latent.astype(BF16)
        queries[one, :, LATENT:] = jnp.where(side == one, query_ref[:, 2 * NOPE :], jnp.zeros((), BF16))

    row = lax.broadcasted_iota(jnp.int32, (2 * BLOCK, SPAN), 0) % BLOCK
    position = (2 * (row // tok) + core) * tok + row % tok
    visible = lax.broadcasted_iota(jnp.int32, (2 * BLOCK, SPAN), 1) <= position

    def attend(part, block, before):
        start = before * SPAN
        first = part * part_rows + block * BLOCK
        rows = pl.ds(first, BLOCK)
        last = pl.ds(start, SPAN)
        query = jnp.concatenate([queries[0, rows, :], queries[1, rows, :]], axis=0)
        near = lax.dot_general(query, keys[part, last, :], contract, preferred_element_type=F32)
        near = jnp.where(visible, near, -1e30)
        top = jnp.max(near, axis=1, keepdims=True)
        if before:
            past = lax.dot_general(query, keys[part, :start, :], contract, preferred_element_type=F32)
            top = jnp.maximum(top, jnp.max(past, axis=1, keepdims=True))
        weights = jnp.exp2((near - top) * EXP_SCALE)
        total = jnp.sum(weights, axis=1, keepdims=True)
        summed = jnp.dot(weights.astype(BF16), keys[part, last, :LATENT], preferred_element_type=F32)
        if before:
            weights = jnp.exp2((past - top) * EXP_SCALE)
            total = total + jnp.sum(weights, axis=1, keepdims=True)
            summed = summed + jnp.dot(
                weights.astype(BF16), keys[part, :start, :LATENT], preferred_element_type=F32
            )
        result = (summed / total).astype(BF16)
        mixed[0, rows, :] = result[:BLOCK]
        mixed[1, rows, :] = result[BLOCK:]

    blocks = part_rows // BLOCK
    if split.wide:
        for half in range(2):

            @pl.when(rank_ref[0] // (split.shards // 2) == half)
            def _():
                for part in range(split.parts):
                    for block in range(blocks):
                        attend(part, block, half * blocks + block)

    else:
        for block in range(blocks):
            attend(0, block, block)

    for one in range(2):
        out_ref[:, one * VDIM : (one + 1) * VDIM] = jnp.dot(
            mixed[one], weight(2 + one), preferred_element_type=F32
        ).astype(BF16)


def attention(split, place, queries, keys, other_keys, weights, other_weights):
    count = queries.shape[0]
    length = 2 * keys.shape[0] * keys.shape[1] // split.parts
    whole = pl.BlockSpec(keys.shape, lambda p, place: (0, 0, 0))
    each = split.pairs // 2
    return call(
        functools.partial(attention_kernel, split),
        "causal_attention",
        flops=4 * count * length * split.pairs * (2 * LATENT + ROPE),
        moved=4 * (queries.size + keys.size + weights.size),
        grid_spec=pltpu.PrefetchScalarGridSpec(
            num_scalar_prefetch=1,
            grid=(split.pairs,),
            in_specs=[
                pl.BlockSpec((count, 2 * (NOPE + ROPE)), lambda p, place: (0, p)),
                whole,
                whole,
                pl.BlockSpec((1, 4, LATENT, VDIM), lambda p, place: (jnp.minimum(p, each - 1), 0, 0, 0)),
                pl.BlockSpec((1, 4, LATENT, VDIM), lambda p, place: (jnp.maximum(p - each, 0), 0, 0, 0)),
            ],
            out_specs=pl.BlockSpec((count, 2 * VDIM), lambda p, place: (0, p)),
            scratch_shapes=[
                pltpu.VMEM((split.parts, length, LATENT + 2 * ROPE), BF16),
                pltpu.VMEM((2, count, LATENT + 2 * ROPE), BF16),
                pltpu.VMEM((2, count, LATENT), BF16),
            ],
        ),
        out_shape=jax.ShapeDtypeStruct((count, 2 * split.pairs * VDIM), BF16),
    )(place, queries, keys, other_keys, weights, other_weights)


def send(array, mask):
    count = lax.axis_size("groups") * lax.axis_size("ctx")
    return lax.ppermute(array, ("groups", "ctx"), [(i, i ^ mask) for i in range(count)])


def swap_chips(array):
    shards = lax.axis_size("ctx")
    return lax.all_to_all(
        array,
        "ctx",
        split_axis=0,
        concat_axis=0,
        axis_index_groups=[list(range(core, shards, 2)) for core in range(2)],
        tiled=True,
    )


def after(array, *others):
    return lax.optimization_barrier((array, *others))[0]


def gather_masks(split):
    top, below = split.shards // 2, split.shards // 4
    later = [1 << bit for bit in reversed(range(1, below.bit_length() - 1))]
    return [top, below, top ^ below], ([split.shards] if split.wide else []) + later


def gather_order(split):
    direct, later = gather_masks(split)
    order = [0] + direct
    for mask in later:
        order = order + [offset ^ mask for offset in order]
    return order


def on_device(
    queries,
    latent_kv,
    key_proj,
    value_proj,
    moe_input,
    routes,
    gates,
    expert_gate,
    expert_up,
    expert_down,
):
    shards = lax.axis_size("ctx")
    split = Split(lax.axis_size("groups"), shards, HEADS)
    tok = queries.shape[0]
    experts = shards // 2
    capacity = 2 * ((4 * tok * TOP + 6 * experts - 1) // (6 * experts))
    rows = -(-capacity // 8) * 8
    rank = lax.axis_index("ctx").astype(jnp.int32).reshape(1)
    group = lax.axis_index("groups").astype(jnp.int32).reshape(1)
    place = jnp.concatenate([rank, group])

    direct, later = gather_masks(split)
    keys = [latent_kv] + [send(latent_kv, offset) for offset in direct]

    buckets = after(build_buckets(routes, moe_input, experts, rows), *keys)
    arrived = swap_chips(buckets.reshape(experts, rows, D)).reshape(experts * rows, D)

    sent = split_queries(split, rank, queries)
    keys = after(jnp.stack(keys), sent)
    for mask in later:
        keys = jnp.concatenate([keys, send(keys, mask)], axis=0)
    other_keys = send(keys, 1)
    own_half = [expert_gate, expert_up, expert_down]
    other_half = [send(after(part, buckets), 1) for part in own_half]
    sent = after(sent, other_keys, arrived, *other_half)
    held = split.exchange(sent).reshape(experts * tok, -1)

    weights = jnp.concatenate(
        [
            key_proj.swapaxes(1, 2).reshape(-1, 2, LATENT, NOPE),
            value_proj.reshape(-1, 2, LATENT, VDIM),
        ],
        axis=1,
    )
    if split.wide:
        weights = lax.dynamic_slice_in_dim(weights, group[0] * split.own_pairs, split.own_pairs, axis=0)
        weights = after(weights, arrived)
        weights = jnp.concatenate([weights, send(weights, shards // 2)], axis=0)

    result = expert_rows(arrived, own_half, other_half)
    other_weights = send(after(weights, result), 1)
    result, held = lax.optimization_barrier((result, held))
    back = swap_chips(result.reshape(experts, rows, D))
    values = attention(split, place, held, keys, other_keys, weights, other_weights)
    values, back = lax.optimization_barrier((values, back))
    values = split.exchange(values.reshape(experts, tok, values.shape[1]))
    moe_out = combine(routes, gates, back.reshape(experts * rows, D), rows)
    return (join_values(split, rank, values), moe_out)


def solution(mesh):
    return jax.shard_map(
        on_device,
        mesh=mesh,
        in_specs=(
            P(("groups", "ctx"), None),
            P(("groups", "ctx"), None),
            P("ctx", None, None),
            P("ctx", None, None),
            P(("groups", "ctx"), None),
            P(("groups", "ctx"), None),
            P(("groups", "ctx"), None),
            P("ctx", None, None),
            P("ctx", None, None),
            P("ctx", None, None),
        ),
        out_specs=(P(("groups", "ctx"), None), P(("groups", "ctx"), None)),
        check_vma=False,
    )
```

```python
import functools
import math

import jax
import jax.numpy as jnp
from jax import lax
from jax.experimental import pallas as pl
from jax.experimental.pallas import tpu as pltpu
from jax.sharding import PartitionSpec as P

D = 3584
HEADS = 64
NOPE = 128
ROPE = 64
LATENT = 512
VDIM = 128
TOP = 2
HALF = 512
VMEM_LIMIT = 50 * 1024 * 1024
F32 = jnp.float32
BF16 = jnp.bfloat16


SMEM = pl.BlockSpec(memory_space=pltpu.SMEM)
VMEM = pl.BlockSpec(memory_space=pltpu.VMEM)


def call(kernel, name, flops=0, moved=0, **options):
    return pl.pallas_call(
        kernel,
        name=name,
        cost_estimate=pl.CostEstimate(flops=flops, bytes_accessed=moved, transcendentals=0),
        compiler_params=pltpu.CompilerParams(vmem_limit_bytes=VMEM_LIMIT),
        **options,
    )


def slot_targets(routes, rows):
    tok = routes.shape[0]
    lane = lax.broadcasted_iota(jnp.int32, (tok, 128), 1)
    first = routes[:, 0:1]
    second = routes[:, 1:2]
    hot0 = jnp.where(lane == first, 1.0, 0.0)
    hot1 = jnp.where(lane == second, 1.0, 0.0)
    earlier = jnp.where(
        lax.broadcasted_iota(jnp.int32, (tok, tok), 1) < lax.broadcasted_iota(jnp.int32, (tok, tok), 0),
        1.0,
        0.0,
    )
    counts = jnp.dot(earlier.astype(BF16), (hot0 + hot1).astype(BF16), preferred_element_type=F32)
    slot0 = jnp.sum(counts * hot0, axis=1, keepdims=True).astype(jnp.int32)
    slot1 = jnp.sum(counts * hot1, axis=1, keepdims=True).astype(jnp.int32)
    return first * rows + slot0, second * rows + slot1


def bucket_kernel(rows, routes_ref, x_ref, out_ref):
    target0, target1 = slot_targets(routes_ref[...], rows)
    column = lax.broadcasted_iota(jnp.int32, (x_ref.shape[0], out_ref.shape[0]), 1)
    chosen = jnp.where((column == target0) | (column == target1), 1.0, 0.0).astype(BF16)
    out_ref[...] = lax.dot_general(
        chosen, x_ref[...], (((0,), (0,)), ((), ())), preferred_element_type=F32
    ).astype(BF16)


def build_buckets(routes, moe_input, experts, rows):
    return call(
        functools.partial(bucket_kernel, rows),
        "bucket_rows",
        moved=2 * D * (moe_input.shape[0] + experts * rows),
        out_shape=jax.ShapeDtypeStruct((experts * rows, D), BF16),
    )(routes, moe_input)


def combine_kernel(rows, routes_ref, gates_ref, back_ref, out_ref):
    back = back_ref[...]
    tok = routes_ref.shape[0]
    target0, target1 = slot_targets(routes_ref[...], rows)
    targets = jnp.concatenate([target0, target1], axis=0)
    column = lax.broadcasted_iota(jnp.int32, (2 * tok, back.shape[0]), 1)
    chosen = jnp.where(column == targets, 1.0, 0.0).astype(BF16)
    picked = jnp.dot(chosen, back, preferred_element_type=F32)
    out_ref[...] = (picked[:tok] * gates_ref[:, 0:1] + picked[tok:] * gates_ref[:, 1:2]).astype(BF16)


def combine(routes, gates, back, rows):
    return call(
        functools.partial(combine_kernel, rows),
        "combine_routes",
        moved=2 * D * (routes.shape[0] + back.shape[0]),
        out_shape=jax.ShapeDtypeStruct((routes.shape[0], D), BF16),
    )(routes, gates, back)


STEP = 896
STEPS = D // STEP


def expert_kernel(x_ref, gate0, up0, gate1, up1, down0, down1, out_ref, sums, hidden):
    step = pl.program_id(0)

    @pl.when(step < STEPS)
    def _():
        x = x_ref[...]
        for index, weight_ref in enumerate((gate0, up0, gate1, up1)):
            part = jnp.dot(x, weight_ref[0], preferred_element_type=F32)
            sums[index] = jnp.where(step == 0, part, sums[index] + part)

    @pl.when(step == STEPS)
    def _():
        for half in range(2):
            value = sums[2 * half]
            hidden[half] = (value / (1.0 + jnp.exp(-value)) * sums[2 * half + 1]).astype(BF16)

    @pl.when(step >= STEPS)
    def _():
        first = jnp.dot(hidden[0], down0[0], preferred_element_type=F32).astype(BF16)
        second = jnp.dot(hidden[1], down1[0], preferred_element_type=F32).astype(BF16)
        out_ref[...] = (first.astype(F32) + second.astype(F32)).astype(BF16)


def expert_rows(x, own, other):
    count = x.shape[0]
    weights = pl.BlockSpec((1, STEP, HALF), lambda k: (0, jnp.minimum(k, STEPS - 1), 0))
    down = pl.BlockSpec((1, HALF, STEP), lambda k: (0, 0, jnp.maximum(k - STEPS, 0)))
    return call(
        expert_kernel,
        "expert_rows",
        flops=12 * count * D * HALF,
        moved=12 * D * HALF + 4 * count * D,
        grid=(2 * STEPS,),
        in_specs=[pl.BlockSpec((count, STEP), lambda k: (0, jnp.minimum(k, STEPS - 1)))] + [weights] * 4 + [down] * 2,
        out_specs=pl.BlockSpec((count, STEP), lambda k: (0, jnp.maximum(k - STEPS, 0))),
        scratch_shapes=[pltpu.VMEM((4, count, HALF), F32), pltpu.VMEM((2, count, HALF), BF16)],
        out_shape=jax.ShapeDtypeStruct((count, D), BF16),
    )(x, own[0], own[1], other[0], other[1], own[2], other[2])


class Split:
    def __init__(self, groups, shards, heads):
        self.groups, self.shards = groups, shards
        self.each = heads // shards
        self.wide = groups == 2 and self.each % (2 * groups) == 0
        self.chips = shards // 2
        self.own_pairs = self.each // 2 // (groups if self.wide else 1)
        self.holders = 2 if self.wide else 1
        self.pairs = 2 * self.holders * self.own_pairs
        self.parts = groups if self.wide else 1

    def first_head(self, rank, chip, pair):
        core, rest = divmod(pair, self.holders * self.own_pairs)
        holder, own = divmod(rest, self.own_pairs)
        if not self.wide:
            return (2 * chip + ((rank & 1) ^ core)) * self.each + 2 * own
        group, low = divmod(chip, self.shards // 4)
        top = (rank & (self.shards // 2)) ^ (holder * (self.shards // 2))
        return (top + 2 * low + ((rank & 1) ^ core)) * self.each + 2 * (group * self.own_pairs + own)

    def exchange(self, array):
        half = self.shards // 2
        if self.wide:
            tops, steps = (0, half), [g * self.shards + c for g in range(self.groups) for c in range(0, half, 2)]
            sets = [[start + core + step for step in steps] for start in tops for core in range(2)]
        else:
            starts = range(0, self.groups * self.shards, self.shards)
            sets = [[start + core + c for c in range(0, self.shards, 2)] for start in starts for core in range(2)]
        return lax.all_to_all(
            array, ("groups", "ctx"), split_axis=0, concat_axis=0, axis_index_groups=sets, tiled=True
        )


def split_kernel(split, rank_ref, x_ref, out_ref):
    each = NOPE + ROPE
    for chip in range(split.chips):
        for pair in range(split.pairs):
            start = pl.multiple_of(split.first_head(rank_ref[0], chip, pair) * each, 128)
            part = x_ref[:, pl.ds(start, 2 * each)]
            out_ref[chip, :, pair * 2 * each : (pair + 1) * 2 * each] = jnp.concatenate(
                [part[:, :NOPE], part[:, each : each + NOPE], part[:, NOPE:each], part[:, each + NOPE :]], axis=1
            )


def split_queries(split, rank, queries):
    tok = queries.shape[0]
    return call(
        functools.partial(split_kernel, split),
        "split_queries",
        moved=4 * queries.size,
        in_specs=[SMEM, VMEM],
        out_specs=VMEM,
        out_shape=jax.ShapeDtypeStruct((split.chips, tok, 2 * split.pairs * (NOPE + ROPE)), BF16),
    )(rank, queries)


def join_kernel(split, rank_ref, x_ref, out_ref):
    for chip in range(split.chips):
        for pair in range(split.pairs):
            start = pl.multiple_of(split.first_head(rank_ref[0], chip, pair) * VDIM, 128)
            out_ref[:, pl.ds(start, 2 * VDIM)] = x_ref[chip, :, pair * 2 * VDIM : (pair + 1) * 2 * VDIM]


def join_values(split, rank, values):
    return call(
        functools.partial(join_kernel, split),
        "join_values",
        moved=4 * values.size,
        in_specs=[SMEM, VMEM],
        out_specs=VMEM,
        out_shape=jax.ShapeDtypeStruct((values.shape[1], HEADS * VDIM), BF16),
    )(rank, values)


BLOCK = 128
SPAN = 2 * BLOCK
EXP_SCALE = math.log2(math.e) / math.sqrt(NOPE + ROPE)


def attention_kernel(
    split, rank_ref, query_ref, kv_ref, other_kv_ref, weight_ref, other_weight_ref, out_ref, keys, queries, mixed
):
    tok = kv_ref.shape[1]
    part_rows = query_ref.shape[0] // split.parts
    core = rank_ref[0] & 1

    @pl.when(pl.program_id(0) == 0)
    def _():
        for index, offset in enumerate(gather_order(split)):
            for from_ref, swapped in ((kv_ref, 0), (other_kv_ref, 1)):
                group, ctx = divmod(offset ^ swapped, split.shards)
                group = rank_ref[1] ^ group if split.wide else 0
                place = pl.ds(pl.multiple_of((rank_ref[0] ^ ctx) * tok, tok), tok)
                keys[group, place, : LATENT + ROPE] = from_ref[index]
                keys[group, place, LATENT + ROPE :] = from_ref[index, :, LATENT:]

    own_core = pl.program_id(0) < split.pairs // 2

    def weight(index):
        return jnp.where(own_core, weight_ref[0, index], other_weight_ref[0, index])

    contract = (((1,), (1,)), ((), ()))
    side = lax.broadcasted_iota(jnp.int32, (1, 2 * ROPE), 1) // ROPE
    for one in range(2):
        latent = lax.dot_general(
            query_ref[:, one * NOPE : (one + 1) * NOPE], weight(one), contract, preferred_element_type=F32
        )
        queries[one, :, :LATENT] = latent.astype(BF16)
        queries[one, :, LATENT:] = jnp.where(side == one, query_ref[:, 2 * NOPE :], jnp.zeros((), BF16))

    row = lax.broadcasted_iota(jnp.int32, (2 * BLOCK, SPAN), 0) % BLOCK
    position = (2 * (row // tok) + core) * tok + row % tok
    visible = lax.broadcasted_iota(jnp.int32, (2 * BLOCK, SPAN), 1) <= position

    def attend(part, block, before):
        start = before * SPAN
        first = part * part_rows + block * BLOCK
        rows = pl.ds(first, BLOCK)
        last = pl.ds(start, SPAN)
        query = jnp.concatenate([queries[0, rows, :], queries[1, rows, :]], axis=0)
        near = lax.dot_general(query, keys[part, last, :], contract, preferred_element_type=F32)
        near = jnp.where(visible, near, -1e30)
        top = jnp.max(near, axis=1, keepdims=True)
        if before:
            past = lax.dot_general(query, keys[part, :start, :], contract, preferred_element_type=F32)
            top = jnp.maximum(top, jnp.max(past, axis=1, keepdims=True))
        weights = jnp.exp2((near - top) * EXP_SCALE)
        total = jnp.sum(weights, axis=1, keepdims=True)
        summed = jnp.dot(weights.astype(BF16), keys[part, last, :LATENT], preferred_element_type=F32)
        if before:
            weights = jnp.exp2((past - top) * EXP_SCALE)
            total = total + jnp.sum(weights, axis=1, keepdims=True)
            summed = summed + jnp.dot(
                weights.astype(BF16), keys[part, :start, :LATENT], preferred_element_type=F32
            )
        result = (summed / total).astype(BF16)
        mixed[0, rows, :] = result[:BLOCK]
        mixed[1, rows, :] = result[BLOCK:]

    blocks = part_rows // BLOCK
    if split.wide:
        for half in range(2):

            @pl.when(rank_ref[0] // (split.shards // 2) == half)
            def _():
                for part in range(split.parts):
                    for block in range(blocks):
                        attend(part, block, half * blocks + block)

    else:
        for block in range(blocks):
            attend(0, block, block)

    for one in range(2):
        out_ref[:, one * VDIM : (one + 1) * VDIM] = jnp.dot(
            mixed[one], weight(2 + one), preferred_element_type=F32
        ).astype(BF16)


def attention(split, place, queries, keys, other_keys, weights, other_weights):
    count = queries.shape[0]
    length = 2 * keys.shape[0] * keys.shape[1] // split.parts
    whole = pl.BlockSpec(keys.shape, lambda p, place: (0, 0, 0))
    each = split.pairs // 2
    return call(
        functools.partial(attention_kernel, split),
        "causal_attention",
        flops=4 * count * length * split.pairs * (2 * LATENT + ROPE),
        moved=4 * (queries.size + keys.size + weights.size),
        grid_spec=pltpu.PrefetchScalarGridSpec(
            num_scalar_prefetch=1,
            grid=(split.pairs,),
            in_specs=[
                pl.BlockSpec((count, 2 * (NOPE + ROPE)), lambda p, place: (0, p)),
                whole,
                whole,
                pl.BlockSpec((1, 4, LATENT, VDIM), lambda p, place: (jnp.minimum(p, each - 1), 0, 0, 0)),
                pl.BlockSpec((1, 4, LATENT, VDIM), lambda p, place: (jnp.maximum(p - each, 0), 0, 0, 0)),
            ],
            out_specs=pl.BlockSpec((count, 2 * VDIM), lambda p, place: (0, p)),
            scratch_shapes=[
                pltpu.VMEM((split.parts, length, LATENT + 2 * ROPE), BF16),
                pltpu.VMEM((2, count, LATENT + 2 * ROPE), BF16),
                pltpu.VMEM((2, count, LATENT), BF16),
            ],
        ),
        out_shape=jax.ShapeDtypeStruct((count, 2 * split.pairs * VDIM), BF16),
    )(place, queries, keys, other_keys, weights, other_weights)


def send(array, mask):
    count = lax.axis_size("groups") * lax.axis_size("ctx")
    return lax.ppermute(array, ("groups", "ctx"), [(i, i ^ mask) for i in range(count)])


def swap_chips(array):
    shards = lax.axis_size("ctx")
    return lax.all_to_all(
        array,
        "ctx",
        split_axis=0,
        concat_axis=0,
        axis_index_groups=[list(range(core, shards, 2)) for core in range(2)],
        tiled=True,
    )


def after(array, *others):
    return lax.optimization_barrier((array, *others))[0]


def gather_masks(split):
    top, below = split.shards // 2, split.shards // 4
    later = [1 << bit for bit in reversed(range(1, below.bit_length() - 1))]
    return [top, below, top ^ below], ([split.shards] if split.wide else []) + later


def gather_order(split):
    direct, later = gather_masks(split)
    order = [0] + direct
    for mask in later:
        order = order + [offset ^ mask for offset in order]
    return order


def on_device(
    queries,
    latent_kv,
    key_proj,
    value_proj,
    moe_input,
    routes,
    gates,
    expert_gate,
    expert_up,
    expert_down,
):
    shards = lax.axis_size("ctx")
    split = Split(lax.axis_size("groups"), shards, HEADS)
    tok = queries.shape[0]
    experts = shards // 2
    capacity = 2 * ((4 * tok * TOP + 6 * experts - 1) // (6 * experts))
    rows = -(-capacity // 8) * 8
    rank = lax.axis_index("ctx").astype(jnp.int32).reshape(1)
    group = lax.axis_index("groups").astype(jnp.int32).reshape(1)
    place = jnp.concatenate([rank, group])

    direct, later = gather_masks(split)
    keys = [latent_kv] + [send(latent_kv, offset) for offset in direct]

    buckets = after(build_buckets(routes, moe_input, experts, rows), *keys)
    arrived = swap_chips(buckets.reshape(experts, rows, D)).reshape(experts * rows, D)

    sent = split_queries(split, rank, queries)
    keys = after(jnp.stack(keys), sent)
    for mask in later:
        keys = jnp.concatenate([keys, send(keys, mask)], axis=0)
    other_keys = send(keys, 1)
    own_half = [expert_gate, expert_up, expert_down]
    other_half = [send(after(part, buckets), 1) for part in own_half]
    sent = after(sent, keys, arrived, *other_half)
    held = split.exchange(sent).reshape(experts * tok, -1)

    weights = jnp.concatenate(
        [
            key_proj.swapaxes(1, 2).reshape(-1, 2, LATENT, NOPE),
            value_proj.reshape(-1, 2, LATENT, VDIM),
        ],
        axis=1,
    )
    if split.wide:
        weights = lax.dynamic_slice_in_dim(weights, group[0] * split.own_pairs, split.own_pairs, axis=0)
        weights = after(weights, arrived)
        weights = jnp.concatenate([weights, send(weights, shards // 2)], axis=0)

    result = expert_rows(arrived, own_half, other_half)
    other_weights = send(after(weights, result), 1)
    result, held = lax.optimization_barrier((result, held))
    back = swap_chips(result.reshape(experts, rows, D))
    values = attention(split, place, held, keys, other_keys, weights, other_weights)
    values, back = lax.optimization_barrier((values, back))
    values = split.exchange(values.reshape(experts, tok, values.shape[1]))
    moe_out = combine(routes, gates, back.reshape(experts * rows, D), rows)
    return (join_values(split, rank, values), moe_out)


def solution(mesh):
    return jax.shard_map(
        on_device,
        mesh=mesh,
        in_specs=(
            P(("groups", "ctx"), None),
            P(("groups", "ctx"), None),
            P("ctx", None, None),
            P("ctx", None, None),
            P(("groups", "ctx"), None),
            P(("groups", "ctx"), None),
            P(("groups", "ctx"), None),
            P("ctx", None, None),
            P("ctx", None, None),
            P("ctx", None, None),
        ),
        out_specs=(P(("groups", "ctx"), None), P(("groups", "ctx"), None)),
        check_vma=False,
    )
```

```python
import functools
import math

import jax
import jax.numpy as jnp
from jax import lax
from jax.experimental import pallas as pl
from jax.experimental.pallas import tpu as pltpu
from jax.sharding import PartitionSpec as P

D = 3584
HEADS = 64
NOPE = 128
ROPE = 64
LATENT = 512
VDIM = 128
TOP = 2
HALF = 512
VMEM_LIMIT = 50 * 1024 * 1024
F32 = jnp.float32
BF16 = jnp.bfloat16


SMEM = pl.BlockSpec(memory_space=pltpu.SMEM)
VMEM = pl.BlockSpec(memory_space=pltpu.VMEM)


def call(kernel, name, flops=0, moved=0, **options):
    return pl.pallas_call(
        kernel,
        name=name,
        cost_estimate=pl.CostEstimate(flops=flops, bytes_accessed=moved, transcendentals=0),
        compiler_params=pltpu.CompilerParams(vmem_limit_bytes=VMEM_LIMIT),
        **options,
    )


def slot_targets(routes, rows):
    tok = routes.shape[0]
    lane = lax.broadcasted_iota(jnp.int32, (tok, 128), 1)
    first = routes[:, 0:1]
    second = routes[:, 1:2]
    hot0 = jnp.where(lane == first, 1.0, 0.0)
    hot1 = jnp.where(lane == second, 1.0, 0.0)
    earlier = jnp.where(
        lax.broadcasted_iota(jnp.int32, (tok, tok), 1) < lax.broadcasted_iota(jnp.int32, (tok, tok), 0),
        1.0,
        0.0,
    )
    counts = jnp.dot(earlier.astype(BF16), (hot0 + hot1).astype(BF16), preferred_element_type=F32)
    slot0 = jnp.sum(counts * hot0, axis=1, keepdims=True).astype(jnp.int32)
    slot1 = jnp.sum(counts * hot1, axis=1, keepdims=True).astype(jnp.int32)
    return first * rows + slot0, second * rows + slot1


STEP = 896
STEPS = D // STEP


def bucket_kernel(rows, routes_ref, x_ref, out_ref):
    target0, target1 = slot_targets(routes_ref[...], STEPS * rows)
    column = lax.broadcasted_iota(jnp.int32, (x_ref.shape[0], out_ref.shape[0]), 1)
    chosen = []
    for part in range(STEPS):
        hit = (column == target0 + part * rows) | (column == target1 + part * rows)
        chosen.append(jnp.where(hit, 1.0, 0.0).astype(BF16))
    parts = [x_ref[:, part * STEP : (part + 1) * STEP] for part in range(STEPS)]
    out_ref[...] = lax.dot_general(
        jnp.concatenate(chosen, axis=0),
        jnp.concatenate(parts, axis=0),
        (((0,), (0,)), ((), ())),
        preferred_element_type=F32,
    ).astype(BF16)


def build_buckets(routes, moe_input, experts, rows):
    return call(
        functools.partial(bucket_kernel, rows),
        "bucket_rows",
        moved=2 * D * (moe_input.shape[0] + experts * rows),
        out_shape=jax.ShapeDtypeStruct((experts * STEPS * rows, STEP), BF16),
    )(routes, moe_input)


def combine_kernel(rows, routes_ref, gates_ref, back_ref, out_ref):
    tok = routes_ref.shape[0]
    target0, target1 = slot_targets(routes_ref[...], STEPS * rows)
    targets = jnp.concatenate([target0, target1], axis=0)
    column = lax.broadcasted_iota(jnp.int32, (2 * tok, back_ref.shape[0]), 1)
    for part in range(STEPS):
        chosen = jnp.where(column == targets + part * rows, 1.0, 0.0).astype(BF16)
        picked = jnp.dot(chosen, back_ref[...], preferred_element_type=F32)
        out_ref[:, part * STEP : (part + 1) * STEP] = (
            picked[:tok] * gates_ref[:, 0:1] + picked[tok:] * gates_ref[:, 1:2]
        ).astype(BF16)


def combine(routes, gates, back, rows):
    return call(
        functools.partial(combine_kernel, rows),
        "combine_routes",
        moved=2 * D * (routes.shape[0] + back.shape[0]),
        out_shape=jax.ShapeDtypeStruct((routes.shape[0], D), BF16),
    )(routes, gates, back)


def rows_of_part(experts, rows, part):
    shape = (experts * rows, experts * STEPS * rows)
    row = lax.broadcasted_iota(jnp.int32, shape, 0)
    source = row + part * rows
    for chip in range(1, experts):
        source = source + jnp.where(row >= chip * rows, (STEPS - 1) * rows, 0)
    return jnp.where(lax.broadcasted_iota(jnp.int32, shape, 1) == source, 1.0, 0.0).astype(BF16)


def expert_kernel(experts, x_ref, gate0, up0, gate1, up1, down0, down1, out_ref, x, sums, hidden, result):
    step = pl.program_id(0)
    rows = x.shape[1] // experts

    @pl.when(step == 0)
    def _():
        for part in range(STEPS):
            chosen = rows_of_part(experts, rows, part)
            x[part] = jnp.dot(chosen, x_ref[...], preferred_element_type=F32).astype(BF16)

    @pl.when(step < STEPS)
    def _():
        for index, weight_ref in enumerate((gate0, up0, gate1, up1)):
            product = jnp.dot(x[step], weight_ref[0], preferred_element_type=F32)
            sums[index] = jnp.where(step == 0, product, sums[index] + product)

    @pl.when(step == STEPS)
    def _():
        for half in range(2):
            value = sums[2 * half]
            hidden[half] = (value / (1.0 + jnp.exp(-value)) * sums[2 * half + 1]).astype(BF16)

    @pl.when(step >= STEPS)
    def _():
        first = jnp.dot(hidden[0], down0[0], preferred_element_type=F32).astype(BF16)
        second = jnp.dot(hidden[1], down1[0], preferred_element_type=F32).astype(BF16)
        result[step - STEPS] = (first.astype(F32) + second.astype(F32)).astype(BF16)

    @pl.when(step == 2 * STEPS - 1)
    def _():
        total = jnp.zeros(out_ref.shape, F32)
        for part in range(STEPS):
            total = total + lax.dot_general(
                rows_of_part(experts, rows, part),
                result[part],
                (((0,), (0,)), ((), ())),
                preferred_element_type=F32,
            )
        out_ref[...] = total.astype(BF16)


def expert_rows(x, own, other, experts):
    count = x.shape[0] // STEPS
    weights = pl.BlockSpec((1, STEP, HALF), lambda k: (0, jnp.minimum(k, STEPS - 1), 0))
    down = pl.BlockSpec((1, HALF, STEP), lambda k: (0, 0, jnp.maximum(k - STEPS, 0)))
    whole = pl.BlockSpec(x.shape, lambda k: (0, 0))
    return call(
        functools.partial(expert_kernel, experts),
        "expert_rows",
        flops=12 * count * D * HALF,
        moved=12 * D * HALF + 4 * count * D,
        grid=(2 * STEPS,),
        in_specs=[whole] + [weights] * 4 + [down] * 2,
        out_specs=whole,
        scratch_shapes=[
            pltpu.VMEM((STEPS, count, STEP), BF16),
            pltpu.VMEM((4, count, HALF), F32),
            pltpu.VMEM((2, count, HALF), BF16),
            pltpu.VMEM((STEPS, count, STEP), BF16),
        ],
        out_shape=jax.ShapeDtypeStruct(x.shape, BF16),
    )(x, own[0], own[1], other[0], other[1], own[2], other[2])


class Split:
    def __init__(self, groups, shards, heads):
        self.groups, self.shards = groups, shards
        self.each = heads // shards
        self.wide = groups == 2 and self.each % (2 * groups) == 0
        self.chips = shards // 2
        self.own_pairs = self.each // 2 // (groups if self.wide else 1)
        self.holders = 2 if self.wide else 1
        self.pairs = 2 * self.holders * self.own_pairs
        self.parts = groups if self.wide else 1

    def first_head(self, rank, chip, pair):
        core, rest = divmod(pair, self.holders * self.own_pairs)
        holder, own = divmod(rest, self.own_pairs)
        if not self.wide:
            return (2 * chip + ((rank & 1) ^ core)) * self.each + 2 * own
        group, low = divmod(chip, self.shards // 4)
        top = (rank & (self.shards // 2)) ^ (holder * (self.shards // 2))
        return (top + 2 * low + ((rank & 1) ^ core)) * self.each + 2 * (group * self.own_pairs + own)

    def exchange(self, array):
        half = self.shards // 2
        if self.wide:
            tops, steps = (0, half), [g * self.shards + c for g in range(self.groups) for c in range(0, half, 2)]
            sets = [[start + core + step for step in steps] for start in tops for core in range(2)]
        else:
            starts = range(0, self.groups * self.shards, self.shards)
            sets = [[start + core + c for c in range(0, self.shards, 2)] for start in starts for core in range(2)]
        return lax.all_to_all(
            array, ("groups", "ctx"), split_axis=0, concat_axis=0, axis_index_groups=sets, tiled=True
        )


def split_kernel(split, rank_ref, x_ref, out_ref):
    each = NOPE + ROPE
    for chip in range(split.chips):
        for pair in range(split.pairs):
            start = pl.multiple_of(split.first_head(rank_ref[0], chip, pair) * each, 128)
            part = x_ref[:, pl.ds(start, 2 * each)]
            out_ref[chip, :, pair * 2 * each : (pair + 1) * 2 * each] = jnp.concatenate(
                [part[:, :NOPE], part[:, each : each + NOPE], part[:, NOPE:each], part[:, each + NOPE :]], axis=1
            )


def split_queries(split, rank, queries):
    tok = queries.shape[0]
    return call(
        functools.partial(split_kernel, split),
        "split_queries",
        moved=4 * queries.size,
        in_specs=[SMEM, VMEM],
        out_specs=VMEM,
        out_shape=jax.ShapeDtypeStruct((split.chips, tok, 2 * split.pairs * (NOPE + ROPE)), BF16),
    )(rank, queries)


def join_kernel(split, rank_ref, x_ref, out_ref):
    for chip in range(split.chips):
        for pair in range(split.pairs):
            start = pl.multiple_of(split.first_head(rank_ref[0], chip, pair) * VDIM, 128)
            out_ref[:, pl.ds(start, 2 * VDIM)] = x_ref[chip, :, pair * 2 * VDIM : (pair + 1) * 2 * VDIM]


def join_values(split, rank, values):
    return call(
        functools.partial(join_kernel, split),
        "join_values",
        moved=4 * values.size,
        in_specs=[SMEM, VMEM],
        out_specs=VMEM,
        out_shape=jax.ShapeDtypeStruct((values.shape[1], HEADS * VDIM), BF16),
    )(rank, values)


BLOCK = 128
SPAN = 2 * BLOCK
EXP_SCALE = math.log2(math.e) / math.sqrt(NOPE + ROPE)


def attention_kernel(
    split, rank_ref, query_ref, kv_ref, other_kv_ref, weight_ref, other_weight_ref, out_ref, keys, queries, mixed
):
    tok = kv_ref.shape[1]
    part_rows = query_ref.shape[0] // split.parts
    core = rank_ref[0] & 1

    @pl.when(pl.program_id(0) == 0)
    def _():
        for index, offset in enumerate(gather_order(split)):
            for from_ref, swapped in ((kv_ref, 0), (other_kv_ref, 1)):
                group, ctx = divmod(offset ^ swapped, split.shards)
                group = rank_ref[1] ^ group if split.wide else 0
                place = pl.ds(pl.multiple_of((rank_ref[0] ^ ctx) * tok, tok), tok)
                keys[group, place, : LATENT + ROPE] = from_ref[index]
                keys[group, place, LATENT + ROPE :] = from_ref[index, :, LATENT:]

    own_core = pl.program_id(0) < split.pairs // 2

    def weight(index):
        return jnp.where(own_core, weight_ref[0, index], other_weight_ref[0, index])

    contract = (((1,), (1,)), ((), ()))
    side = lax.broadcasted_iota(jnp.int32, (1, 2 * ROPE), 1) // ROPE
    for one in range(2):
        latent = lax.dot_general(
            query_ref[:, one * NOPE : (one + 1) * NOPE], weight(one), contract, preferred_element_type=F32
        )
        queries[one, :, :LATENT] = latent.astype(BF16)
        queries[one, :, LATENT:] = jnp.where(side == one, query_ref[:, 2 * NOPE :], jnp.zeros((), BF16))

    row = lax.broadcasted_iota(jnp.int32, (2 * BLOCK, SPAN), 0) % BLOCK
    position = (2 * (row // tok) + core) * tok + row % tok
    visible = lax.broadcasted_iota(jnp.int32, (2 * BLOCK, SPAN), 1) <= position

    def attend(part, block, before):
        start = before * SPAN
        first = part * part_rows + block * BLOCK
        rows = pl.ds(first, BLOCK)
        last = pl.ds(start, SPAN)
        query = jnp.concatenate([queries[0, rows, :], queries[1, rows, :]], axis=0)
        near = lax.dot_general(query, keys[part, last, :], contract, preferred_element_type=F32)
        near = jnp.where(visible, near, -1e30)
        top = jnp.max(near, axis=1, keepdims=True)
        if before:
            past = lax.dot_general(query, keys[part, :start, :], contract, preferred_element_type=F32)
            top = jnp.maximum(top, jnp.max(past, axis=1, keepdims=True))
        weights = jnp.exp2((near - top) * EXP_SCALE)
        total = jnp.sum(weights, axis=1, keepdims=True)
        summed = jnp.dot(weights.astype(BF16), keys[part, last, :LATENT], preferred_element_type=F32)
        if before:
            weights = jnp.exp2((past - top) * EXP_SCALE)
            total = total + jnp.sum(weights, axis=1, keepdims=True)
            summed = summed + jnp.dot(
                weights.astype(BF16), keys[part, :start, :LATENT], preferred_element_type=F32
            )
        result = (summed / total).astype(BF16)
        mixed[0, rows, :] = result[:BLOCK]
        mixed[1, rows, :] = result[BLOCK:]

    blocks = part_rows // BLOCK
    if split.wide:
        for half in range(2):

            @pl.when(rank_ref[0] // (split.shards // 2) == half)
            def _():
                for part in range(split.parts):
                    for block in range(blocks):
                        attend(part, block, half * blocks + block)

    else:
        for block in range(blocks):
            attend(0, block, block)

    for one in range(2):
        out_ref[:, one * VDIM : (one + 1) * VDIM] = jnp.dot(
            mixed[one], weight(2 + one), preferred_element_type=F32
        ).astype(BF16)


def attention(split, place, queries, keys, other_keys, weights, other_weights):
    count = queries.shape[0]
    length = 2 * keys.shape[0] * keys.shape[1] // split.parts
    whole = pl.BlockSpec(keys.shape, lambda p, place: (0, 0, 0))
    each = split.pairs // 2
    return call(
        functools.partial(attention_kernel, split),
        "causal_attention",
        flops=4 * count * length * split.pairs * (2 * LATENT + ROPE),
        moved=4 * (queries.size + keys.size + weights.size),
        grid_spec=pltpu.PrefetchScalarGridSpec(
            num_scalar_prefetch=1,
            grid=(split.pairs,),
            in_specs=[
                pl.BlockSpec((count, 2 * (NOPE + ROPE)), lambda p, place: (0, p)),
                whole,
                whole,
                pl.BlockSpec((1, 4, LATENT, VDIM), lambda p, place: (jnp.minimum(p, each - 1), 0, 0, 0)),
                pl.BlockSpec((1, 4, LATENT, VDIM), lambda p, place: (jnp.maximum(p - each, 0), 0, 0, 0)),
            ],
            out_specs=pl.BlockSpec((count, 2 * VDIM), lambda p, place: (0, p)),
            scratch_shapes=[
                pltpu.VMEM((split.parts, length, LATENT + 2 * ROPE), BF16),
                pltpu.VMEM((2, count, LATENT + 2 * ROPE), BF16),
                pltpu.VMEM((2, count, LATENT), BF16),
            ],
        ),
        out_shape=jax.ShapeDtypeStruct((count, 2 * split.pairs * VDIM), BF16),
    )(place, queries, keys, other_keys, weights, other_weights)


def send(array, mask):
    count = lax.axis_size("groups") * lax.axis_size("ctx")
    return lax.ppermute(array, ("groups", "ctx"), [(i, i ^ mask) for i in range(count)])


def swap_chips(array):
    shards = lax.axis_size("ctx")
    return lax.all_to_all(
        array,
        "ctx",
        split_axis=0,
        concat_axis=0,
        axis_index_groups=[list(range(core, shards, 2)) for core in range(2)],
        tiled=True,
    )


def after(array, *others):
    return lax.optimization_barrier((array, *others))[0]


def gather_masks(split):
    top, below = split.shards // 2, split.shards // 4
    later = [1 << bit for bit in reversed(range(1, below.bit_length() - 1))]
    return [top, below, top ^ below], ([split.shards] if split.wide else []) + later


def gather_order(split):
    direct, later = gather_masks(split)
    order = [0] + direct
    for mask in later:
        order = order + [offset ^ mask for offset in order]
    return order


def on_device(
    queries,
    latent_kv,
    key_proj,
    value_proj,
    moe_input,
    routes,
    gates,
    expert_gate,
    expert_up,
    expert_down,
):
    shards = lax.axis_size("ctx")
    split = Split(lax.axis_size("groups"), shards, HEADS)
    tok = queries.shape[0]
    experts = shards // 2
    capacity = 2 * ((4 * tok * TOP + 6 * experts - 1) // (6 * experts))
    rows = capacity
    rank = lax.axis_index("ctx").astype(jnp.int32).reshape(1)
    group = lax.axis_index("groups").astype(jnp.int32).reshape(1)
    place = jnp.concatenate([rank, group])

    direct, later = gather_masks(split)
    keys = [latent_kv] + [send(latent_kv, offset) for offset in direct]

    buckets = after(build_buckets(routes, moe_input, experts, rows), *keys)
    arrived = swap_chips(buckets.reshape(experts, STEPS * rows, STEP)).reshape(-1, STEP)

    sent = split_queries(split, rank, queries)
    keys = after(jnp.stack(keys), sent)
    for mask in later:
        keys = jnp.concatenate([keys, send(keys, mask)], axis=0)
    other_keys = send(keys, 1)
    own_half = [expert_gate, expert_up, expert_down]
    other_half = [send(after(part, buckets), 1) for part in own_half]
    sent = after(sent, keys, arrived, *other_half)
    held = split.exchange(sent).reshape(experts * tok, -1)

    weights = jnp.concatenate(
        [
            key_proj.swapaxes(1, 2).reshape(-1, 2, LATENT, NOPE),
            value_proj.reshape(-1, 2, LATENT, VDIM),
        ],
        axis=1,
    )
    if split.wide:
        weights = lax.dynamic_slice_in_dim(weights, group[0] * split.own_pairs, split.own_pairs, axis=0)
        weights = after(weights, arrived)
        weights = jnp.concatenate([weights, send(weights, shards // 2)], axis=0)

    result = expert_rows(arrived, own_half, other_half, experts)
    other_weights = send(after(weights, result), 1)
    result, held = lax.optimization_barrier((result, held))
    back = swap_chips(result.reshape(experts, STEPS * rows, STEP))
    values = attention(split, place, held, keys, other_keys, weights, other_weights)
    values, back = lax.optimization_barrier((values, back))
    values = split.exchange(values.reshape(experts, tok, values.shape[1]))
    moe_out = combine(routes, gates, back.reshape(-1, STEP), rows)
    return (join_values(split, rank, values), moe_out)


def solution(mesh):
    return jax.shard_map(
        on_device,
        mesh=mesh,
        in_specs=(
            P(("groups", "ctx"), None),
            P(("groups", "ctx"), None),
            P("ctx", None, None),
            P("ctx", None, None),
            P(("groups", "ctx"), None),
            P(("groups", "ctx"), None),
            P(("groups", "ctx"), None),
            P("ctx", None, None),
            P("ctx", None, None),
            P("ctx", None, None),
        ),
        out_specs=(P(("groups", "ctx"), None), P(("groups", "ctx"), None)),
        check_vma=False,
    )
```
